512 devices in a mesh: seq: 32 (over z, core), exp: 16 (over y, x).
Axes of the slice: x: 4, y: 4, z: 16, core: 2. Of those that a mesh axis runs over, the one named last changes fastest.
Arguments:
- queries: bfloat16 [4096, 64, 576], P('seq', 'exp'), may hold values from -16 to 16
- latents: bfloat16 [4096, 576], P('seq'), may hold values from -4.5 to 4.5
- cache: bfloat16 [512, 576], P('seq'), may hold values from -4 to 4
- prefix_len: int32 [1], replicated, may hold values from 256 to 512
- value_up: bfloat16 [64, 512, 128], P('exp'), may hold values from -2.5 to 2.5
- out_proj: bfloat16 [8192, 7168], P('exp', 'seq'), may hold values from -0.0625 to 0.0625
- residual: bfloat16 [4096, 7168], P('exp', 'seq'), may hold values from -24 to 24
- norm_gain: float32 [7168], P('seq'), may hold values from 0.25 to 1.75
- w_gate: bfloat16 [16, 7168, 2048], P('exp', 'seq'), may hold values from -0.0625 to 0.0625
- w_up: bfloat16 [16, 7168, 2048], P('exp', 'seq'), may hold values from -0.0625 to 0.0625
- w_down: bfloat16 [16, 2048, 7168], P('exp', None, 'seq'), may hold values from -0.125 to 0.125
- routes: int32 [4096, 8], replicated, may hold values from 0 to 255, as said below
- route_weights: bfloat16 [4096, 8], replicated, may hold values from 0.5 to 2
Outputs:
- layer_out: bfloat16 [4096, 7168], P('exp', 'seq')
The draws below stay inside these ranges and needn't reach their ends.
Inputs may be any that keep to these rules, and one draw needn't show every extreme that they name: `routes`: each row names 8 different expert ids. Of the tokens of one aligned block of 256 rows, at most 32 name one held expert (0 to 15); over all tokens, at most 192 name one held expert. Both bounds are reached.
All inputs are finite; a program needn't handle non-finite values.
Results may differ from the reference program's by a relative error of at most 0.02.
Values may be sent and summed in bfloat16 or wider, within the bound.
A program may use at most 64 MiB of HBM per device.

```python
import math
import jax
import jax.numpy as jnp
from jax import lax

D = 7168
LAT = 512
ROPE = 64
QK_NOPE = 128
VHEAD = 128
EFF = 2048
ROUTED = 256
TOP = 8
HEADS_DEV = 4
SRC_CAP = 32
TOKENS = 4096
CAP = 192
CACHE = 512
HEADS = 64
EXPERTS = 16
N_EXP = 16


def base_rows(key):
    normal_part = jnp.clip(jax.random.normal(key, (TOKENS, LAT + ROPE), jnp.float32), -4.0, 4.0)
    return normal_part


def draw_latents(key, part):
    rows = base_rows(key)
    return rows.astype(jnp.bfloat16)


def draw_queries(key, part):
    key = jax.random.fold_in(key, 7)
    shape = (TOKENS, HEADS, LAT + ROPE)
    rows = jnp.clip(jax.random.normal(key, shape, jnp.float32), -4.0, 4.0)
    return rows.astype(jnp.bfloat16)


def column_scale(low, ratio):
    place = jnp.arange(D, dtype=jnp.float32) / (D - 1)
    return low * jnp.exp(place * jnp.log(ratio))


def draw_residual(key, part):
    key = jax.random.fold_in(key, 23)
    row_factor = jnp.exp(jax.random.uniform(jax.random.fold_in(key, 5), (TOKENS, 1), jnp.float32, math.log(0.4), math.log(4.0)))
    values = jnp.clip(jax.random.normal(key, (TOKENS, D), jnp.float32), -4.0, 4.0)
    rows = values * column_scale(0.25, 6.0)[None, :]
    rows = jnp.clip(rows * row_factor, -24.0, 24.0)
    return rows.astype(jnp.bfloat16)


def draw_routes(key, part):
    key = jax.random.fold_in(key, 11)
    keys = jax.random.split(key, 6)
    index = jnp.arange(ROUTED, dtype=jnp.int32)
    base = jax.random.randint(keys[0], (TOKENS, ROUTED), 0, 65536, jnp.int32) * ROUTED + index[None, :]
    lift = jax.random.randint(keys[1], (ROUTED,), 0, 4, jnp.int32) * (65536 * ROUTED)
    huge = 2 ** 28
    hot = jax.random.randint(keys[2], (), 0, EXPERTS, jnp.int32)
    block = TOKENS // N_EXP
    hot_count = CAP // SRC_CAP
    hot_blocks = jax.random.permutation(keys[3], N_EXP) < hot_count
    expert_ids = jnp.arange(EXPERTS, dtype=jnp.int32)
    counts = jax.random.randint(keys[4], (EXPERTS, N_EXP), 1, CAP // N_EXP + 1, jnp.int32)
    hot_counts = jnp.where(hot_blocks, SRC_CAP, 0).astype(jnp.int32)
    counts = jnp.where((expert_ids == hot)[:, None], hot_counts[None, :], counts)
    ranks = jax.vmap(lambda sub: jax.random.permutation(sub, block))(jax.random.split(keys[5], EXPERTS * N_EXP))
    ranks = ranks.reshape(EXPERTS, N_EXP, block)
    take = (ranks < counts[:, :, None]).reshape(EXPERTS, TOKENS).T
    is_hot = expert_ids[None, :] == hot
    held_base = base[:, :EXPERTS]
    held_score = jnp.where(take, jnp.where(is_hot, held_base + 2 * huge, held_base + huge), -1)
    scores = jnp.concatenate([held_score, base[:, EXPERTS:] + lift[None, EXPERTS:]], axis=1)
    return lax.top_k(scores, TOP)[1].astype(jnp.int32)


def shard_levels(key, shape, cuts, least, largest):
    level = 1.0
    for position, shards_of in cuts:
        heights = jax.random.uniform(jax.random.fold_in(jax.random.fold_in(key, 6), position), (shards_of,), jnp.float32, least / len(cuts), largest / len(cuts))
        level = level * jnp.repeat(jnp.exp(heights), shape[position] // shards_of).reshape((-1,) + (1,) * (len(shape) - 1 - position))
    return level


def gaussian(own_key, dims, scale, limit, pieces=(), kind=jnp.bfloat16):
    result = scale * jax.random.normal(own_key, dims, jnp.float32)
    if pieces:
        result = result * shard_levels(own_key, dims, pieces, -0.22, 0.18)
    return jnp.clip(result, -limit, limit).astype(kind)


def setup_inputs(seed: int = 0) -> dict:
    splits = jax.random.split(jax.random.key(seed), 14)
    queries = draw_queries(jax.random.fold_in(splits[13], 71), 0)
    latents = draw_latents(jax.random.fold_in(splits[13], 71), 0)
    cache = gaussian(splits[2], (CACHE, LAT + ROPE), 1.0, 4.0, ((0, 32),))
    prefix_len = jax.random.randint(splits[3], (1,), CACHE // 2, CACHE + 1).astype(jnp.int32)
    value_up = gaussian(splits[4], (HEADS, LAT, VHEAD), (max(1, LAT // 100)) ** -0.5, 2.5, ((0, 16),))
    out_proj = gaussian(splits[5], (HEADS * VHEAD, D), (HEADS * VHEAD) ** -0.5, 0.0625, ((0, 16), (1, 32)))
    residual = draw_residual(jax.random.fold_in(splits[13], 71), 0)
    norm_gain = jnp.clip(1.0 + 0.15 * jax.random.normal(splits[7], (D,), jnp.float32), 0.25, 1.75)
    w_gate = gaussian(splits[8], (EXPERTS, D, EFF), D ** -0.5, 0.0625, ((0, 16), (1, 32)))
    w_up = gaussian(splits[9], (EXPERTS, D, EFF), D ** -0.5, 0.0625, ((0, 16), (1, 32)))
    w_down = gaussian(splits[10], (EXPERTS, EFF, D), EFF ** -0.5, 0.125, ((0, 16), (2, 32)))
    routes = draw_routes(jax.random.fold_in(splits[13], 71), 0)
    route_weights = jnp.clip(jax.random.uniform(splits[12], (TOKENS, TOP), jnp.float32, 0.5, 2.0), 0.5, 2.0).astype(jnp.bfloat16)
    return dict(queries=queries, latents=latents, cache=cache, prefix_len=prefix_len, value_up=value_up, out_proj=out_proj, residual=residual, norm_gain=norm_gain, w_gate=w_gate, w_up=w_up, w_down=w_down, routes=routes, route_weights=route_weights)


eps = 1e-06

def reference(queries, latents, cache, prefix_len, value_up, out_proj, residual, norm_gain, w_gate, w_up, w_down, routes, route_weights):
    scale = (QK_NOPE + ROPE) ** (-0.5)
    keys = jnp.concatenate([cache, latents], axis=0)
    values = keys[:, :LAT]
    token_index = jnp.arange(TOKENS, dtype=jnp.int32)
    cache_live = jnp.arange(CACHE, dtype=jnp.int32) < prefix_len[0]
    visible = jnp.concatenate([jnp.broadcast_to(cache_live[None, :], (TOKENS, CACHE)), token_index[None, :] <= token_index[:, None]], axis=1)

    def one_head(head_queries):
        scores = jnp.dot(head_queries, keys.T, preferred_element_type=jnp.float32) * scale
        scores = jnp.where(visible, scores, -jnp.inf)
        top = lax.optimization_barrier(jnp.max(scores, axis=1, keepdims=True))
        weights = jnp.exp(scores - top)
        total = lax.optimization_barrier(jnp.sum(weights, axis=1, keepdims=True))
        context = jnp.dot(weights.astype(jnp.bfloat16), values, preferred_element_type=jnp.float32) / total
        return context.astype(jnp.bfloat16)
    context = lax.map(one_head, jnp.swapaxes(queries, 0, 1))
    head_out = jnp.einsum('htl,hlv->thv', context.astype(jnp.float32), value_up.astype(jnp.float32)).astype(jnp.bfloat16)
    head_out = head_out.reshape(TOKENS, N_EXP, HEADS_DEV * VHEAD)
    groups = out_proj.reshape(N_EXP, HEADS_DEV * VHEAD, D)

    def add_group(total, group):
        term = jnp.dot(head_out[:, group], groups[group], preferred_element_type=jnp.float32).astype(jnp.bfloat16)
        return (total + term.astype(jnp.float32), None)
    attended, _ = lax.scan(add_group, jnp.zeros((TOKENS, D), jnp.float32), jnp.arange(N_EXP, dtype=jnp.int32))
    hidden = residual.astype(jnp.float32) + attended
    normed = (hidden * lax.rsqrt(lax.optimization_barrier(jnp.mean(hidden * hidden, axis=1, keepdims=True)) + eps) * norm_gain).astype(jnp.bfloat16)

    def add_expert(total, expert):
        hit = routes == expert
        chosen = jnp.any(hit, axis=1)
        weight_all = lax.optimization_barrier(jnp.sum(jnp.where(hit, route_weights.astype(jnp.float32), 0.0), axis=1))
        picked = jnp.nonzero(chosen, size=CAP, fill_value=0)[0].astype(jnp.int32)
        valid = jnp.arange(CAP, dtype=jnp.int32) < jnp.sum(chosen.astype(jnp.int32))
        row_weight = jnp.where(valid, weight_all[picked], 0.0)
        rows_in = normed[picked]
        gate = jnp.dot(rows_in, w_gate[expert], preferred_element_type=jnp.float32)
        up = jnp.dot(rows_in, w_up[expert], preferred_element_type=jnp.float32)
        inner = (jax.nn.silu(gate) * up).astype(jnp.bfloat16)
        produced = jnp.dot(inner, w_down[expert], preferred_element_type=jnp.float32)
        weighted = (row_weight[:, None] * produced).astype(jnp.bfloat16)
        return (total.at[picked].add(weighted.astype(jnp.float32)), None)
    routed, _ = lax.scan(add_expert, jnp.zeros((TOKENS, D), jnp.float32), jnp.arange(EXPERTS, dtype=jnp.int32))
    return (hidden + routed).astype(jnp.bfloat16)
```

```python
import functools

import jax
import jax.numpy as jnp
from jax import lax
from jax.experimental import pallas as pl
from jax.experimental.pallas import tpu as pltpu
from jax.sharding import PartitionSpec as P

LAT = 512
ROPE = 64
QK_NOPE = 128
SRC_CAP = 32

EPS = 1e-06
FLOOR = -1e30
SCALE = (QK_NOPE + ROPE) ** (-0.5)
MESH = pl.DeviceIdType.MESH
VMEM = pltpu.VMEM
VMEM_BYTES = 48 * 1024 * 1024


def rdot(a, b):
    return jnp.dot(a, b, preferred_element_type=jnp.float32)


def rdot_t(a, b):
    return lax.dot_general(
        a, b, (((1,), (1,)), ((), ())), preferred_element_type=jnp.float32
    )


def place(zs):
    s = lax.axis_index("seq")
    z, c = s // 2, lax.rem(s, 2)
    above = lax.rem(z + 1, zs) * 2 + c
    below = lax.rem(z + zs - 1, zs) * 2 + c
    twin = 2 * z + 1 - c
    return z, c, above, below, twin


def greet(zs, peers):
    _, _, above, below, twin = place(zs)
    e = lax.axis_index("exp")
    barrier = pltpu.get_barrier_semaphore()
    for to in (above, below, twin):
        pl.semaphore_signal(
            barrier, inc=1, device_id={"seq": to, "exp": e}, device_id_type=MESH
        )
    if peers > 1:
        s = lax.axis_index("seq")

        def hello(j, carry):
            pl.semaphore_signal(
                barrier,
                inc=1,
                device_id={"seq": s, "exp": lax.rem(e + j, peers)},
                device_id_type=MESH,
            )
            return carry

        lax.fori_loop(1, peers, hello, 0)
    pl.semaphore_wait(barrier, 3 + max(peers - 1, 0))


def ring_sems(zs):
    up, down = zs // 2, zs // 2 - 1
    dma = pltpu.SemaphoreType.DMA
    return [dma((up,)), dma((up,)), dma((down,)), dma((down,)), dma((zs,)), dma((zs,))]


def ring_gather(zs, buf, sems, own, visit):
    us, ur, ds, dr, ts, tr = sems
    up, down = zs // 2, zs // 2 - 1
    z, c, above, below, twin = place(zs)
    e = lax.axis_index("exp")

    def copy(zb, core, ssem, rsem, to):
        slot = buf.at[2 * zb + core]
        return pltpu.make_async_remote_copy(
            src_ref=slot,
            dst_ref=slot,
            send_sem=ssem,
            recv_sem=rsem,
            device_id={"seq": to, "exp": e},
            device_id_type=MESH,
        )

    def lower(k):
        return lax.rem(z - k + zs, zs)

    def upper(k):
        return lax.rem(z + k, zs)

    copy(z, c, us.at[0], ur.at[0], above).start()
    copy(z, c, ds.at[0], dr.at[0], below).start()
    copy(z, c, ts.at[0], tr.at[0], twin).start()

    def step(k, carry):
        @pl.when(k <= up)
        def _():
            copy(lower(k), c, us.at[k - 1], ur.at[k - 1], above).wait_recv()

            @pl.when(k < up)
            def _():
                copy(lower(k), c, us.at[k], ur.at[k], above).start()

            copy(lower(k), c, ts.at[k], tr.at[k], twin).start()

        @pl.when(k <= down)
        def _():
            copy(upper(k), c, ds.at[k - 1], dr.at[k - 1], below).wait_recv()

            @pl.when(k < down)
            def _():
                copy(upper(k), c, ds.at[k], dr.at[k], below).start()

            copy(upper(k), c, ts.at[up + k], tr.at[up + k], twin).start()

        @pl.when(k == 1)
        def _():
            copy(z, 1 - c, ts.at[0], tr.at[0], twin).wait_recv()
            own()

        def side(which, inner):
            j = k - 1

            @pl.when((which == 0) | (j <= down))
            def _():
                zb = lax.rem(z + jnp.where(which == 0, zs - j, j), zs)
                index = jnp.where(which == 0, j, up + j)
                copy(zb, 1 - c, ts.at[index], tr.at[index], twin).wait_recv()
                visit(zb)

            return inner

        @pl.when(k > 1)
        def _():
            lax.fori_loop(0, 2, side, 0)

        return carry

    lax.fori_loop(1, up + 2, step, 0)

    def drain(k, carry):
        copy(lower(k), c, us.at[k], ur.at[k], above).wait_send()
        copy(lower(k), c, ts.at[k], tr.at[k], twin).wait_send()

        @pl.when(k < down)
        def _():
            copy(upper(k), c, ds.at[k], dr.at[k], below).wait_send()
            copy(upper(k), c, ts.at[up + 1 + k], tr.at[up + 1 + k], twin).wait_send()

        return carry

    lax.fori_loop(0, up, drain, 0)
    copy(lower(up), c, ts.at[up], tr.at[up], twin).wait_send()


def attention_kernel(
    zs, q_ref, lat_ref, cache_ref, live_ref, vup_ref, out_ref, buf, best, total, acc, *sems
):
    tok = lat_ref.shape[0]
    slots = cache_ref.shape[0]
    rows, width = q_ref.shape
    heads = rows // tok
    z, c, _, _, _ = place(zs)
    s = 2 * z + c
    greet(zs, 0)
    buf[s, 0:tok, :] = lat_ref[...]
    buf[s, tok : tok + slots, :] = cache_ref[...]

    def absorb(keys, visible, first):
        scores = rdot_t(q_ref[...], keys) * SCALE
        if visible is not None:
            scores = jnp.where(visible, scores, FLOOR)
        top = jnp.max(scores, axis=1, keepdims=True)
        if first:
            newest = top
            weights = jnp.exp(scores - newest)
            total[...] = jnp.sum(weights, axis=1, keepdims=True)
            acc[...] = rdot(weights.astype(jnp.bfloat16), keys[:, :LAT])
        else:
            before = best[...]
            newest = jnp.maximum(before, top)
            fade = jnp.exp(before - newest)
            weights = jnp.exp(scores - newest)
            total[...] = total[...] * fade + jnp.sum(weights, axis=1, keepdims=True)
            acc[...] = acc[...] * fade + rdot(weights.astype(jnp.bfloat16), keys[:, :LAT])
        best[...] = newest

    def pair(zb):
        return buf[pl.ds(2 * zb, 2), 0:tok, :].reshape(2 * tok, width)

    def own():
        row = lax.broadcasted_iota(jnp.int32, (rows, 2 * tok), 0)
        key = lax.broadcasted_iota(jnp.int32, (rows, 2 * tok), 1)
        absorb(pair(z), key <= lax.rem(row, tok) + c * tok, True)

    def visit(zb):
        @pl.when(zb < z)
        def _():
            absorb(pair(zb), None, False)

    ring_gather(zs, buf, sems, own, visit)

    live = live_ref[0]
    group = max(1, min(256, slots * 2 * zs) // slots)

    def prefix(i, carry):
        keys = buf[pl.ds(i * group, group), tok : tok + slots, :].reshape(group * slots, width)
        key = lax.broadcasted_iota(jnp.int32, (rows, group * slots), 1) + i * (group * slots)
        absorb(keys, key < live, False)
        return carry

    lax.fori_loop(0, 2 * zs // group, prefix, 0)

    for h in range(heads):
        part = pl.ds(h * tok, tok)
        context = (acc[part, :] / total[part, :]).astype(jnp.bfloat16)
        vh = vup_ref.shape[2]
        out_ref[:, h * vh : (h + 1) * vh] = rdot(context, vup_ref[h]).astype(jnp.bfloat16)


def project_kernel(zs, peers, head_ref, proj_ref, out_ref, buf, terms, got, t_send, t_recv, *sems):
    tok, inner = head_ref.shape
    width = proj_ref.shape[1]
    z, c, _, _, _ = place(zs)
    s = 2 * z + c
    e = lax.axis_index("exp")
    greet(zs, peers)
    buf[s] = head_ref[...]

    def hand(zb):
        return pltpu.make_async_remote_copy(
            src_ref=terms.at[zb],
            dst_ref=got.at[e],
            send_sem=t_send.at[zb],
            recv_sem=t_recv.at[e],
            device_id={"seq": s, "exp": zb},
            device_id_type=MESH,
        )

    def visit(zb):
        rows = buf[pl.ds(2 * zb, 2)].reshape(2 * tok, inner)
        terms[zb] = rdot(rows, proj_ref[...]).astype(jnp.bfloat16)

        @pl.when(zb != e)
        def _():
            hand(zb).start()

    ring_gather(zs, buf, sems, lambda: visit(z), visit)
    out_ref[...] = terms[e].astype(jnp.float32)

    def collect(j, carry):
        g = lax.rem(e + j, peers)
        pltpu.make_async_remote_copy(
            src_ref=terms.at[g],
            dst_ref=got.at[g],
            send_sem=t_send.at[g],
            recv_sem=t_recv.at[g],
            device_id={"seq": s, "exp": g},
            device_id_type=MESH,
        ).wait_recv()
        out_ref[...] += got[g].astype(jnp.float32)
        return carry

    lax.fori_loop(1, peers, collect, 0)

    def drain(j, carry):
        hand(lax.rem(e + j, peers)).wait_send()
        return carry

    lax.fori_loop(1, peers, drain, 0)


def swap_exp(peers, send, recv, s_sem, r_sem):
    s = lax.axis_index("seq")
    e = lax.axis_index("exp")

    def copy(j, to, slot):
        return pltpu.make_async_remote_copy(
            src_ref=send.at[to],
            dst_ref=recv.at[slot],
            send_sem=s_sem.at[j],
            recv_sem=r_sem.at[j],
            device_id={"seq": s, "exp": to},
            device_id_type=MESH,
        )

    def start(j, carry):
        copy(j, lax.rem(e + j, peers), e).start()
        return carry

    lax.fori_loop(1, peers, start, 0)
    recv[e] = send[e]

    def finish(j, carry):
        copy(j, lax.rem(e + j, peers), lax.rem(e + peers - j, peers)).wait_recv()
        return carry

    lax.fori_loop(1, peers, finish, 0)

    def drain(j, carry):
        copy(j, lax.rem(e + j, peers), e).wait_send()
        return carry

    lax.fori_loop(1, peers, drain, 0)


def split_rows(v):
    row = lax.broadcasted_iota(jnp.int32, v.shape, 0)
    high = v.astype(jnp.bfloat16).astype(jnp.float32)
    rest = v - high
    mid = rest.astype(jnp.bfloat16).astype(jnp.float32)
    low = rest - mid
    parts = jnp.where(row == 0, high, jnp.where(row == 1, mid, jnp.where(row == 2, low, 0.0)))
    return parts.astype(jnp.bfloat16)


def join_rows(block):
    return jnp.sum(block.astype(jnp.float32), axis=0, keepdims=True)


def experts_kernel(
    zs,
    peers,
    features,
    att_ref,
    res_ref,
    gain_ref,
    pick_ref,
    mix_ref,
    pack_ref,
    unpack_ref,
    wg_ref,
    wu_ref,
    wd_ref,
    out_ref,
    hid,
    d_send,
    d_recv,
    xs,
    sqv,
    mine,
    other,
    theirs,
    up_out,
    up_in,
    dn_out,
    dn_in,
    ibuf,
    acc,
    c_send,
    c_recv,
    ds_sem,
    dr_sem,
    ps_sem,
    pr_sem,
    us_sem,
    ur_sem,
    ls_sem,
    lr_sem,
    cs_sem,
    cr_sem,
    *sems,
):
    tokens, width = res_ref.shape
    wide = hid.shape[1]
    cap = pack_ref.shape[0]
    half = cap // 2
    cols = ibuf.shape[2]
    up, down = zs // 2, zs // 2 - 1
    z, c, above, below, twin = place(zs)
    e = lax.axis_index("exp")
    greet(zs, peers)

    hid[...] = jnp.zeros_like(hid)
    hid[:, 0:width] = res_ref[...].astype(jnp.float32) + att_ref[...]
    hidden = hid[...]
    squares = jnp.sum(hidden * hidden, axis=1, keepdims=True)
    high = squares.astype(jnp.bfloat16).astype(jnp.float32)
    rest = squares - high
    mid = rest.astype(jnp.bfloat16).astype(jnp.float32)
    low = rest - mid
    lane = lax.broadcasted_iota(jnp.int32, (tokens, wide), 1)
    ext = jnp.where(
        lane < width,
        hidden * gain_ref[...],
        jnp.where(
            lane == width,
            high,
            jnp.where(lane == width + 1, mid, jnp.where(lane == width + 2, low, 0.0)),
        ),
    ).astype(jnp.bfloat16)
    d_send[...] = rdot(pick_ref[...], ext).astype(jnp.bfloat16).reshape(d_send.shape)
    swap_exp(peers, d_send, d_recv, ds_sem, dr_sem)

    arrived = d_recv[...].reshape(peers * SRC_CAP, wide)
    packed = rdot(pack_ref[...], arrived).astype(jnp.bfloat16)
    xs[...] = packed
    mark = lax.broadcasted_iota(jnp.int32, (16, wide), 1)
    ones = jnp.where((mark >= width) & (mark < width + 3), 1.0, 0.0).astype(jnp.bfloat16)
    sqv[...] = jnp.zeros_like(sqv)
    sqv[:, 0:cap] = rdot_t(ones, packed)
    own_sq = sqv[...]
    tail = split_rows(own_sq)
    x_mine = xs[pl.ds(pl.multiple_of(c * half, 16), half), 0:width]
    x_other = xs[pl.ds(pl.multiple_of((1 - c) * half, 16), half), 0:width]

    def to_twin(d):
        return pltpu.make_async_remote_copy(
            src_ref=other.at[d],
            dst_ref=theirs.at[d],
            send_sem=ps_sem.at[d],
            recv_sem=pr_sem.at[d],
            device_id={"seq": twin, "exp": e},
            device_id_type=MESH,
        )

    def partial(i, carry):
        t = i // 2
        d = lax.rem(z + jnp.where(lax.rem(i, 2) == 0, up - t, zs - down + t), zs)
        span = pl.ds(pl.multiple_of(d * cols, cols), cols)
        other[d, 0:half, 0:cols] = rdot(x_other, wg_ref[:, span]).astype(jnp.bfloat16)
        other[d, 0:half, cols : 2 * cols] = rdot(x_other, wu_ref[:, span]).astype(jnp.bfloat16)
        other[d, half : half + 16, :] = tail
        to_twin(d).start()
        mine[d, :, 0:cols] = rdot(x_mine, wg_ref[:, span])
        mine[d, :, cols : 2 * cols] = rdot(x_mine, wu_ref[:, span])
        return carry

    lax.fori_loop(0, zs, partial, 0)

    def up_copy(t):
        return pltpu.make_async_remote_copy(
            src_ref=up_out.at[t],
            dst_ref=up_in.at[t],
            send_sem=us_sem.at[t],
            recv_sem=ur_sem.at[t],
            device_id={"seq": above, "exp": e},
            device_id_type=MESH,
        )

    def dn_copy(t):
        return pltpu.make_async_remote_copy(
            src_ref=dn_out.at[t],
            dst_ref=dn_in.at[t],
            send_sem=ls_sem.at[t],
            recv_sem=lr_sem.at[t],
            device_id={"seq": below, "exp": e},
            device_id_type=MESH,
        )

    def pair_sum(d):
        to_twin(d).wait_recv()
        body = mine[d] + theirs[d, 0:half, :].astype(jnp.float32)
        sq = own_sq + join_rows(theirs[d, half : half + 16, :])
        return body, sq

    def relay(d, out, into, copy, t, first):
        body, sq = pair_sum(d)
        if not first:
            copy(t - 1).wait_recv()
            body = body + into[t - 1, 0:half, :].astype(jnp.float32)
            sq = sq + join_rows(into[t - 1, half : half + 16, :])
        out[t, 0:half, :] = body.astype(jnp.bfloat16)
        out[t, half : half + 16, :] = split_rows(sq)
        copy(t).start()

    relay(lax.rem(z + up, zs), up_out, up_in, up_copy, 0, True)
    relay(lax.rem(z + zs - down, zs), dn_out, dn_in, dn_copy, 0, True)

    def ring(t, carry):
        relay(lax.rem(z + up - t, zs), up_out, up_in, up_copy, t, False)

        @pl.when(t < down)
        def _():
            relay(lax.rem(z + zs - down + t, zs), dn_out, dn_in, dn_copy, t, False)

        return carry

    lax.fori_loop(1, up, ring, 0)

    body, sq = pair_sum(z)
    up_copy(up - 1).wait_recv()
    dn_copy(down - 1).wait_recv()
    body = (
        body
        + up_in[up - 1, 0:half, :].astype(jnp.float32)
        + dn_in[down - 1, 0:half, :].astype(jnp.float32)
    )
    sq = (
        sq
        + join_rows(up_in[up - 1, half : half + 16, :])
        + join_rows(dn_in[down - 1, half : half + 16, :])
    )
    factor = lax.rsqrt(sq[0:1, :] / features + EPS)
    row = lax.broadcasted_iota(jnp.int32, (half, wide), 0) + c * half
    lane = lax.broadcasted_iota(jnp.int32, (half, wide), 1)
    factor = jnp.sum(jnp.where(row == lane, factor, 0.0), axis=1, keepdims=True)
    gate = body[:, 0:cols] * factor
    lift = body[:, cols : 2 * cols] * factor
    ibuf[2 * z + c] = (gate / (1.0 + jnp.exp(-gate)) * lift).astype(jnp.bfloat16)

    acc[...] = jnp.zeros_like(acc)

    def visit(zb):
        block = ibuf[pl.ds(2 * zb, 2)].reshape(cap, cols)
        acc[...] += rdot(block, wd_ref[pl.ds(pl.multiple_of(zb * cols, cols), cols), :])

    ring_gather(zs, ibuf, sems, lambda: visit(z), visit)

    produced = acc[...].astype(jnp.bfloat16)
    c_send[...] = rdot(unpack_ref[...], produced).astype(jnp.bfloat16).reshape(c_send.shape)
    swap_exp(peers, c_send, c_recv, cs_sem, cr_sem)
    back = c_recv[...].reshape(peers * SRC_CAP, width)
    out_ref[...] = (hid[:, 0:width] + rdot(mix_ref[...], back)).astype(jnp.bfloat16)

    def drain(d, carry):
        to_twin(d).wait_send()
        return carry

    lax.fori_loop(0, zs, drain, 0)

    def drain_ring(t, carry):
        up_copy(t).wait_send()

        @pl.when(t < down)
        def _():
            dn_copy(t).wait_send()

        return carry

    lax.fori_loop(0, up, drain_ring, 0)


def call(body, out, scratch, number, operands, spaces=None):
    spaces = spaces or [VMEM] * len(operands)
    return pl.pallas_call(
        body,
        out_shape=out,
        in_specs=[pl.BlockSpec(memory_space=space) for space in spaces],
        out_specs=pl.BlockSpec(memory_space=VMEM),
        scratch_shapes=scratch,
        compiler_params=pltpu.CompilerParams(
            collective_id=number, has_side_effects=True, vmem_limit_bytes=VMEM_BYTES
        ),
    )(*operands)


def tables(routes, route_weights, peers, cap):
    e = lax.axis_index("exp")
    tokens = routes.shape[0]
    block = tokens // peers
    experts = jnp.arange(peers, dtype=jnp.int32)
    slot = jnp.arange(SRC_CAP, dtype=jnp.int32)
    named = lax.dynamic_slice_in_dim(routes, e * block, block, 0)
    weights = lax.dynamic_slice_in_dim(route_weights, e * block, block, 0).astype(jnp.float32)
    hit = named[:, :, None] == experts[None, None, :]
    chosen = jnp.any(hit, axis=1)
    weight = jnp.sum(jnp.where(hit, weights[:, :, None], 0.0), axis=1)
    order = jnp.arange(block, dtype=jnp.int32)
    earlier = (order[None, :] < order[:, None]).astype(jnp.bfloat16)
    rank = rdot(earlier, chosen.astype(jnp.bfloat16)).astype(jnp.int32)
    rank = jnp.where(chosen, rank, -1)
    pick = (rank.T[:, None, :] == slot[None, :, None]).astype(jnp.bfloat16)
    pick = pick.reshape(peers * SRC_CAP, block)
    mix = jnp.where(rank[:, :, None] == slot[None, None, :], weight[:, :, None], 0.0)
    mix = mix.astype(jnp.bfloat16).reshape(block, peers * SRC_CAP)
    count = jnp.sum((routes == e).astype(jnp.int32).reshape(peers, -1), axis=1)
    start = jnp.sum(jnp.where(experts[None, :] < experts[:, None], count[None, :], 0), axis=1)
    at = jnp.where(slot[None, :] < count[:, None], start[:, None] + slot[None, :], -1)
    at = at.reshape(peers * SRC_CAP)
    rows = jnp.arange(cap, dtype=jnp.int32)
    pack = (rows[:, None] == at[None, :]).astype(jnp.bfloat16)
    unpack = (at[:, None] == rows[None, :]).astype(jnp.bfloat16)
    return pick, mix, pack, unpack


def local(
    zs,
    peers,
    queries,
    latents,
    cache,
    prefix_len,
    value_up,
    out_proj,
    residual,
    norm_gain,
    w_gate,
    w_up,
    w_down,
    routes,
    route_weights,
):
    bf16, f32 = jnp.bfloat16, jnp.float32
    dma = pltpu.SemaphoreType.DMA
    tok, heads, qwidth = queries.shape
    slots = cache.shape[0]
    width = residual.shape[1]
    block = residual.shape[0]
    inner = out_proj.shape[0]
    cap = SRC_CAP * min(peers, 6)
    half = cap // 2
    wide = -(-(width + 3) // 128) * 128
    eff = w_gate.shape[2]
    cols = eff // zs
    up, down = zs // 2, zs // 2 - 1
    features = width * 2 * zs
    rows = tok * heads

    pick, mix, pack, unpack = tables(routes, route_weights, peers, cap)
    q = jnp.swapaxes(queries, 0, 1).reshape(rows, qwidth)
    head_out = call(
        functools.partial(attention_kernel, zs),
        jax.ShapeDtypeStruct((tok, inner), bf16),
        [
            VMEM((2 * zs, tok + slots, qwidth), bf16),
            VMEM((rows, 1), f32),
            VMEM((rows, 1), f32),
            VMEM((rows, LAT), f32),
        ]
        + ring_sems(zs),
        1,
        (q, latents, cache, prefix_len, value_up),
        [VMEM, VMEM, VMEM, pltpu.SMEM, VMEM],
    )
    attended = call(
        functools.partial(project_kernel, zs, peers),
        jax.ShapeDtypeStruct((block, width), f32),
        [
            VMEM((2 * zs, tok, inner), bf16),
            VMEM((peers, block, width), bf16),
            VMEM((peers, block, width), bf16),
            dma((peers,)),
            dma((peers,)),
        ]
        + ring_sems(zs),
        2,
        (head_out, out_proj),
    )
    gain = jnp.pad(norm_gain, (0, wide - width)).reshape(1, wide)
    return call(
        functools.partial(experts_kernel, zs, peers, features),
        jax.ShapeDtypeStruct((block, width), bf16),
        [
            VMEM((block, wide), f32),
            VMEM((peers, SRC_CAP, wide), bf16),
            VMEM((peers, SRC_CAP, wide), bf16),
            VMEM((cap, wide), bf16),
            VMEM((16, 2 * cols), f32),
            VMEM((zs, half, 2 * cols), f32),
            VMEM((zs, half + 16, 2 * cols), bf16),
            VMEM((zs, half + 16, 2 * cols), bf16),
            VMEM((up, half + 16, 2 * cols), bf16),
            VMEM((up, half + 16, 2 * cols), bf16),
            VMEM((down, half + 16, 2 * cols), bf16),
            VMEM((down, half + 16, 2 * cols), bf16),
            VMEM((2 * zs, half, cols), bf16),
            VMEM((cap, width), f32),
            VMEM((peers, SRC_CAP, width), bf16),
            VMEM((peers, SRC_CAP, width), bf16),
            dma((peers,)),
            dma((peers,)),
            dma((zs,)),
            dma((zs,)),
            dma((up,)),
            dma((up,)),
            dma((down,)),
            dma((down,)),
            dma((peers,)),
            dma((peers,)),
        ]
        + ring_sems(zs),
        3,
        (
            attended,
            residual,
            gain,
            pick,
            mix,
            pack,
            unpack,
            w_gate[0],
            w_up[0],
            w_down[0],
        ),
    )


def solution(mesh):
    in_specs = (
        P("seq", "exp", None),
        P("seq", None),
        P("seq", None),
        P(),
        P("exp", None, None),
        P("exp", "seq"),
        P("exp", "seq"),
        P("seq"),
        P("exp", "seq", None),
        P("exp", "seq", None),
        P("exp", None, "seq"),
        P(),
        P(),
    )
    zs, peers = mesh.shape["seq"] // 2, mesh.shape["exp"]
    return jax.shard_map(
        functools.partial(local, zs, peers),
        mesh=mesh,
        in_specs=in_specs,
        out_specs=P("exp", "seq"),
        check_vma=False,
    )
```

```python
import functools
import math

import jax
import jax.numpy as jnp
from jax import lax
from jax.experimental import pallas as pl
from jax.experimental.pallas import tpu as pltpu
from jax.sharding import PartitionSpec as P

LAT = 512
ROPE = 64
QK_NOPE = 128
SRC_CAP = 32

EPS = 1e-06
FLOOR = -1e30
SCALE = (QK_NOPE + ROPE) ** (-0.5)
MESH = pl.DeviceIdType.MESH
VMEM = pltpu.VMEM
VMEM_BYTES = 48 * 1024 * 1024


def rdot(a, b):
    return jnp.dot(a, b, preferred_element_type=jnp.float32)


def rdot_t(a, b):
    return lax.dot_general(
        a, b, (((1,), (1,)), ((), ())), preferred_element_type=jnp.float32
    )


def place(zs):
    s = lax.axis_index("seq")
    z, c = s // 2, lax.rem(s, 2)
    above = lax.rem(z + 1, zs) * 2 + c
    below = lax.rem(z + zs - 1, zs) * 2 + c
    twin = 2 * z + 1 - c
    return z, c, above, below, twin


def greet(zs, reach, peers):
    z, c, _, _, twin = place(zs)
    s = 2 * z + c
    e = lax.axis_index("exp")
    barrier = pltpu.get_barrier_semaphore()

    def hello(seq, exp):
        pl.semaphore_signal(
            barrier, inc=1, device_id={"seq": seq, "exp": exp}, device_id_type=MESH
        )

    hello(twin, e)
    for k in range(1, reach + 1):
        hello(lax.rem(z + k, zs) * 2 + c, e)
        hello(lax.rem(z + zs - k, zs) * 2 + c, e)

    def along(j, carry):
        hello(s, lax.rem(e + j, peers))
        return carry

    lax.fori_loop(1, peers, along, 0)
    pl.semaphore_wait(barrier, 1 + 2 * reach + peers - 1)


def remote(src, dst, ssem, rsem, seq, exp):
    return pltpu.make_async_remote_copy(
        src_ref=src,
        dst_ref=dst,
        send_sem=ssem,
        recv_sem=rsem,
        device_id={"seq": seq, "exp": exp},
        device_id_type=MESH,
    )


def ring_sems(zs, parts):
    dma = pltpu.SemaphoreType.DMA
    return [dma((zs, parts)), dma((zs, parts)), dma((zs,)), dma((zs,))]


def ring_gather(zs, buf, sems, own, visit, stride=1, parts=1, after=None, delay=0):
    rs, rr, ts, tr = sems
    up, down = zs // 2, zs // 2 - 1
    z, c, _, _, twin = place(zs)
    e = lax.axis_index("exp")
    size = buf.shape[1] // parts

    def far(side, k):
        return lax.rem(z + (zs - k if side == 0 else k), zs)

    def index(side, k):
        return k if side == 0 else up + k

    def hop(side, k, p, step):
        slot = buf.at[2 * far(side, k) + c, pl.ds(p * size, size)]
        i = index(side, k + step)
        to = lax.rem(z + (step if side == 0 else zs - step), zs) * 2 + c
        return remote(slot, slot, rs.at[i, p], rr.at[i, p], to, e)

    def came(side, k, p):
        slot = buf.at[2 * far(side, k) + c, pl.ds(p * size, size)]
        i = index(side, k)
        return remote(slot, slot, rs.at[i, p], rr.at[i, p], twin, e)

    def share(i, zb, core):
        slot = buf.at[2 * zb + core]
        return remote(slot, slot, ts.at[i], tr.at[i], twin, e)

    limits = (up, down)
    for p in range(parts):
        for k in range(1, stride + 1):
            for side in range(2):
                if k <= limits[side]:
                    hop(side, 0, p, k).start()
    share(0, z, c).start()

    def step(k, carry):
        for side in range(2):

            @pl.when(k <= limits[side])
            def _():
                for p in range(parts):
                    came(side, k, p).wait_recv()

                    @pl.when(k + stride <= limits[side])
                    def _():
                        hop(side, k, p, stride).start()

                share(index(side, k), far(side, k), c).start()

        @pl.when(k == 1)
        def _():
            share(0, z, 1 - c).wait_recv()
            own()

        def both(j, act):
            def one(side, inner):
                @pl.when((side == 0) | (j <= down))
                def _():
                    zb = lax.rem(z + jnp.where(side == 0, zs - j, j), zs)
                    act(zb, jnp.where(side == 0, j, up + j))

                return inner

            lax.fori_loop(0, 2, one, 0)

        def arrive(zb, i):
            share(i, zb, 1 - c).wait_recv()
            visit(zb)

        @pl.when((k > 1) & (k <= up + 1))
        def _():
            both(k - 1, arrive)

        if after is not None:

            @pl.when(k == delay + 1)
            def _():
                after(z)

            @pl.when(k > delay + 1)
            def _():
                both(k - 1 - delay, lambda zb, i: after(zb))

        return carry

    lax.fori_loop(1, up + 2 + delay, step, 0)

    def drain(k, carry):
        for side in range(2):

            @pl.when(k <= limits[side])
            def _():
                for p in range(parts):
                    came(side, k, p).wait_send()
                share(index(side, k), far(side, k), c).wait_send()

        return carry

    lax.fori_loop(1, up + 1, drain, 0)
    share(0, z, c).wait_send()


def attention_kernel(
    zs,
    peers,
    side,
    q_ref,
    lat_ref,
    cache_ref,
    live_ref,
    vup_ref,
    out_ref,
    buf,
    cbuf,
    best,
    total,
    acc,
    rs,
    rr,
    cs,
    cr,
    ls,
    lr,
    ms,
    mr,
    ts,
    tr,
    ns,
    nr,
):
    tok = lat_ref.shape[0]
    slots = cache_ref.shape[0]
    rows, width = q_ref.shape
    heads = rows // tok
    stride = 2
    up, down = zs // 2, zs // 2 - 1
    limits = (up, down)
    z, c, _, _, twin = place(zs)
    s = 2 * z + c
    e = lax.axis_index("exp")
    ey, ex = e // side, lax.rem(e, side)
    q = jnp.where(c == 0, ex, ey)
    size = tok // side

    def line(j):
        p = lax.rem(q + j, side)
        return jnp.where(c == 0, ey * side + p, p * side + ex)

    greet(zs, stride, peers)
    buf[s] = lat_ref[...]
    cbuf[s] = cache_ref[...]

    def absorb(keys, visible, first):
        scores = rdot_t(q_ref[...], keys) * SCALE
        if visible is not None:
            scores = jnp.where(visible, scores, FLOOR)
        top = jnp.max(scores, axis=1, keepdims=True)
        if first:
            newest = top
            weights = jnp.exp(scores - newest)
            total[...] = jnp.sum(weights, axis=1, keepdims=True)
            acc[...] = rdot(weights.astype(jnp.bfloat16), keys[:, :LAT])
        else:
            before = best[...]
            newest = jnp.maximum(before, top)
            fade = jnp.exp(before - newest)
            weights = jnp.exp(scores - newest)
            total[...] = total[...] * fade + jnp.sum(weights, axis=1, keepdims=True)
            acc[...] = acc[...] * fade + rdot(weights.astype(jnp.bfloat16), keys[:, :LAT])
        best[...] = newest

    def pair(zb):
        return buf[pl.ds(2 * zb, 2)].reshape(2 * tok, width)

    def far(way, k):
        return lax.rem(z + (zs - k if way == 0 else k), zs)

    def index(way, k):
        return k if way == 0 else up + k

    def piece(zb, p):
        return buf.at[2 * zb + c, pl.ds(pl.multiple_of(p * size, size), size)]

    def hop(way, k, step):
        i = index(way, k + step)
        to = lax.rem(z + (step if way == 0 else zs - step), zs) * 2 + c
        slot = piece(far(way, k), q)
        return remote(slot, slot, rs.at[i], rr.at[i], to, e)

    def cache_hop(way, k, step):
        i = index(way, k + step)
        to = lax.rem(z + (step if way == 0 else zs - step), zs) * 2 + c
        slot = cbuf.at[2 * far(way, k) + c]
        return remote(slot, slot, cs.at[i], cr.at[i], to, e)

    def came(way, k):
        i = index(way, k)
        slot = piece(far(way, k), q)
        return remote(slot, slot, rs.at[i], rr.at[i], twin, e)

    def cache_came(way, k):
        i = index(way, k)
        slot = cbuf.at[2 * far(way, k) + c]
        return remote(slot, slot, cs.at[i], cr.at[i], twin, e)

    def spread(i, zb, j):
        slot = piece(zb, q)
        return remote(slot, slot, ls.at[i, j], lr.at[i, j], s, line(j))

    def spread_in(i, zb, j):
        slot = piece(zb, lax.rem(q + side - j, side))
        return remote(slot, slot, ls.at[i, j], lr.at[i, j], s, line(j))

    def cache_spread(i, zb, j):
        slot = cbuf.at[2 * zb + c]
        return remote(slot, slot, ms.at[i, j], mr.at[i], s, line(j))

    def share(i, zb, core):
        slot = buf.at[2 * zb + core]
        return remote(slot, slot, ts.at[i], tr.at[i], twin, e)

    def cache_share(i, zb, core):
        slot = cbuf.at[2 * zb + core]
        return remote(slot, slot, ns.at[i], nr.at[i], twin, e)

    def carries(zb):
        return lax.rem(zb, side) == q

    for k in range(1, stride + 1):
        for way in range(2):
            if k <= limits[way]:
                hop(way, 0, k).start()

                @pl.when(carries(z))
                def _():
                    cache_hop(way, 0, k).start()

    share(0, z, c).start()
    cache_share(0, z, c).start()

    def step(k, carry):
        for way in range(2):
            zb, i = far(way, k), index(way, k)

            @pl.when(k <= limits[way])
            def _():
                came(way, k).wait_recv()

                @pl.when(k + stride <= limits[way])
                def _():
                    hop(way, k, stride).start()

                @pl.when(zb < z)
                def _():
                    for j in range(1, side):
                        spread(i, zb, j).start()

                @pl.when(carries(zb))
                def _():
                    cache_came(way, k).wait_recv()

                    @pl.when(k + stride <= limits[way])
                    def _():
                        cache_hop(way, k, stride).start()

                    for j in range(1, side):
                        cache_spread(i, zb, j).start()

        for way in range(2):
            zl, il = far(way, k - 1), index(way, k - 1)

            @pl.when((k > 1) & (k - 1 <= limits[way]))
            def _():
                @pl.when(zl < z)
                def _():
                    for j in range(1, side):
                        spread_in(il, zl, j).wait_recv()
                    share(il, zl, c).start()

                @pl.when(jnp.logical_not(carries(zl)))
                def _():
                    cache_spread(il, zl, 1).wait_recv()

                cache_share(il, zl, c).start()

        @pl.when(k == 2)
        def _():
            share(0, z, 1 - c).wait_recv()
            cache_share(0, z, 1 - c).wait_recv()
            row = lax.broadcasted_iota(jnp.int32, (rows, 2 * tok), 0)
            key = lax.broadcasted_iota(jnp.int32, (rows, 2 * tok), 1)
            absorb(pair(z), key <= lax.rem(row, tok) + c * tok, True)

        def one(way, inner):
            j = k - 2

            @pl.when((way == 0) | (j <= down))
            def _():
                zb = lax.rem(z + jnp.where(way == 0, zs - j, j), zs)
                i = jnp.where(way == 0, j, up + j)
                cache_share(i, zb, 1 - c).wait_recv()

                @pl.when(zb < z)
                def _():
                    share(i, zb, 1 - c).wait_recv()
                    absorb(pair(zb), None, False)

            return inner

        @pl.when(k > 2)
        def _():
            lax.fori_loop(0, 2, one, 0)

        return carry

    lax.fori_loop(1, up + 3, step, 0)

    live = live_ref[0]
    group = max(1, min(256, slots * 2 * zs) // slots)

    def prefix(i, carry):
        keys = cbuf[pl.ds(i * group, group)].reshape(group * slots, width)
        key = lax.broadcasted_iota(jnp.int32, (rows, group * slots), 1) + i * (group * slots)
        absorb(keys, key < live, False)
        return carry

    lax.fori_loop(0, 2 * zs // group, prefix, 0)

    for h in range(heads):
        part = pl.ds(h * tok, tok)
        context = (acc[part, :] / total[part, :]).astype(jnp.bfloat16)
        vh = vup_ref.shape[2]
        out_ref[:, h * vh : (h + 1) * vh] = rdot(context, vup_ref[h]).astype(jnp.bfloat16)

    def drain(k, carry):
        for way in range(2):
            zb, i = far(way, k), index(way, k)

            @pl.when(k <= limits[way])
            def _():
                came(way, k).wait_send()

                @pl.when(zb < z)
                def _():
                    for j in range(1, side):
                        spread(i, zb, j).wait_send()
                    share(i, zb, c).wait_send()

                origin = jnp.maximum(k - stride, 0)

                @pl.when(carries(lax.rem(z + (zs - origin if way == 0 else origin), zs)))
                def _():
                    cache_came(way, k).wait_send()

                @pl.when(carries(zb))
                def _():
                    for j in range(1, side):
                        cache_spread(i, zb, j).wait_send()

                cache_share(i, zb, c).wait_send()

        return carry

    lax.fori_loop(1, up + 1, drain, 0)
    share(0, z, c).wait_send()
    cache_share(0, z, c).wait_send()


def project_kernel(
    zs,
    peers,
    side,
    head_ref,
    proj_ref,
    out_ref,
    buf,
    terms,
    row_in,
    sums,
    col_in,
    x_send,
    x_recv,
    y_send,
    y_recv,
    *sems,
):
    tok, inner = head_ref.shape
    z, c, _, _, _ = place(zs)
    s = 2 * z + c
    e = lax.axis_index("exp")
    ey, ex = e // side, lax.rem(e, side)
    greet(zs, 1, peers)
    buf[s] = head_ref[...]

    def along_x(zb):
        to_y, to_x = zb // side, lax.rem(zb, side)
        return remote(
            terms.at[zb],
            row_in.at[to_y, ex],
            x_send.at[zb],
            x_recv.at[to_y, ex],
            s,
            ey * side + to_x,
        )

    def along_y(to_y):
        return remote(
            sums.at[to_y], col_in.at[ey], y_send.at[to_y], y_recv.at[ey], s, to_y * side + ex
        )

    def visit(zb):
        rows = buf[pl.ds(2 * zb, 2)].reshape(2 * tok, inner)
        terms[zb] = rdot(rows, proj_ref[...]).astype(jnp.bfloat16)

        @pl.when(lax.rem(zb, side) != ex)
        def _():
            along_x(zb).start()

    def after(zb):
        @pl.when(lax.rem(zb, side) == ex)
        def _():
            to_y = zb // side
            part = terms[zb].astype(jnp.float32)
            for j in range(1, side):
                g = lax.rem(ex + j, side)
                slot = row_in.at[to_y, g]
                remote(
                    slot, slot, x_send.at[zb], x_recv.at[to_y, g], s, ey * side + g
                ).wait_recv()
                part = part + row_in[to_y, g].astype(jnp.float32)

            @pl.when(to_y == ey)
            def _():
                out_ref[...] = part

            @pl.when(to_y != ey)
            def _():
                sums[to_y] = part.astype(jnp.bfloat16)
                along_y(to_y).start()

    ring_gather(zs, buf, sems, lambda: visit(z), visit, parts=2, after=after, delay=2)

    for j in range(1, side):
        g = lax.rem(ey + j, side)
        slot = col_in.at[g]
        remote(slot, slot, y_send.at[g], y_recv.at[g], s, g * side + ex).wait_recv()
        out_ref[...] += col_in[g].astype(jnp.float32)

    def drain(zb, carry):
        @pl.when(lax.rem(zb, side) != ex)
        def _():
            along_x(zb).wait_send()

        return carry

    lax.fori_loop(0, zs, drain, 0)
    for j in range(1, side):
        along_y(lax.rem(ey + j, side)).wait_send()


def swap_exp(peers, send, recv, s_sem, r_sem):
    s = lax.axis_index("seq")
    e = lax.axis_index("exp")

    def copy(j, to, slot):
        return pltpu.make_async_remote_copy(
            src_ref=send.at[to],
            dst_ref=recv.at[slot],
            send_sem=s_sem.at[j],
            recv_sem=r_sem.at[j],
            device_id={"seq": s, "exp": to},
            device_id_type=MESH,
        )

    def start(j, carry):
        copy(j, lax.rem(e + j, peers), e).start()
        return carry

    lax.fori_loop(1, peers, start, 0)
    recv[e] = send[e]

    def finish(j, carry):
        copy(j, lax.rem(e + j, peers), lax.rem(e + peers - j, peers)).wait_recv()
        return carry

    lax.fori_loop(1, peers, finish, 0)

    def drain(j, carry):
        copy(j, lax.rem(e + j, peers), e).wait_send()
        return carry

    lax.fori_loop(1, peers, drain, 0)


def split_rows(v):
    row = lax.broadcasted_iota(jnp.int32, v.shape, 0)
    high = v.astype(jnp.bfloat16).astype(jnp.float32)
    rest = v - high
    mid = rest.astype(jnp.bfloat16).astype(jnp.float32)
    low = rest - mid
    parts = jnp.where(row == 0, high, jnp.where(row == 1, mid, jnp.where(row == 2, low, 0.0)))
    return parts.astype(jnp.bfloat16)


def join_rows(block):
    return jnp.sum(block.astype(jnp.float32), axis=0, keepdims=True)


def experts_kernel(
    zs,
    peers,
    features,
    att_ref,
    res_ref,
    gain_ref,
    pick_ref,
    mix_ref,
    pack_ref,
    unpack_ref,
    wg_ref,
    wu_ref,
    wd_ref,
    out_ref,
    wgu,
    hid,
    d_send,
    d_recv,
    xs,
    xo,
    sqv,
    mine,
    other,
    theirs,
    up_out,
    up_in,
    dn_out,
    dn_in,
    ibuf,
    acc,
    c_send,
    c_recv,
    w_sem,
    ds_sem,
    dr_sem,
    ps_sem,
    pr_sem,
    us_sem,
    ur_sem,
    ls_sem,
    lr_sem,
    cs_sem,
    cr_sem,
    *sems,
):
    tokens, width = res_ref.shape
    wide = hid.shape[1]
    cap = pack_ref.shape[0]
    half = cap // 2
    cols = ibuf.shape[2]
    up, down = zs // 2, zs // 2 - 1
    z, c, above, below, twin = place(zs)
    e = lax.axis_index("exp")

    def load(d, which):
        span = pl.ds(pl.multiple_of(d * cols, cols), cols)
        return pltpu.make_async_copy(
            (wg_ref, wu_ref)[which].at[:, span],
            wgu.at[d, :, pl.ds(which * cols, cols)],
            w_sem.at[d, which],
        )

    def load_all(i, carry):
        t = i // 2
        d = lax.rem(z + jnp.where(lax.rem(i, 2) == 0, up - t, zs - down + t), zs)
        load(d, 0).start()
        load(d, 1).start()
        return carry

    lax.fori_loop(0, zs, load_all, 0)
    greet(zs, 2, peers)

    hid[...] = jnp.zeros_like(hid)
    hid[:, 0:width] = res_ref[...].astype(jnp.float32) + att_ref[...]
    hidden = hid[...]
    squares = jnp.sum(hidden * hidden, axis=1, keepdims=True)
    high = squares.astype(jnp.bfloat16).astype(jnp.float32)
    rest = squares - high
    mid = rest.astype(jnp.bfloat16).astype(jnp.float32)
    low = rest - mid
    lane = lax.broadcasted_iota(jnp.int32, (tokens, wide), 1)
    ext = jnp.where(
        lane < width,
        hidden * gain_ref[...],
        jnp.where(
            lane == width,
            high,
            jnp.where(lane == width + 1, mid, jnp.where(lane == width + 2, low, 0.0)),
        ),
    ).astype(jnp.bfloat16)
    d_send[...] = rdot(pick_ref[...], ext).astype(jnp.bfloat16).reshape(d_send.shape)
    swap_exp(peers, d_send, d_recv, ds_sem, dr_sem)

    arrived = d_recv[...].reshape(peers * SRC_CAP, wide)
    packed = rdot(pack_ref[...], arrived).astype(jnp.bfloat16)
    xs[...] = packed
    mark = lax.broadcasted_iota(jnp.int32, (16, wide), 1)
    ones = jnp.where((mark >= width) & (mark < width + 3), 1.0, 0.0).astype(jnp.bfloat16)
    sqv[...] = jnp.zeros_like(sqv)
    sqv[:, 0:cap] = rdot_t(ones, packed)
    own_sq = sqv[...]
    tail = split_rows(own_sq)
    xo[0:half, :] = xs[pl.ds(pl.multiple_of(c * half, 16), half), 0:width]
    xo[half:cap, :] = xs[pl.ds(pl.multiple_of((1 - c) * half, 16), half), 0:width]

    def to_twin(d):
        return pltpu.make_async_remote_copy(
            src_ref=other.at[d],
            dst_ref=theirs.at[d],
            send_sem=ps_sem.at[d],
            recv_sem=pr_sem.at[d],
            device_id={"seq": twin, "exp": e},
            device_id_type=MESH,
        )

    def partial(d):
        load(d, 0).wait()
        load(d, 1).wait()
        both = rdot(xo[...], wgu[d])
        other[d, 0:half, :] = both[half:].astype(jnp.bfloat16)
        other[d, half : half + 16, :] = tail
        to_twin(d).start()
        mine[d] = both[:half]

    def up_copy(t):
        return pltpu.make_async_remote_copy(
            src_ref=up_out.at[t],
            dst_ref=up_in.at[t],
            send_sem=us_sem.at[t],
            recv_sem=ur_sem.at[t],
            device_id={"seq": above, "exp": e},
            device_id_type=MESH,
        )

    def dn_copy(t):
        return pltpu.make_async_remote_copy(
            src_ref=dn_out.at[t],
            dst_ref=dn_in.at[t],
            send_sem=ls_sem.at[t],
            recv_sem=lr_sem.at[t],
            device_id={"seq": below, "exp": e},
            device_id_type=MESH,
        )

    def pair_sum(d):
        to_twin(d).wait_recv()
        body = mine[d] + theirs[d, 0:half, :].astype(jnp.float32)
        sq = own_sq + join_rows(theirs[d, half : half + 16, :])
        return body, sq

    def relay(d, out, into, copy, t, first):
        body, sq = pair_sum(d)
        if not first:
            copy(t - 1).wait_recv()
            body = body + into[t - 1, 0:half, :].astype(jnp.float32)
            sq = sq + join_rows(into[t - 1, half : half + 16, :])
        out[t, 0:half, :] = body.astype(jnp.bfloat16)
        out[t, half : half + 16, :] = split_rows(sq)
        copy(t).start()

    def up_dest(t):
        return lax.rem(z + up - t, zs)

    def dn_dest(t):
        return lax.rem(z + zs - down + t, zs)

    partial(up_dest(0))
    partial(dn_dest(0))
    partial(up_dest(1))
    partial(dn_dest(1))
    relay(up_dest(0), up_out, up_in, up_copy, 0, True)
    relay(dn_dest(0), dn_out, dn_in, dn_copy, 0, True)

    def ring(t, carry):
        @pl.when(t < up - 1)
        def _():
            partial(up_dest(t + 1))
            partial(dn_dest(t + 1))

        relay(up_dest(t), up_out, up_in, up_copy, t, False)

        @pl.when(t < down)
        def _():
            relay(dn_dest(t), dn_out, dn_in, dn_copy, t, False)

        return carry

    lax.fori_loop(1, up, ring, 0)

    body, sq = pair_sum(z)
    up_copy(up - 1).wait_recv()
    dn_copy(down - 1).wait_recv()
    body = (
        body
        + up_in[up - 1, 0:half, :].astype(jnp.float32)
        + dn_in[down - 1, 0:half, :].astype(jnp.float32)
    )
    sq = (
        sq
        + join_rows(up_in[up - 1, half : half + 16, :])
        + join_rows(dn_in[down - 1, half : half + 16, :])
    )
    factor = lax.rsqrt(sq[0:1, :] / features + EPS)
    row = lax.broadcasted_iota(jnp.int32, (half, wide), 0) + c * half
    lane = lax.broadcasted_iota(jnp.int32, (half, wide), 1)
    factor = jnp.sum(jnp.where(row == lane, factor, 0.0), axis=1, keepdims=True)
    gate = body[:, 0:cols] * factor
    lift = body[:, cols : 2 * cols] * factor
    ibuf[2 * z + c] = (gate / (1.0 + jnp.exp(-gate)) * lift).astype(jnp.bfloat16)

    acc[...] = jnp.zeros_like(acc)

    def visit(zb):
        block = ibuf[pl.ds(2 * zb, 2)].reshape(cap, cols)
        acc[...] += rdot(block, wd_ref[pl.ds(pl.multiple_of(zb * cols, cols), cols), :])

    ring_gather(zs, ibuf, sems, lambda: visit(z), visit, stride=2)

    produced = acc[...].astype(jnp.bfloat16)
    c_send[...] = rdot(unpack_ref[...], produced).astype(jnp.bfloat16).reshape(c_send.shape)
    swap_exp(peers, c_send, c_recv, cs_sem, cr_sem)
    back = c_recv[...].reshape(peers * SRC_CAP, width)
    out_ref[...] = (hid[:, 0:width] + rdot(mix_ref[...], back)).astype(jnp.bfloat16)

    def drain(d, carry):
        to_twin(d).wait_send()
        return carry

    lax.fori_loop(0, zs, drain, 0)

    def drain_ring(t, carry):
        up_copy(t).wait_send()

        @pl.when(t < down)
        def _():
            dn_copy(t).wait_send()

        return carry

    lax.fori_loop(0, up, drain_ring, 0)


def call(body, out, scratch, number, operands, spaces=None):
    spaces = spaces or [VMEM] * len(operands)
    return pl.pallas_call(
        body,
        out_shape=out,
        in_specs=[pl.BlockSpec(memory_space=space) for space in spaces],
        out_specs=pl.BlockSpec(memory_space=VMEM),
        scratch_shapes=scratch,
        compiler_params=pltpu.CompilerParams(
            collective_id=number, has_side_effects=True, vmem_limit_bytes=VMEM_BYTES
        ),
    )(*operands)


def tables(routes, route_weights, peers, cap):
    e = lax.axis_index("exp")
    tokens = routes.shape[0]
    block = tokens // peers
    experts = jnp.arange(peers, dtype=jnp.int32)
    slot = jnp.arange(SRC_CAP, dtype=jnp.int32)
    named = lax.dynamic_slice_in_dim(routes, e * block, block, 0)
    weights = lax.dynamic_slice_in_dim(route_weights, e * block, block, 0).astype(jnp.float32)
    hit = named[:, :, None] == experts[None, None, :]
    chosen = jnp.any(hit, axis=1)
    weight = jnp.sum(jnp.where(hit, weights[:, :, None], 0.0), axis=1)
    order = jnp.arange(block, dtype=jnp.int32)
    earlier = (order[None, :] < order[:, None]).astype(jnp.bfloat16)
    rank = rdot(earlier, chosen.astype(jnp.bfloat16)).astype(jnp.int32)
    rank = jnp.where(chosen, rank, -1)
    pick = (rank.T[:, None, :] == slot[None, :, None]).astype(jnp.bfloat16)
    pick = pick.reshape(peers * SRC_CAP, block)
    mix = jnp.where(rank[:, :, None] == slot[None, None, :], weight[:, :, None], 0.0)
    mix = mix.astype(jnp.bfloat16).reshape(block, peers * SRC_CAP)
    count = jnp.sum((routes == e).astype(jnp.int32).reshape(peers, -1), axis=1)
    start = jnp.sum(jnp.where(experts[None, :] < experts[:, None], count[None, :], 0), axis=1)
    at = jnp.where(slot[None, :] < count[:, None], start[:, None] + slot[None, :], -1)
    at = at.reshape(peers * SRC_CAP)
    rows = jnp.arange(cap, dtype=jnp.int32)
    pack = (rows[:, None] == at[None, :]).astype(jnp.bfloat16)
    unpack = (at[:, None] == rows[None, :]).astype(jnp.bfloat16)
    return pick, mix, pack, unpack


def local(
    zs,
    peers,
    queries,
    latents,
    cache,
    prefix_len,
    value_up,
    out_proj,
    residual,
    norm_gain,
    w_gate,
    w_up,
    w_down,
    routes,
    route_weights,
):
    bf16, f32 = jnp.bfloat16, jnp.float32
    dma = pltpu.SemaphoreType.DMA
    tok, heads, qwidth = queries.shape
    slots = cache.shape[0]
    width = residual.shape[1]
    block = residual.shape[0]
    inner = out_proj.shape[0]
    cap = SRC_CAP * min(peers, 6)
    half = cap // 2
    wide = -(-(width + 3) // 128) * 128
    eff = w_gate.shape[2]
    cols = eff // zs
    up, down = zs // 2, zs // 2 - 1
    features = width * 2 * zs
    rows = tok * heads

    side = math.isqrt(peers)

    pick, mix, pack, unpack = tables(routes, route_weights, peers, cap)
    q = jnp.swapaxes(queries, 0, 1).reshape(rows, qwidth)
    head_out = call(
        functools.partial(attention_kernel, zs, peers, side),
        jax.ShapeDtypeStruct((tok, inner), bf16),
        [
            VMEM((2 * zs, tok, qwidth), bf16),
            VMEM((2 * zs, slots, qwidth), bf16),
            VMEM((rows, 1), f32),
            VMEM((rows, 1), f32),
            VMEM((rows, LAT), f32),
            dma((zs,)),
            dma((zs,)),
            dma((zs,)),
            dma((zs,)),
            dma((zs, side)),
            dma((zs, side)),
            dma((zs, side)),
            dma((zs,)),
            dma((zs,)),
            dma((zs,)),
            dma((zs,)),
            dma((zs,)),
        ],
        1,
        (q, latents, cache, prefix_len, value_up),
        [VMEM, VMEM, VMEM, pltpu.SMEM, VMEM],
    )
    attended = call(
        functools.partial(project_kernel, zs, peers, side),
        jax.ShapeDtypeStruct((block, width), f32),
        [
            VMEM((2 * zs, tok, inner), bf16),
            VMEM((peers, block, width), bf16),
            VMEM((side, side, block, width), bf16),
            VMEM((side, block, width), bf16),
            VMEM((side, block, width), bf16),
            dma((peers,)),
            dma((side, side)),
            dma((side,)),
            dma((side,)),
        ]
        + ring_sems(zs, 2),
        2,
        (head_out, out_proj),
    )
    gain = jnp.pad(norm_gain, (0, wide - width)).reshape(1, wide)
    return call(
        functools.partial(experts_kernel, zs, peers, features),
        jax.ShapeDtypeStruct((block, width), bf16),
        [
            VMEM((zs, width, 2 * cols), bf16),
            VMEM((block, wide), f32),
            VMEM((peers, SRC_CAP, wide), bf16),
            VMEM((peers, SRC_CAP, wide), bf16),
            VMEM((cap, wide), bf16),
            VMEM((cap, width), bf16),
            VMEM((16, 2 * cols), f32),
            VMEM((zs, half, 2 * cols), f32),
            VMEM((zs, half + 16, 2 * cols), bf16),
            VMEM((zs, half + 16, 2 * cols), bf16),
            VMEM((up, half + 16, 2 * cols), bf16),
            VMEM((up, half + 16, 2 * cols), bf16),
            VMEM((down, half + 16, 2 * cols), bf16),
            VMEM((down, half + 16, 2 * cols), bf16),
            VMEM((2 * zs, half, cols), bf16),
            VMEM((cap, width), f32),
            VMEM((peers, SRC_CAP, width), bf16),
            VMEM((peers, SRC_CAP, width), bf16),
            dma((zs, 2)),
            dma((peers,)),
            dma((peers,)),
            dma((zs,)),
            dma((zs,)),
            dma((up,)),
            dma((up,)),
            dma((down,)),
            dma((down,)),
            dma((peers,)),
            dma((peers,)),
        ]
        + ring_sems(zs, 1),
        3,
        (
            attended,
            residual,
            gain,
            pick,
            mix,
            pack,
            unpack,
            w_gate[0],
            w_up[0],
            w_down[0],
        ),
        [VMEM] * 7 + [pl.ANY, pl.ANY, VMEM],
    )


def solution(mesh):
    in_specs = (
        P("seq", "exp", None),
        P("seq", None),
        P("seq", None),
        P(),
        P("exp", None, None),
        P("exp", "seq"),
        P("exp", "seq"),
        P("seq"),
        P("exp", "seq", None),
        P("exp", "seq", None),
        P("exp", None, "seq"),
        P(),
        P(),
    )
    zs, peers = mesh.shape["seq"] // 2, mesh.shape["exp"]
    return jax.shard_map(
        functools.partial(local, zs, peers),
        mesh=mesh,
        in_specs=in_specs,
        out_specs=P("exp", "seq"),
        check_vma=False,
    )
```

```python
import functools
import math
import types

import jax
import jax.numpy as jnp
from jax import lax
from jax.experimental import pallas as pl
from jax.experimental.pallas import tpu as pltpu
from jax.sharding import PartitionSpec as P

LAT = 512
ROPE = 64
QK_NOPE = 128
SRC_CAP = 32

EPS = 1e-06
FLOOR = -1e30
SCALE2 = (QK_NOPE + ROPE) ** (-0.5) * math.log2(math.e)
MESH = pl.DeviceIdType.MESH
VMEM = pltpu.VMEM
VMEM_BYTES = 48 * 1024 * 1024


def rdot(a, b):
    return jnp.dot(a, b, preferred_element_type=jnp.float32)


def rdot_t(a, b):
    return lax.dot_general(
        a, b, (((1,), (1,)), ((), ())), preferred_element_type=jnp.float32
    )


def rdot_tn(a, b):
    return lax.dot_general(
        a, b, (((0,), (0,)), ((), ())), preferred_element_type=jnp.float32
    )


def place(zs):
    s = lax.axis_index("seq")
    z, c = s // 2, lax.rem(s, 2)
    above = lax.rem(z + 1, zs) * 2 + c
    below = lax.rem(z + zs - 1, zs) * 2 + c
    twin = 2 * z + 1 - c
    return z, c, above, below, twin


def greet(zs, reach, peers):
    z, c, _, _, twin = place(zs)
    s = 2 * z + c
    e = lax.axis_index("exp")
    barrier = pltpu.get_barrier_semaphore()

    def hello(seq, exp):
        pl.semaphore_signal(
            barrier, inc=1, device_id={"seq": seq, "exp": exp}, device_id_type=MESH
        )

    def along(j, carry):
        hello(s, lax.rem(e + j, peers))
        return carry

    lax.fori_loop(1, peers, along, 0)
    for k in range(1, reach + 1):
        hello(lax.rem(z + k, zs) * 2 + c, e)
        hello(lax.rem(z + zs - k, zs) * 2 + c, e)
    hello(twin, e)
    return lambda: pl.semaphore_wait(barrier, 1 + 2 * reach + peers - 1)


def remote(src, dst, ssem, rsem, seq, exp):
    return pltpu.make_async_remote_copy(
        src_ref=src,
        dst_ref=dst,
        send_sem=ssem,
        recv_sem=rsem,
        device_id={"seq": seq, "exp": exp},
        device_id_type=MESH,
    )


def ring_sems(zs, parts):
    dma = pltpu.SemaphoreType.DMA
    return [dma((zs, parts)), dma((zs, parts)), dma((zs,)), dma((zs,))]


def ring_gather(
    zs, buf, sems, own, visit, stride=1, parts=1, after=None, delay=0, meanwhile=None
):
    rs, rr, ts, tr = sems
    up, down = zs // 2, zs // 2 - 1
    z, c, _, _, twin = place(zs)
    e = lax.axis_index("exp")
    size = buf.shape[1] // parts

    def far(side, k):
        return lax.rem(z + (zs - k if side == 0 else k), zs)

    def index(side, k):
        return k if side == 0 else up + k

    def hop(side, k, p, step):
        slot = buf.at[2 * far(side, k) + c, pl.ds(p * size, size)]
        i = index(side, k + step)
        to = lax.rem(z + (step if side == 0 else zs - step), zs) * 2 + c
        return remote(slot, slot, rs.at[i, p], rr.at[i, p], to, e)

    def came(side, k, p):
        slot = buf.at[2 * far(side, k) + c, pl.ds(p * size, size)]
        i = index(side, k)
        return remote(slot, slot, rs.at[i, p], rr.at[i, p], twin, e)

    def share(i, zb, core):
        slot = buf.at[2 * zb + core]
        return remote(slot, slot, ts.at[i], tr.at[i], twin, e)

    limits = (up, down)
    for p in range(parts):
        for k in range(1, stride + 1):
            for side in range(2):
                if k <= limits[side]:
                    hop(side, 0, p, k).start()
    share(0, z, c).start()
    if meanwhile is not None:
        meanwhile()

    def step(k, carry):
        for p in range(parts):
            for side in range(2):

                @pl.when(k <= limits[side])
                def _():
                    came(side, k, p).wait_recv()

                    @pl.when(k + stride <= limits[side])
                    def _():
                        hop(side, k, p, stride).start()

                    if p == parts - 1:
                        share(index(side, k), far(side, k), c).start()

        @pl.when(k == 1)
        def _():
            share(0, z, 1 - c).wait_recv()
            own()

        def both(j, act):
            def one(side, inner):
                @pl.when((side == 0) | (j <= down))
                def _():
                    zb = lax.rem(z + jnp.where(side == 0, zs - j, j), zs)
                    act(zb, jnp.where(side == 0, j, up + j))

                return inner

            lax.fori_loop(0, 2, one, 0)

        def arrive(zb, i):
            share(i, zb, 1 - c).wait_recv()
            visit(zb)

        @pl.when((k > 1) & (k <= up + 1))
        def _():
            both(k - 1, arrive)

        if after is not None:

            @pl.when(k == delay + 1)
            def _():
                after(z)

            @pl.when(k > delay + 1)
            def _():
                both(k - 1 - delay, lambda zb, i: after(zb))

        return carry

    lax.fori_loop(1, up + 2 + delay, step, 0)

    def settle():
        def drain(k, carry):
            for side in range(2):

                @pl.when(k <= limits[side])
                def _():
                    for p in range(parts):
                        came(side, k, p).wait_send()
                    share(index(side, k), far(side, k), c).wait_send()

            return carry

        lax.fori_loop(1, up + 1, drain, 0)
        share(0, z, c).wait_send()

    return settle


def attend(zs, peers, side, r, meanwhile):
    q_ref, buf, cbuf = r.q, r.keys, r.prefix
    best, total, acc = r.best, r.total, r.acc
    tok, width = buf.shape[1:]
    slots = cbuf.shape[1]
    rows = q_ref.shape[0]
    heads = rows // tok
    stride = 2
    up, down = zs // 2, zs // 2 - 1
    limits = (up, down)
    z, c, _, _, twin = place(zs)
    s = 2 * z + c
    e = lax.axis_index("exp")
    ey, ex = e // side, lax.rem(e, side)
    q = jnp.where(c == 0, ex, ey)
    size = tok // side

    def line(j):
        p = lax.rem(q + j, side)
        return jnp.where(c == 0, ey * side + p, p * side + ex)

    def lanes(x, fold):
        parts = [x[:, i * 128 : (i + 1) * 128] for i in range(x.shape[1] // 128)]
        return functools.reduce(fold, parts)

    def wide(x, like):
        return jnp.concatenate([x] * (like // 128), axis=1)

    def absorb(blocks, first=False):
        scores = []
        for keys, visible in blocks:
            raw = rdot_t(q_ref[...], keys)
            scores.append(raw if visible is None else jnp.where(visible, raw, FLOOR))
        top = functools.reduce(jnp.maximum, [lanes(x, jnp.maximum) for x in scores])
        top = jnp.max(top, axis=1, keepdims=True) * SCALE2
        newest = jnp.broadcast_to(top, best.shape)
        if not first:
            before = best[...]
            newest = jnp.maximum(before, newest)
            fade = jnp.exp2(before - newest)
        best[...] = newest
        weights = [jnp.exp2(x * SCALE2 - wide(newest, x.shape[1])) for x in scores]
        added = functools.reduce(jnp.add, [lanes(x, jnp.add) for x in weights])
        total[...] = added if first else total[...] * fade + added
        summed = functools.reduce(
            jnp.add,
            [
                rdot(x.astype(jnp.bfloat16), keys[:, :LAT])
                for x, (keys, _) in zip(weights, blocks)
            ],
        )
        acc[...] = summed if first else acc[...] * wide(fade, LAT) + summed

    def pair(zb):
        return buf[pl.ds(2 * zb, 2)].reshape(2 * tok, width)

    def far(way, k):
        return lax.rem(z + (zs - k if way == 0 else k), zs)

    def index(way, k):
        return k if way == 0 else up + k

    def piece(zb, p):
        return buf.at[2 * zb + c, pl.ds(pl.multiple_of(p * size, size), size)]

    def hop(way, k, step):
        i = index(way, k + step)
        to = lax.rem(z + (step if way == 0 else zs - step), zs) * 2 + c
        slot = piece(far(way, k), q)
        return remote(slot, slot, r.rs.at[i], r.rr.at[i], to, e)

    def cache_hop(way, k, step):
        i = index(way, k + step)
        to = lax.rem(z + (step if way == 0 else zs - step), zs) * 2 + c
        slot = cbuf.at[2 * far(way, k) + c]
        return remote(slot, slot, r.cs.at[i], r.cr.at[i], to, e)

    def came(way, k):
        i = index(way, k)
        slot = piece(far(way, k), q)
        return remote(slot, slot, r.rs.at[i], r.rr.at[i], twin, e)

    def cache_came(way, k):
        i = index(way, k)
        slot = cbuf.at[2 * far(way, k) + c]
        return remote(slot, slot, r.cs.at[i], r.cr.at[i], twin, e)

    def spread(i, zb, j):
        slot = piece(zb, q)
        return remote(slot, slot, r.ls.at[i, j], r.lr.at[i, j], s, line(j))

    def spread_in(i, zb, j):
        slot = piece(zb, lax.rem(q + side - j, side))
        return remote(slot, slot, r.ls.at[i, j], r.lr.at[i, j], s, line(j))

    def cache_spread(i, zb, j):
        slot = cbuf.at[2 * zb + c]
        return remote(slot, slot, r.ms.at[i, j], r.mr.at[i], s, line(j))

    def share(i, zb, core):
        slot = buf.at[2 * zb + core]
        return remote(slot, slot, r.ts.at[i], r.tr.at[i], twin, e)

    def cache_share(i, zb, core):
        slot = cbuf.at[2 * zb + core]
        return remote(slot, slot, r.ns.at[i], r.nr.at[i], twin, e)

    def carries(zb):
        return lax.rem(zb, side) == q

    for k in range(1, stride + 1):
        for way in range(2):
            if k <= limits[way]:
                hop(way, 0, k).start()

                @pl.when(carries(z))
                def _():
                    cache_hop(way, 0, k).start()

    share(0, z, c).start()
    cache_share(0, z, c).start()
    meanwhile()

    def step(k, carry):
        for way in range(2):
            zb, i = far(way, k), index(way, k)

            @pl.when(k <= limits[way])
            def _():
                came(way, k).wait_recv()

                @pl.when(k + stride <= limits[way])
                def _():
                    hop(way, k, stride).start()

                @pl.when(zb < z)
                def _():
                    for j in range(1, side):
                        spread(i, zb, j).start()

                @pl.when(carries(zb))
                def _():
                    cache_came(way, k).wait_recv()

                    @pl.when(k + stride <= limits[way])
                    def _():
                        cache_hop(way, k, stride).start()

                    for j in range(1, side):
                        cache_spread(i, zb, j).start()

        for way in range(2):
            zl, il = far(way, k - 1), index(way, k - 1)

            @pl.when((k > 1) & (k - 1 <= limits[way]))
            def _():
                @pl.when(zl < z)
                def _():
                    for j in range(1, side):
                        spread_in(il, zl, j).wait_recv()
                    share(il, zl, c).start()

                @pl.when(jnp.logical_not(carries(zl)))
                def _():
                    cache_spread(il, zl, 1).wait_recv()

                cache_share(il, zl, c).start()

        @pl.when(k == 2)
        def _():
            share(0, z, 1 - c).wait_recv()
            cache_share(0, z, 1 - c).wait_recv()
            row = lax.broadcasted_iota(jnp.int32, (rows, 2 * tok), 0)
            key = lax.broadcasted_iota(jnp.int32, (rows, 2 * tok), 1)
            absorb([(pair(z), key <= lax.rem(row, tok) + c * tok)], True)

        j = k - 2
        lower, upper = far(0, j), far(1, j)
        has_lower = (j >= 1) & (lower < z)
        has_upper = (j >= 1) & (j <= down) & (upper < z)

        @pl.when(j >= 1)
        def _():
            cache_share(j, lower, 1 - c).wait_recv()

        @pl.when((j >= 1) & (j <= down))
        def _():
            cache_share(up + j, upper, 1 - c).wait_recv()

        @pl.when(has_lower)
        def _():
            share(j, lower, 1 - c).wait_recv()

        @pl.when(has_upper)
        def _():
            share(up + j, upper, 1 - c).wait_recv()

        @pl.when(has_lower & has_upper)
        def _():
            absorb([(pair(lower), None), (pair(upper), None)])

        @pl.when(has_lower != has_upper)
        def _():
            absorb([(pair(jnp.where(has_lower, lower, upper)), None)])

        return carry

    lax.fori_loop(1, up + 3, step, 0)

    live = r.live[0]
    group = max(1, min(256, slots * 2 * zs) // slots)
    prefix = []
    for i in range(2 * zs // group):
        keys = cbuf[i * group : (i + 1) * group].reshape(group * slots, width)
        key = lax.broadcasted_iota(jnp.int32, (rows, group * slots), 1) + i * (group * slots)
        prefix.append((keys, key < live))
    absorb(prefix)

    r.vup_copy().wait()
    for h in range(heads):
        part = pl.ds(h * tok, tok)
        weight = jnp.sum(total[part, :], axis=1, keepdims=True)
        context = (acc[part, :] / weight).astype(jnp.bfloat16)
        vh = r.vup.shape[2]
        r.heads[s, :, h * vh : (h + 1) * vh] = rdot(context, r.vup[h]).astype(jnp.bfloat16)

    def settle():
        def drain(k, carry):
            for way in range(2):
                zb, i = far(way, k), index(way, k)

                @pl.when(k <= limits[way])
                def _():
                    came(way, k).wait_send()

                    @pl.when(zb < z)
                    def _():
                        for j in range(1, side):
                            spread(i, zb, j).wait_send()
                        share(i, zb, c).wait_send()

                    origin = jnp.maximum(k - stride, 0)
                    source = lax.rem(z + (zs - origin if way == 0 else origin), zs)

                    @pl.when(carries(source))
                    def _():
                        cache_came(way, k).wait_send()

                    @pl.when(carries(zb))
                    def _():
                        for j in range(1, side):
                            cache_spread(i, zb, j).wait_send()

                    cache_share(i, zb, c).wait_send()

            return carry

        lax.fori_loop(1, up + 1, drain, 0)
        share(0, z, c).wait_send()
        cache_share(0, z, c).wait_send()

    return settle


def project(zs, peers, side, r, meanwhile):
    buf, terms = r.heads, r.terms
    _, tok, inner = buf.shape
    width = r.proj.shape[0]
    z, c, _, _, _ = place(zs)
    s = 2 * z + c
    e = lax.axis_index("exp")
    ey, ex = e // side, lax.rem(e, side)

    def along_x(zb):
        to_y, to_x = zb // side, lax.rem(zb, side)
        return remote(
            terms.at[zb],
            r.row_in.at[to_y, ex],
            r.x_send.at[zb],
            r.x_recv.at[to_y, ex],
            s,
            ey * side + to_x,
        )

    def along_y(to_y):
        return remote(
            r.sums.at[to_y],
            r.col_in.at[ey],
            r.y_send.at[to_y],
            r.y_recv.at[ey],
            s,
            to_y * side + ex,
        )

    def visit(zb):
        rows = buf[pl.ds(2 * zb, 2)].reshape(2 * tok, inner)
        terms[zb] = rdot_t(rows, r.proj[...]).astype(jnp.bfloat16)

        @pl.when(lax.rem(zb, side) != ex)
        def _():
            along_x(zb).start()

    def after(zb):
        @pl.when(lax.rem(zb, side) == ex)
        def _():
            to_y = zb // side
            part = terms[zb].astype(jnp.float32)
            for j in range(1, side):
                g = lax.rem(ex + j, side)
                slot = r.row_in.at[to_y, g]
                remote(
                    slot, slot, r.x_send.at[zb], r.x_recv.at[to_y, g], s, ey * side + g
                ).wait_recv()
                part = part + r.row_in[to_y, g].astype(jnp.float32)

            @pl.when(to_y == ey)
            def _():
                r.hid[:, 0:width] += part

            @pl.when(to_y != ey)
            def _():
                r.sums[to_y] = part.astype(jnp.bfloat16)
                along_y(to_y).start()

    def first():
        r.proj_copy().wait()
        r.hid[...] = jnp.zeros_like(r.hid)
        r.hid[:, 0:width] = r.residual[...].astype(jnp.float32).T
        meanwhile()

    sems = (r.hs, r.hr, r.hts, r.htr)
    settle_ring = ring_gather(
        zs, buf, sems, lambda: visit(z), visit, parts=2, after=after, delay=2, meanwhile=first
    )

    for j in range(1, side):
        g = lax.rem(ey + j, side)
        slot = r.col_in.at[g]
        remote(slot, slot, r.y_send.at[g], r.y_recv.at[g], s, g * side + ex).wait_recv()
        r.hid[:, 0:width] += r.col_in[g].astype(jnp.float32)

    def settle():
        settle_ring()

        def drain(zb, carry):
            @pl.when(lax.rem(zb, side) != ex)
            def _():
                along_x(zb).wait_send()

            return carry

        lax.fori_loop(0, zs, drain, 0)
        for j in range(1, side):
            along_y(lax.rem(ey + j, side)).wait_send()

    return settle


def swap_exp(peers, send, recv, s_sem, r_sem, meanwhile):
    s = lax.axis_index("seq")
    e = lax.axis_index("exp")

    def copy(j, to, slot):
        return remote(send.at[to], recv.at[slot], s_sem.at[j], r_sem.at[j], s, to)

    def start(j, carry):
        copy(j, lax.rem(e + j, peers), e).start()
        return carry

    lax.fori_loop(1, peers, start, 0)
    recv[e] = send[e]
    meanwhile()

    def finish(j, carry):
        copy(j, lax.rem(e + j, peers), lax.rem(e + peers - j, peers)).wait_recv()
        return carry

    lax.fori_loop(1, peers, finish, 0)

    def settle():
        def drain(j, carry):
            copy(j, lax.rem(e + j, peers), e).wait_send()
            return carry

        lax.fori_loop(1, peers, drain, 0)

    return settle


def tables(peers, r):
    e = lax.axis_index("exp")
    block = r.pick.shape[1]
    cap = r.pack.shape[0]
    span = pl.ds(pl.multiple_of(e * block, block), block)
    named, weights = r.routes[:, span], r.weights[:, span].astype(jnp.float32)
    hits, scaled = [], []
    for x in range(peers):
        hit = named == x
        hits.append(jnp.max(jnp.where(hit, 1.0, 0.0), axis=0, keepdims=True))
        scaled.append(jnp.sum(jnp.where(hit, weights, 0.0), axis=0, keepdims=True))
    chosen = jnp.concatenate(hits, axis=0)
    before = lax.broadcasted_iota(jnp.int32, (block, block), 0)
    order = lax.broadcasted_iota(jnp.int32, (block, block), 1)
    earlier = jnp.where(before < order, 1.0, 0.0).astype(jnp.bfloat16)
    rank = rdot(chosen.astype(jnp.bfloat16), earlier)
    slot = lax.broadcasted_iota(jnp.int32, (SRC_CAP, block), 0).astype(jnp.float32)
    for x in range(peers):
        part = pl.ds(x * SRC_CAP, SRC_CAP)
        here = jnp.where((rank[x : x + 1] == slot) & (hits[x] > 0.0), 1.0, 0.0)
        r.pick[part, :] = here.astype(jnp.bfloat16)
        r.mix[part, :] = (here * scaled[x]).astype(jnp.bfloat16)
    mine = jnp.sum(jnp.where(r.routes[...] == e, 1.0, 0.0), axis=0, keepdims=True)
    mine = [mine[:, x * block : (x + 1) * block] for x in range(peers)]
    count = jnp.sum(jnp.concatenate(mine, axis=0), axis=1, keepdims=True)
    spots = peers * SRC_CAP
    lane = lax.broadcasted_iota(jnp.int32, (peers, spots), 1) // SRC_CAP
    source = lax.broadcasted_iota(jnp.int32, (peers, spots), 0)
    own = jnp.sum(jnp.where(lane == source, count, 0.0), axis=0, keepdims=True)
    start = jnp.sum(jnp.where(lane > source, count, 0.0), axis=0, keepdims=True)
    turn = lax.rem(lax.broadcasted_iota(jnp.int32, (1, spots), 1), SRC_CAP).astype(jnp.float32)
    at = jnp.where(turn < own, start + turn, -1.0)
    row = lax.broadcasted_iota(jnp.int32, (cap, spots), 0).astype(jnp.float32)
    r.pack[...] = jnp.where(row == at, 1.0, 0.0).astype(jnp.bfloat16)


def split_rows(v):
    row = lax.broadcasted_iota(jnp.int32, v.shape, 0)
    high = v.astype(jnp.bfloat16).astype(jnp.float32)
    rest = v - high
    mid = rest.astype(jnp.bfloat16).astype(jnp.float32)
    low = rest - mid
    parts = jnp.where(row == 0, high, jnp.where(row == 1, mid, jnp.where(row == 2, low, 0.0)))
    return parts.astype(jnp.bfloat16)


def join_rows(block):
    return jnp.sum(block.astype(jnp.float32), axis=0, keepdims=True)


def route(zs, peers, features, r, meanwhile):
    width, tokens = r.residual.shape
    wide = r.hid.shape[1]
    cap = r.pack.shape[0]
    half = cap // 2
    cols = r.ibuf.shape[2]
    up, down = zs // 2, zs // 2 - 1
    z, c, above, below, twin = place(zs)
    e = lax.axis_index("exp")

    hidden = r.hid[...]
    squares = jnp.sum(hidden * hidden, axis=1, keepdims=True)
    high = squares.astype(jnp.bfloat16).astype(jnp.float32)
    rest = squares - high
    mid = rest.astype(jnp.bfloat16).astype(jnp.float32)
    low = rest - mid
    lane = lax.broadcasted_iota(jnp.int32, (tokens, wide), 1)
    ext = jnp.where(
        lane < width,
        hidden * r.gain[...],
        jnp.where(
            lane == width,
            high,
            jnp.where(lane == width + 1, mid, jnp.where(lane == width + 2, low, 0.0)),
        ),
    ).astype(jnp.bfloat16)
    r.d_send[...] = rdot(r.pick[...], ext).astype(jnp.bfloat16).reshape(r.d_send.shape)
    settle_rows = swap_exp(peers, r.d_send, r.d_recv, r.ds_sem, r.dr_sem, meanwhile)

    arrived = r.d_recv[...].reshape(peers * SRC_CAP, wide)
    packed = rdot(r.pack[...], arrived).astype(jnp.bfloat16)
    r.xs[...] = packed
    mark = lax.broadcasted_iota(jnp.int32, (16, wide), 1)
    ones = jnp.where((mark >= width) & (mark < width + 3), 1.0, 0.0).astype(jnp.bfloat16)
    r.sqv[...] = jnp.zeros_like(r.sqv)
    r.sqv[:, 0:cap] = rdot_t(ones, packed)
    own_sq = r.sqv[...]
    tail = split_rows(own_sq)
    r.xo[0:half, :] = r.xs[pl.ds(pl.multiple_of(c * half, 16), half), 0:width]
    r.xo[half:cap, :] = r.xs[pl.ds(pl.multiple_of((1 - c) * half, 16), half), 0:width]

    def to_twin(d):
        return pltpu.make_async_remote_copy(
            src_ref=r.other.at[d],
            dst_ref=r.theirs.at[d],
            send_sem=r.ps_sem.at[d],
            recv_sem=r.pr_sem.at[d],
            device_id={"seq": twin, "exp": e},
            device_id_type=MESH,
        )

    def partial(d):
        r.load(d, 0).wait()
        r.load(d, 1).wait()
        both = rdot(r.xo[...], r.wgu[d])
        r.other[d, 0:half, :] = both[half:].astype(jnp.bfloat16)
        r.other[d, half : half + 16, :] = tail
        to_twin(d).start()
        r.mine[d] = both[:half]

    def up_copy(t):
        return pltpu.make_async_remote_copy(
            src_ref=r.up_out.at[t],
            dst_ref=r.up_in.at[t],
            send_sem=r.us_sem.at[t],
            recv_sem=r.ur_sem.at[t],
            device_id={"seq": above, "exp": e},
            device_id_type=MESH,
        )

    def dn_copy(t):
        return pltpu.make_async_remote_copy(
            src_ref=r.dn_out.at[t],
            dst_ref=r.dn_in.at[t],
            send_sem=r.ls_sem.at[t],
            recv_sem=r.lr_sem.at[t],
            device_id={"seq": below, "exp": e},
            device_id_type=MESH,
        )

    def pair_sum(d):
        to_twin(d).wait_recv()
        body = r.mine[d] + r.theirs[d, 0:half, :].astype(jnp.float32)
        sq = own_sq + join_rows(r.theirs[d, half : half + 16, :])
        return body, sq

    def relay(d, out, into, copy, t, first):
        body, sq = pair_sum(d)
        if not first:
            copy(t - 1).wait_recv()
            body = body + into[t - 1, 0:half, :].astype(jnp.float32)
            sq = sq + join_rows(into[t - 1, half : half + 16, :])
        out[t, 0:half, :] = body.astype(jnp.bfloat16)
        out[t, half : half + 16, :] = split_rows(sq)
        copy(t).start()

    def up_dest(t):
        return lax.rem(z + up - t, zs)

    def dn_dest(t):
        return lax.rem(z + zs - down + t, zs)

    partial(up_dest(0))
    partial(dn_dest(0))
    partial(up_dest(1))
    partial(dn_dest(1))
    relay(up_dest(0), r.up_out, r.up_in, up_copy, 0, True)
    relay(dn_dest(0), r.dn_out, r.dn_in, dn_copy, 0, True)

    def ring(t, carry):
        @pl.when(t < up - 1)
        def _():
            partial(up_dest(t + 1))
            partial(dn_dest(t + 1))

        relay(up_dest(t), r.up_out, r.up_in, up_copy, t, False)

        @pl.when(t < down)
        def _():
            relay(dn_dest(t), r.dn_out, r.dn_in, dn_copy, t, False)

        return carry

    lax.fori_loop(1, up, ring, 0)

    body, sq = pair_sum(z)
    up_copy(up - 1).wait_recv()
    dn_copy(down - 1).wait_recv()
    body = (
        body
        + r.up_in[up - 1, 0:half, :].astype(jnp.float32)
        + r.dn_in[down - 1, 0:half, :].astype(jnp.float32)
    )
    sq = (
        sq
        + join_rows(r.up_in[up - 1, half : half + 16, :])
        + join_rows(r.dn_in[down - 1, half : half + 16, :])
    )
    factor = lax.rsqrt(sq[0:1, :] / features + EPS)
    row = lax.broadcasted_iota(jnp.int32, (half, wide), 0) + c * half
    lane = lax.broadcasted_iota(jnp.int32, (half, wide), 1)
    factor = jnp.sum(jnp.where(row == lane, factor, 0.0), axis=1, keepdims=True)
    gate = body[:, 0:cols] * factor
    lift = body[:, cols : 2 * cols] * factor
    r.ibuf[2 * z + c] = (gate / (1.0 + jnp.exp(-gate)) * lift).astype(jnp.bfloat16)

    r.produced[...] = jnp.zeros_like(r.produced)

    def visit(zb):
        block = r.ibuf[pl.ds(2 * zb, 2)].reshape(cap, cols)
        span = pl.ds(pl.multiple_of(zb * cols, cols), cols)
        r.produced[...] += rdot_t(block, r.wd[:, span])

    def settle_sums():
        settle_rows()

        def drain(d, carry):
            to_twin(d).wait_send()
            return carry

        lax.fori_loop(0, zs, drain, 0)

        def drain_ring(t, carry):
            up_copy(t).wait_send()

            @pl.when(t < down)
            def _():
                dn_copy(t).wait_send()

            return carry

        lax.fori_loop(0, up, drain_ring, 0)
        r.wd_copy().wait()

    sems = (r.is_, r.ir, r.its, r.itr)
    settle_ring = ring_gather(
        zs, r.ibuf, sems, lambda: visit(z), visit, stride=2, meanwhile=settle_sums
    )

    produced = r.produced[...].astype(jnp.bfloat16)
    r.c_send[...] = rdot_tn(r.pack[...], produced).astype(jnp.bfloat16).reshape(r.c_send.shape)
    settle_back = swap_exp(peers, r.c_send, r.c_recv, r.cs_sem, r.cr_sem, settle_ring)
    back = r.c_recv[...].reshape(peers * SRC_CAP, width)
    r.out[...] = (r.hid[:, 0:width] + rdot_tn(r.mix[...], back)).astype(jnp.bfloat16)
    settle_back()


def layer_kernel(zs, peers, side, features, names, *refs):
    r = types.SimpleNamespace(**dict(zip(names, refs)))
    z, c, _, _, _ = place(zs)
    s = 2 * z + c
    cols = r.ibuf.shape[2]
    up, down = zs // 2, zs // 2 - 1

    def load(d, which):
        span = pl.ds(pl.multiple_of(d * cols, cols), cols)
        return pltpu.make_async_copy(
            (r.wg_hbm, r.wu_hbm)[which].at[:, span],
            r.wgu.at[d, :, pl.ds(which * cols, cols)],
            r.w_sem.at[d, which],
        )

    def load_all(d, carry):
        load(d, 0).start()
        load(d, 1).start()
        return carry

    r.load = load
    r.vup_copy = lambda: pltpu.make_async_copy(r.vup_hbm, r.vup, r.b_sem.at[0])
    r.proj_copy = lambda: pltpu.make_async_copy(r.proj_hbm, r.proj, r.b_sem.at[1])
    r.wd_copy = lambda: pltpu.make_async_copy(r.wd_hbm, r.wd, r.b_sem.at[2])
    greeted = greet(zs, 2, peers)
    r.keys[s] = r.latents[...]
    r.prefix[s] = r.cache[...]
    r.vup_copy().start()
    r.proj_copy().start()
    r.wd_copy().start()
    lax.fori_loop(0, zs, load_all, 0)
    greeted()
    settle = attend(zs, peers, side, r, lambda: tables(peers, r))
    settle = project(zs, peers, side, r, settle)
    route(zs, peers, features, r, settle)


def local(
    zs,
    peers,
    queries,
    latents,
    cache,
    prefix_len,
    value_up,
    out_proj,
    residual,
    norm_gain,
    w_gate,
    w_up,
    w_down,
    routes,
    route_weights,
):
    bf16, f32 = jnp.bfloat16, jnp.float32
    dma = pltpu.SemaphoreType.DMA
    tok, heads, qwidth = queries.shape
    slots = cache.shape[0]
    block, width = residual.shape
    inner = out_proj.shape[0]
    cap = SRC_CAP * min(peers, 6)
    half = cap // 2
    wide = -(-(width + 3) // 128) * 128
    cols = w_gate.shape[2] // zs
    up, down = zs // 2, zs // 2 - 1
    features = width * 2 * zs
    rows = tok * heads
    side = math.isqrt(peers)

    q = jnp.swapaxes(queries, 0, 1).reshape(rows, qwidth)
    operands = dict(
        q=(q, VMEM),
        latents=(latents, VMEM),
        cache=(cache, VMEM),
        live=(prefix_len, pltpu.SMEM),
        residual=(residual.T, VMEM),
        gain=(jnp.pad(norm_gain, (0, wide - width)).reshape(1, wide), VMEM),
        routes=(routes.T, VMEM),
        weights=(route_weights.T, VMEM),
        vup_hbm=(value_up, pl.ANY),
        proj_hbm=(out_proj.T, pl.ANY),
        wg_hbm=(w_gate[0], pl.ANY),
        wu_hbm=(w_up[0], pl.ANY),
        wd_hbm=(w_down[0].T, pl.ANY),
    )
    scratch = dict(
        keys=VMEM((2 * zs, tok, qwidth), bf16),
        prefix=VMEM((2 * zs, slots, qwidth), bf16),
        best=VMEM((rows, 128), f32),
        total=VMEM((rows, 128), f32),
        acc=VMEM((rows, LAT), f32),
        vup=VMEM(value_up.shape, bf16),
        rs=dma((zs,)),
        rr=dma((zs,)),
        cs=dma((zs,)),
        cr=dma((zs,)),
        ls=dma((zs, side)),
        lr=dma((zs, side)),
        ms=dma((zs, side)),
        mr=dma((zs,)),
        ts=dma((zs,)),
        tr=dma((zs,)),
        ns=dma((zs,)),
        nr=dma((zs,)),
        heads=VMEM((2 * zs, tok, inner), bf16),
        proj=VMEM((width, inner), bf16),
        terms=VMEM((peers, block, width), bf16),
        row_in=VMEM((side, side, block, width), bf16),
        sums=VMEM((side, block, width), bf16),
        col_in=VMEM((side, block, width), bf16),
        hid=VMEM((block, wide), f32),
        x_send=dma((peers,)),
        x_recv=dma((side, side)),
        y_send=dma((side,)),
        y_recv=dma((side,)),
        **dict(zip(("hs", "hr", "hts", "htr"), ring_sems(zs, 2))),
        pick=VMEM((peers * SRC_CAP, block), bf16),
        mix=VMEM((peers * SRC_CAP, block), bf16),
        pack=VMEM((cap, peers * SRC_CAP), bf16),
        wgu=VMEM((zs, width, 2 * cols), bf16),
        wd=VMEM((width, w_down.shape[1]), bf16),
        d_send=VMEM((peers, SRC_CAP, wide), bf16),
        d_recv=VMEM((peers, SRC_CAP, wide), bf16),
        xs=VMEM((cap, wide), bf16),
        xo=VMEM((cap, width), bf16),
        sqv=VMEM((16, 2 * cols), f32),
        mine=VMEM((zs, half, 2 * cols), f32),
        other=VMEM((zs, half + 16, 2 * cols), bf16),
        theirs=VMEM((zs, half + 16, 2 * cols), bf16),
        up_out=VMEM((up, half + 16, 2 * cols), bf16),
        up_in=VMEM((up, half + 16, 2 * cols), bf16),
        dn_out=VMEM((down, half + 16, 2 * cols), bf16),
        dn_in=VMEM((down, half + 16, 2 * cols), bf16),
        ibuf=VMEM((2 * zs, half, cols), bf16),
        produced=VMEM((cap, width), f32),
        c_send=VMEM((peers, SRC_CAP, width), bf16),
        c_recv=VMEM((peers, SRC_CAP, width), bf16),
        w_sem=dma((zs, 2)),
        b_sem=dma((3,)),
        ds_sem=dma((peers,)),
        dr_sem=dma((peers,)),
        ps_sem=dma((zs,)),
        pr_sem=dma((zs,)),
        us_sem=dma((up,)),
        ur_sem=dma((up,)),
        ls_sem=dma((down,)),
        lr_sem=dma((down,)),
        cs_sem=dma((peers,)),
        cr_sem=dma((peers,)),
        **dict(zip(("is_", "ir", "its", "itr"), ring_sems(zs, 1))),
    )
    names = [*operands, "out", *scratch]
    return pl.pallas_call(
        functools.partial(layer_kernel, zs, peers, side, features, names),
        out_shape=jax.ShapeDtypeStruct((block, width), bf16),
        in_specs=[pl.BlockSpec(memory_space=space) for _, space in operands.values()],
        out_specs=pl.BlockSpec(memory_space=VMEM),
        scratch_shapes=list(scratch.values()),
        compiler_params=pltpu.CompilerParams(
            collective_id=1, has_side_effects=True, vmem_limit_bytes=VMEM_BYTES
        ),
    )(*[value for value, _ in operands.values()])


def solution(mesh):
    in_specs = (
        P("seq", "exp", None),
        P("seq", None),
        P("seq", None),
        P(),
        P("exp", None, None),
        P("exp", "seq"),
        P("exp", "seq"),
        P("seq"),
        P("exp", "seq", None),
        P("exp", "seq", None),
        P("exp", None, "seq"),
        P(),
        P(),
    )
    zs, peers = mesh.shape["seq"] // 2, mesh.shape["exp"]
    return jax.shard_map(
        functools.partial(local, zs, peers),
        mesh=mesh,
        in_specs=in_specs,
        out_specs=P("exp", "seq"),
        check_vma=False,
    )
```

```python
import functools
import math
import types

import jax
import jax.numpy as jnp
from jax import lax
from jax.experimental import pallas as pl
from jax.experimental.pallas import tpu as pltpu
from jax.sharding import PartitionSpec as P

LAT = 512
ROPE = 64
QK_NOPE = 128
SRC_CAP = 32

EPS = 1e-06
FLOOR = -1e30
SCALE2 = (QK_NOPE + ROPE) ** (-0.5) * math.log2(math.e)
MESH = pl.DeviceIdType.MESH
VMEM = pltpu.VMEM
VMEM_BYTES = 60 * 1024 * 1024


def rdot(a, b):
    return jnp.dot(a, b, preferred_element_type=jnp.float32)


def rdot_t(a, b):
    return lax.dot_general(
        a, b, (((1,), (1,)), ((), ())), preferred_element_type=jnp.float32
    )


def rdot_tn(a, b):
    return lax.dot_general(
        a, b, (((0,), (0,)), ((), ())), preferred_element_type=jnp.float32
    )


def turn(x):
    return x.astype(jnp.float32).T.astype(jnp.bfloat16)


def place(zs):
    s = lax.axis_index("seq")
    z, c = s // 2, lax.rem(s, 2)
    above = lax.rem(z + 1, zs) * 2 + c
    below = lax.rem(z + zs - 1, zs) * 2 + c
    twin = 2 * z + 1 - c
    return z, c, above, below, twin


def greet(zs, reach, peers):
    z, c, _, _, twin = place(zs)
    s = 2 * z + c
    e = lax.axis_index("exp")
    barrier = pltpu.get_barrier_semaphore()

    def hello(seq, exp):
        pl.semaphore_signal(
            barrier, inc=1, device_id={"seq": seq, "exp": exp}, device_id_type=MESH
        )

    def along(j, carry):
        hello(s, lax.rem(e + j, peers))
        return carry

    lax.fori_loop(1, peers, along, 0)
    for k in range(1, reach + 1):
        hello(lax.rem(z + k, zs) * 2 + c, e)
        hello(lax.rem(z + zs - k, zs) * 2 + c, e)
    hello(twin, e)
    return lambda: pl.semaphore_wait(barrier, 1 + 2 * reach + peers - 1)


def remote(src, dst, ssem, rsem, seq, exp):
    return pltpu.make_async_remote_copy(
        src_ref=src,
        dst_ref=dst,
        send_sem=ssem,
        recv_sem=rsem,
        device_id={"seq": seq, "exp": exp},
        device_id_type=MESH,
    )


def ring_sems(zs, parts):
    dma = pltpu.SemaphoreType.DMA
    return [dma((zs, parts)), dma((zs, parts)), dma((zs,)), dma((zs,))]


def ring_gather(
    zs, buf, sems, own, visit, stride=1, parts=1, after=None, delay=0, meanwhile=None
):
    rs, rr, ts, tr = sems
    up, down = zs // 2, zs // 2 - 1
    z, c, _, _, twin = place(zs)
    e = lax.axis_index("exp")
    size = buf.shape[1] // parts

    def far(side, k):
        return lax.rem(z + (zs - k if side == 0 else k), zs)

    def index(side, k):
        return k if side == 0 else up + k

    def hop(side, k, p, step):
        slot = buf.at[2 * far(side, k) + c, pl.ds(p * size, size)]
        i = index(side, k + step)
        to = lax.rem(z + (step if side == 0 else zs - step), zs) * 2 + c
        return remote(slot, slot, rs.at[i, p], rr.at[i, p], to, e)

    def came(side, k, p):
        slot = buf.at[2 * far(side, k) + c, pl.ds(p * size, size)]
        i = index(side, k)
        return remote(slot, slot, rs.at[i, p], rr.at[i, p], twin, e)

    def share(i, zb, core):
        slot = buf.at[2 * zb + core]
        return remote(slot, slot, ts.at[i], tr.at[i], twin, e)

    limits = (up, down)
    for p in range(parts):
        for k in range(1, stride + 1):
            for side in range(2):
                if k <= limits[side]:
                    hop(side, 0, p, k).start()
    share(0, z, c).start()
    if meanwhile is not None:
        meanwhile()

    def step(k, carry):
        for p in range(parts):
            for side in range(2):

                @pl.when(k <= limits[side])
                def _():
                    came(side, k, p).wait_recv()

                    @pl.when(k + stride <= limits[side])
                    def _():
                        hop(side, k, p, stride).start()

                    if p == parts - 1:
                        share(index(side, k), far(side, k), c).start()

        @pl.when(k == 1)
        def _():
            share(0, z, 1 - c).wait_recv()
            own()

        def both(j, act):
            def one(side, inner):
                @pl.when((side == 0) | (j <= down))
                def _():
                    zb = lax.rem(z + jnp.where(side == 0, zs - j, j), zs)
                    act(zb, jnp.where(side == 0, j, up + j))

                return inner

            lax.fori_loop(0, 2, one, 0)

        def arrive(zb, i):
            share(i, zb, 1 - c).wait_recv()
            visit(zb)

        @pl.when((k > 1) & (k <= up + 1))
        def _():
            both(k - 1, arrive)

        if after is not None:

            @pl.when(k == delay + 1)
            def _():
                after(z)

            @pl.when(k > delay + 1)
            def _():
                both(k - 1 - delay, lambda zb, i: after(zb))

        return carry

    lax.fori_loop(1, up + 2 + delay, step, 0)

    def settle():
        def drain(k, carry):
            for side in range(2):

                @pl.when(k <= limits[side])
                def _():
                    for p in range(parts):
                        came(side, k, p).wait_send()
                    share(index(side, k), far(side, k), c).wait_send()

            return carry

        lax.fori_loop(1, up + 1, drain, 0)
        share(0, z, c).wait_send()

    return settle


def attend(zs, peers, side, r, meanwhile):
    q_ref, buf, cbuf = r.q, r.keys, r.prefix
    best, total, acc = r.best, r.total, r.acc
    tok, width = buf.shape[1:]
    slots = cbuf.shape[2]
    rows = q_ref.shape[0]
    heads = rows // tok
    hand, use = 2, 4
    stride = 2
    up, down = zs // 2, zs // 2 - 1
    limits = (up, down)
    z, c, _, _, twin = place(zs)
    s = 2 * z + c
    e = lax.axis_index("exp")
    ey, ex = e // side, lax.rem(e, side)
    q = jnp.where(c == 0, ex, ey)
    size = tok // side

    def line(j):
        p = lax.rem(q + j, side)
        return jnp.where(c == 0, ey * side + p, p * side + ex)

    def lanes(x, fold):
        parts = [x[:, i * 128 : (i + 1) * 128] for i in range(x.shape[1] // 128)]
        return functools.reduce(fold, parts)

    def wide(x, like):
        return jnp.concatenate([x] * (like // 128), axis=1)

    def absorb(blocks, first=False):
        scores = []
        for keys, visible in blocks:
            raw = rdot_t(q_ref[...], keys)
            scores.append(raw if visible is None else jnp.where(visible, raw, FLOOR))
        top = functools.reduce(jnp.maximum, [lanes(x, jnp.maximum) for x in scores])
        top = jnp.max(top, axis=1, keepdims=True) * SCALE2
        newest = jnp.broadcast_to(top, best.shape)
        if not first:
            before = best[...]
            newest = jnp.maximum(before, newest)
            fade = jnp.exp2(before - newest)
        best[...] = newest
        weights = [jnp.exp2(x * SCALE2 - wide(newest, x.shape[1])) for x in scores]
        added = functools.reduce(jnp.add, [lanes(x, jnp.add) for x in weights])
        total[...] = added if first else total[...] * fade + added
        summed = functools.reduce(
            jnp.add,
            [
                rdot(x.astype(jnp.bfloat16), keys[:, :LAT])
                for x, (keys, _) in zip(weights, blocks)
            ],
        )
        acc[...] = summed if first else acc[...] * wide(fade, LAT) + summed

    def pair(zb):
        return buf[pl.ds(2 * zb, 2)].reshape(2 * tok, width)

    def far(way, k):
        return lax.rem(z + (zs - k if way == 0 else k), zs)

    def index(way, k):
        return k if way == 0 else up + k

    def piece(zb, p):
        return buf.at[2 * zb + c, pl.ds(pl.multiple_of(p * size, size), size)]

    def hop(way, k, step):
        i = index(way, k + step)
        to = lax.rem(z + (step if way == 0 else zs - step), zs) * 2 + c
        slot = piece(far(way, k), q)
        return remote(slot, slot, r.rs.at[i], r.rr.at[i], to, e)

    def cache_hop(way, k, step):
        i = index(way, k + step)
        to = lax.rem(z + (step if way == 0 else zs - step), zs) * 2 + c
        slot = cbuf.at[c, far(way, k)]
        return remote(slot, slot, r.cs.at[i], r.cr.at[i], to, e)

    def came(way, k):
        i = index(way, k)
        slot = piece(far(way, k), q)
        return remote(slot, slot, r.rs.at[i], r.rr.at[i], twin, e)

    def cache_came(way, k):
        i = index(way, k)
        slot = cbuf.at[c, far(way, k)]
        return remote(slot, slot, r.cs.at[i], r.cr.at[i], twin, e)

    def spread(i, zb, j):
        slot = piece(zb, q)
        return remote(slot, slot, r.ls.at[i, j], r.lr.at[i, j], s, line(j))

    def spread_in(i, zb, j):
        slot = piece(zb, lax.rem(q + side - j, side))
        return remote(slot, slot, r.ls.at[i, j], r.lr.at[i, j], s, line(j))

    def cache_spread(i, zb, j):
        slot = cbuf.at[c, zb]
        return remote(slot, slot, r.ms.at[i, j], r.mr.at[i], s, line(j))

    def share(i, zb, core):
        slot = buf.at[2 * zb + core]
        return remote(slot, slot, r.ts.at[i], r.tr.at[i], twin, e)

    def cache_share(core):
        slot = cbuf.at[core]
        return remote(slot, slot, r.ns.at[0], r.nr.at[0], twin, e)

    def carries(zb):
        return lax.rem(zb, side) == q

    for k in range(1, stride + 1):
        for way in range(2):
            if k <= limits[way]:
                hop(way, 0, k).start()

                @pl.when(carries(z))
                def _():
                    cache_hop(way, 0, k).start()

    share(0, z, c).start()
    meanwhile()

    def step(k, carry):
        for way in range(2):
            zb, i = far(way, k), index(way, k)

            @pl.when(k <= limits[way])
            def _():
                came(way, k).wait_recv()

                @pl.when(k + stride <= limits[way])
                def _():
                    hop(way, k, stride).start()

                @pl.when(zb < z)
                def _():
                    for j in range(1, side):
                        spread(i, zb, j).start()

                @pl.when(carries(zb))
                def _():
                    cache_came(way, k).wait_recv()

                    @pl.when(k + stride <= limits[way])
                    def _():
                        cache_hop(way, k, stride).start()

                    for j in range(1, side):
                        cache_spread(i, zb, j).start()

        for way in range(2):
            zl, il = far(way, k - hand), index(way, k - hand)

            @pl.when((k > hand) & (k - hand <= limits[way]))
            def _():
                @pl.when(zl < z)
                def _():
                    for j in range(1, side):
                        spread_in(il, zl, j).wait_recv()
                    share(il, zl, c).start()

                @pl.when(jnp.logical_not(carries(zl)))
                def _():
                    cache_spread(il, zl, 1).wait_recv()

        @pl.when(k == up + hand)
        def _():
            cache_share(c).start()

        @pl.when(k == 2)
        def _():
            share(0, z, 1 - c).wait_recv()
            row = lax.broadcasted_iota(jnp.int32, (rows, 2 * tok), 0)
            key = lax.broadcasted_iota(jnp.int32, (rows, 2 * tok), 1)
            absorb([(pair(z), key <= lax.rem(row, tok) + c * tok)], True)

        j = k - use
        lower, upper = far(0, j), far(1, j)
        has_lower = (j >= 1) & (lower < z)
        has_upper = (j >= 1) & (j <= down) & (upper < z)

        @pl.when(has_lower)
        def _():
            share(j, lower, 1 - c).wait_recv()

        @pl.when(has_upper)
        def _():
            share(up + j, upper, 1 - c).wait_recv()

        @pl.when(has_lower & has_upper)
        def _():
            absorb([(pair(lower), None), (pair(upper), None)])

        @pl.when(has_lower != has_upper)
        def _():
            absorb([(pair(jnp.where(has_lower, lower, upper)), None)])

        return carry

    lax.fori_loop(1, up + use + 1, step, 0)

    cache_share(1 - c).wait_recv()
    live = r.live[0]
    prefix = []
    cores = 1 if zs * slots % 128 == 0 else 2
    for core in range(0, 2, cores):
        count = cores * zs * slots
        at = lax.broadcasted_iota(jnp.int32, (rows, count), 1)
        own_core, rest = core + at // (zs * slots), lax.rem(at, zs * slots)
        at = (rest // slots * 2 + own_core) * slots + lax.rem(rest, slots)
        prefix.append((cbuf[core : core + cores].reshape(count, width), at < live))
    absorb(prefix)

    r.vup_copy().wait()
    for h in range(heads):
        part = pl.ds(h * tok, tok)
        weight = jnp.sum(total[part, :], axis=1, keepdims=True)
        context = (acc[part, :] / weight).astype(jnp.bfloat16)
        vh = r.vup.shape[2]
        r.heads[s, :, h * vh : (h + 1) * vh] = rdot(context, r.vup[h]).astype(jnp.bfloat16)

    def settle():
        def drain(k, carry):
            for way in range(2):
                zb, i = far(way, k), index(way, k)

                @pl.when(k <= limits[way])
                def _():
                    came(way, k).wait_send()

                    @pl.when(zb < z)
                    def _():
                        for j in range(1, side):
                            spread(i, zb, j).wait_send()
                        share(i, zb, c).wait_send()

                    origin = jnp.maximum(k - stride, 0)
                    source = lax.rem(z + (zs - origin if way == 0 else origin), zs)

                    @pl.when(carries(source))
                    def _():
                        cache_came(way, k).wait_send()

                    @pl.when(carries(zb))
                    def _():
                        for j in range(1, side):
                            cache_spread(i, zb, j).wait_send()

            return carry

        lax.fori_loop(1, up + 1, drain, 0)
        share(0, z, c).wait_send()
        cache_share(c).wait_send()

    return settle


def project(zs, peers, side, r, meanwhile):
    buf, terms = r.heads, r.terms
    _, tok, inner = buf.shape
    width = r.proj.shape[0]
    z, c, _, _, _ = place(zs)
    s = 2 * z + c
    e = lax.axis_index("exp")
    ey, ex = e // side, lax.rem(e, side)
    one, two = jnp.where(c == 0, ex, ey), jnp.where(c == 0, ey, ex)

    def split(zb):
        to_y, to_x = zb // side, lax.rem(zb, side)
        return jnp.where(c == 0, to_x, to_y), jnp.where(c == 0, to_y, to_x)

    def column(to_one, to_two):
        return jnp.where(c == 0, to_two * side + to_one, to_one * side + to_two)

    def along_one(zb):
        to_one, to_two = split(zb)
        return remote(
            terms.at[zb],
            r.row_in.at[to_two, one],
            r.x_send.at[zb],
            r.x_recv.at[to_two, one],
            s,
            column(to_one, two),
        )

    def along_two(to_two):
        return remote(
            r.sums.at[to_two],
            r.col_in.at[two],
            r.y_send.at[to_two],
            r.y_recv.at[two],
            s,
            column(one, to_two),
        )

    def visit(zb):
        rows = buf[pl.ds(2 * zb, 2)].reshape(2 * tok, inner)
        terms[zb] = rdot_t(rows, r.proj[...]).astype(jnp.bfloat16)

        @pl.when(split(zb)[0] != one)
        def _():
            along_one(zb).start()

    def after(zb):
        to_one, to_two = split(zb)

        @pl.when(to_one == one)
        def _():
            part = terms[zb].astype(jnp.float32)
            for j in range(1, side):
                g = lax.rem(one + j, side)
                slot = r.row_in.at[to_two, g]
                remote(
                    slot, slot, r.x_send.at[zb], r.x_recv.at[to_two, g], s, column(g, two)
                ).wait_recv()
                part = part + r.row_in[to_two, g].astype(jnp.float32)

            @pl.when(to_two == two)
            def _():
                r.hid[:, 0:width] += part

            @pl.when(to_two != two)
            def _():
                r.sums[to_two] = part.astype(jnp.bfloat16)
                along_two(to_two).start()

    def first():
        r.proj_copy().wait()
        r.res_copy().wait()
        r.hid[...] = jnp.zeros_like(r.hid)
        r.hid[:, 0:width] = r.residual[...].astype(jnp.float32).T
        meanwhile()

    sems = (r.hs, r.hr, r.hts, r.htr)
    settle_ring = ring_gather(
        zs, buf, sems, lambda: visit(z), visit, parts=4, after=after, delay=2, meanwhile=first
    )

    for j in range(1, side):
        g = lax.rem(two + j, side)
        slot = r.col_in.at[g]
        remote(slot, slot, r.y_send.at[g], r.y_recv.at[g], s, column(one, g)).wait_recv()
        r.hid[:, 0:width] += r.col_in[g].astype(jnp.float32)

    def settle():
        settle_ring()

        def drain(zb, carry):
            @pl.when(split(zb)[0] != one)
            def _():
                along_one(zb).wait_send()

            return carry

        lax.fori_loop(0, zs, drain, 0)
        for j in range(1, side):
            along_two(lax.rem(two + j, side)).wait_send()

    return settle


def swap_exp(peers, send, recv, s_sem, r_sem, meanwhile):
    s = lax.axis_index("seq")
    e = lax.axis_index("exp")

    def copy(j, to, slot):
        return remote(send.at[to], recv.at[slot], s_sem.at[j], r_sem.at[j], s, to)

    def start(j, carry):
        copy(j, lax.rem(e + j, peers), e).start()
        return carry

    lax.fori_loop(1, peers, start, 0)
    recv[e] = send[e]
    meanwhile()

    def finish(j, carry):
        copy(j, lax.rem(e + j, peers), lax.rem(e + peers - j, peers)).wait_recv()
        return carry

    lax.fori_loop(1, peers, finish, 0)

    def settle():
        def drain(j, carry):
            copy(j, lax.rem(e + j, peers), e).wait_send()
            return carry

        lax.fori_loop(1, peers, drain, 0)

    return settle


def tables(peers, r):
    e = lax.axis_index("exp")
    block = r.pick.shape[1]
    cap = r.pack.shape[0]
    span = pl.ds(pl.multiple_of(e * block, block), block)
    named, weights = r.routes[:, span], r.weights[:, span].astype(jnp.float32)
    hits, scaled = [], []
    for x in range(peers):
        hit = named == x
        hits.append(jnp.max(jnp.where(hit, 1.0, 0.0), axis=0, keepdims=True))
        scaled.append(jnp.sum(jnp.where(hit, weights, 0.0), axis=0, keepdims=True))
    chosen = jnp.concatenate(hits, axis=0)
    before = lax.broadcasted_iota(jnp.int32, (block, block), 0)
    order = lax.broadcasted_iota(jnp.int32, (block, block), 1)
    earlier = jnp.where(before < order, 1.0, 0.0).astype(jnp.bfloat16)
    rank = rdot(chosen.astype(jnp.bfloat16), earlier)
    slot = lax.broadcasted_iota(jnp.int32, (SRC_CAP, block), 0).astype(jnp.float32)
    for x in range(peers):
        part = pl.ds(x * SRC_CAP, SRC_CAP)
        here = jnp.where((rank[x : x + 1] == slot) & (hits[x] > 0.0), 1.0, 0.0)
        r.pick[part, :] = here.astype(jnp.bfloat16)
        r.mix[part, :] = (here * scaled[x]).astype(jnp.bfloat16)
    mine = jnp.sum(jnp.where(r.routes[...] == e, 1.0, 0.0), axis=0, keepdims=True)
    mine = [mine[:, x * block : (x + 1) * block] for x in range(peers)]
    count = jnp.sum(jnp.concatenate(mine, axis=0), axis=1, keepdims=True)
    spots = peers * SRC_CAP
    lane = lax.broadcasted_iota(jnp.int32, (peers, spots), 1) // SRC_CAP
    source = lax.broadcasted_iota(jnp.int32, (peers, spots), 0)
    own = jnp.sum(jnp.where(lane == source, count, 0.0), axis=0, keepdims=True)
    start = jnp.sum(jnp.where(lane > source, count, 0.0), axis=0, keepdims=True)
    turn = lax.rem(lax.broadcasted_iota(jnp.int32, (1, spots), 1), SRC_CAP).astype(jnp.float32)
    at = jnp.where(turn < own, start + turn, -1.0)
    row = lax.broadcasted_iota(jnp.int32, (cap, spots), 0).astype(jnp.float32)
    r.pack[...] = jnp.where(row == at, 1.0, 0.0).astype(jnp.bfloat16)


def split_rows(v):
    row = lax.broadcasted_iota(jnp.int32, v.shape, 0)
    high = v.astype(jnp.bfloat16).astype(jnp.float32)
    rest = v - high
    mid = rest.astype(jnp.bfloat16).astype(jnp.float32)
    low = rest - mid
    parts = jnp.where(row == 0, high, jnp.where(row == 1, mid, jnp.where(row == 2, low, 0.0)))
    return parts.astype(jnp.bfloat16)


def join_rows(block):
    return jnp.sum(block.astype(jnp.float32), axis=0, keepdims=True)


def route(zs, peers, features, r, meanwhile):
    width, tokens = r.residual.shape
    wide = r.hid.shape[1]
    cap = r.pack.shape[0]
    half = cap // 2
    cols = r.ibuf.shape[2]
    up, down = zs // 2, zs // 2 - 1
    z, c, above, below, twin = place(zs)
    e = lax.axis_index("exp")

    gain = jnp.concatenate([r.gain[...], jnp.zeros((1, wide - width), jnp.float32)], axis=1)
    hidden = r.hid[...]
    squares = jnp.sum(hidden * hidden, axis=1, keepdims=True)
    high = squares.astype(jnp.bfloat16).astype(jnp.float32)
    rest = squares - high
    mid = rest.astype(jnp.bfloat16).astype(jnp.float32)
    low = rest - mid
    lane = lax.broadcasted_iota(jnp.int32, (tokens, wide), 1)
    ext = jnp.where(
        lane < width,
        hidden * gain,
        jnp.where(
            lane == width,
            high,
            jnp.where(lane == width + 1, mid, jnp.where(lane == width + 2, low, 0.0)),
        ),
    ).astype(jnp.bfloat16)
    r.d_send[...] = rdot(r.pick[...], ext).astype(jnp.bfloat16).reshape(r.d_send.shape)
    settle_rows = swap_exp(peers, r.d_send, r.d_recv, r.ds_sem, r.dr_sem, meanwhile)

    arrived = r.d_recv[...].reshape(peers * SRC_CAP, wide)
    packed = rdot(r.pack[...], arrived).astype(jnp.bfloat16)
    r.xs[...] = packed
    mark = lax.broadcasted_iota(jnp.int32, (16, wide), 1)
    ones = jnp.where((mark >= width) & (mark < width + 3), 1.0, 0.0).astype(jnp.bfloat16)
    r.sqv[...] = jnp.zeros_like(r.sqv)
    for h in range(2):
        span = pl.ds(pl.multiple_of((c if h == 0 else 1 - c) * half, 16), half)
        r.xo[h * half : (h + 1) * half, :] = r.xs[span, 0:width]
        r.sqv[h, :, 0:half] = rdot_t(ones, r.xs[span, :])
    own_sq = r.sqv[0]
    tail = split_rows(r.sqv[1])

    def to_twin(d):
        return pltpu.make_async_remote_copy(
            src_ref=r.other.at[d],
            dst_ref=r.theirs.at[d],
            send_sem=r.ps_sem.at[d],
            recv_sem=r.pr_sem.at[d],
            device_id={"seq": twin, "exp": e},
            device_id_type=MESH,
        )

    def partial(d):
        r.load(d, 0).wait()
        r.load(d, 1).wait()
        both = rdot(r.xo[...], r.wgu[d])
        for p in range(2):
            part = both[:, p * cols : (p + 1) * cols]
            r.other[d, p, 0:half, :] = part[half:].astype(jnp.bfloat16)
            r.other[d, p, half : half + 16, :] = tail
            r.mine[d, p] = part[:half]
        to_twin(d).start()

    def sent_rows(p):
        return pl.ds(0, half + 16 if p == 0 else half)

    def up_copy(t, p):
        return remote(
            r.up_out.at[t, p, sent_rows(p)],
            r.up_in.at[t, p, sent_rows(p)],
            r.us_sem.at[t, p],
            r.ur_sem.at[t, p],
            above,
            e,
        )

    def dn_copy(t, p):
        return remote(
            r.dn_out.at[t, p, sent_rows(p)],
            r.dn_in.at[t, p, sent_rows(p)],
            r.ls_sem.at[t, p],
            r.lr_sem.at[t, p],
            below,
            e,
        )

    def pair_sum(d, p):
        if p == 0:
            to_twin(d).wait_recv()
        body = r.mine[d, p] + r.theirs[d, p, 0:half, :].astype(jnp.float32)
        sq = own_sq + join_rows(r.theirs[d, 0, half : half + 16, :]) if p == 0 else None
        return body, sq

    def relay(d, out, into, copy, t, p, first):
        body, sq = pair_sum(d, p)
        if not first:
            copy(t - 1, p).wait_recv()
            body = body + into[t - 1, p, 0:half, :].astype(jnp.float32)
            if p == 0:
                sq = sq + join_rows(into[t - 1, p, half : half + 16, :])
        out[t, p, 0:half, :] = body.astype(jnp.bfloat16)
        if p == 0:
            out[t, p, half : half + 16, :] = split_rows(sq)
        copy(t, p).start()

    def up_dest(t):
        return lax.rem(z + up - t, zs)

    def dn_dest(t):
        return lax.rem(z + zs - down + t, zs)

    partial(up_dest(0))
    partial(dn_dest(0))
    partial(up_dest(1))
    partial(dn_dest(1))
    for p in range(2):
        relay(up_dest(0), r.up_out, r.up_in, up_copy, 0, p, True)
        relay(dn_dest(0), r.dn_out, r.dn_in, dn_copy, 0, p, True)

    def ring(t, carry):
        @pl.when(t < up - 1)
        def _():
            partial(up_dest(t + 1))
            partial(dn_dest(t + 1))

        for p in range(2):
            relay(up_dest(t), r.up_out, r.up_in, up_copy, t, p, False)

            @pl.when(t < down)
            def _():
                relay(dn_dest(t), r.dn_out, r.dn_in, dn_copy, t, p, False)

        return carry

    lax.fori_loop(1, up, ring, 0)

    sums = []
    for p in range(2):
        body, added = pair_sum(z, p)
        up_copy(up - 1, p).wait_recv()
        dn_copy(down - 1, p).wait_recv()
        sums.append(
            body
            + r.up_in[up - 1, p, 0:half, :].astype(jnp.float32)
            + r.dn_in[down - 1, p, 0:half, :].astype(jnp.float32)
        )
        if p == 0:
            sq = (
                added
                + join_rows(r.up_in[up - 1, p, half : half + 16, :])
                + join_rows(r.dn_in[down - 1, p, half : half + 16, :])
            )
    factor = lax.rsqrt(sq[0:1, :] / features + EPS)
    row = lax.broadcasted_iota(jnp.int32, (half, cols), 0)
    lane = lax.broadcasted_iota(jnp.int32, (half, cols), 1)
    factor = jnp.sum(jnp.where(row == lane, factor, 0.0), axis=1, keepdims=True)
    gate = sums[0] * factor
    lift = sums[1] * factor
    r.ibuf[2 * z + c] = (gate / (1.0 + jnp.exp(-gate)) * lift).astype(jnp.bfloat16)

    r.produced[...] = jnp.zeros_like(r.produced)

    def visit(zb):
        block = r.ibuf[pl.ds(2 * zb, 2)].reshape(cap, cols)
        span = pl.ds(pl.multiple_of(zb * cols, cols), cols)
        r.produced[...] += rdot_t(block, r.wd[:, span])

    def settle_sums():
        settle_rows()

        def drain(d, carry):
            to_twin(d).wait_send()
            return carry

        lax.fori_loop(0, zs, drain, 0)

        def drain_ring(t, carry):
            for p in range(2):
                up_copy(t, p).wait_send()

                @pl.when(t < down)
                def _():
                    dn_copy(t, p).wait_send()

            return carry

        lax.fori_loop(0, up, drain_ring, 0)
        r.wd_copy().wait()

    sems = (r.is_, r.ir, r.its, r.itr)
    settle_ring = ring_gather(
        zs, r.ibuf, sems, lambda: visit(z), visit, stride=2, meanwhile=settle_sums
    )

    produced = r.produced[...].astype(jnp.bfloat16)
    r.c_send[...] = rdot_tn(r.pack[...], produced).astype(jnp.bfloat16).reshape(r.c_send.shape)
    settle_back = swap_exp(peers, r.c_send, r.c_recv, r.cs_sem, r.cr_sem, settle_ring)
    back = r.c_recv[...].reshape(peers * SRC_CAP, width)
    r.out[...] = (r.hid[:, 0:width] + rdot_tn(r.mix[...], back)).astype(jnp.bfloat16)
    settle_back()


def layer_kernel(zs, peers, side, features, names, *refs):
    r = types.SimpleNamespace(**dict(zip(names, refs)))
    z, c, _, _, _ = place(zs)
    s = 2 * z + c
    cols = r.ibuf.shape[2]
    up, down = zs // 2, zs // 2 - 1

    def load(d, which):
        span = pl.ds(pl.multiple_of(d * cols, cols), cols)
        return pltpu.make_async_copy(
            (r.wg_hbm, r.wu_hbm)[which].at[:, span],
            r.wgu.at[d, :, pl.ds(which * cols, cols)],
            r.w_sem.at[d, which],
        )

    def load_all(d, carry):
        load(d, 0).start()
        load(d, 1).start()
        return carry

    r.load = load

    def whole(src, dst, i):
        return lambda: pltpu.make_async_copy(src, dst, r.b_sem.at[i])

    latents_copy = whole(r.latents_hbm, r.latents, 0)
    cache_copy = whole(r.cache_hbm, r.prefix.at[c, z], 1)
    queries_copy = whole(r.queries_hbm, r.queries, 2)
    routes_copy = whole(r.routes_hbm, r.routes, 3)
    weights_copy = whole(r.weights_hbm, r.weights, 4)
    r.res_copy = whole(r.residual_hbm, r.residual, 5)
    r.vup_copy = whole(r.vup_hbm, r.vup, 6)
    r.proj_copy = whole(r.proj_hbm, r.proj, 7)
    r.wd_copy = whole(r.wd_hbm, r.wd, 8)
    latents_copy().start()
    cache_copy().start()
    greeted = greet(zs, 2, peers)
    for copy in (queries_copy, routes_copy, weights_copy, r.res_copy, r.vup_copy):
        copy().start()
    r.proj_copy().start()
    r.wd_copy().start()
    lax.fori_loop(0, zs, load_all, 0)
    latents_copy().wait()
    r.keys[s] = turn(r.latents[...])
    cache_copy().wait()
    greeted()

    def prepare():
        tok = r.keys.shape[1]
        queries_copy().wait()
        for h in range(r.queries.shape[0]):
            r.q[h * tok : (h + 1) * tok, :] = turn(r.queries[h])
        routes_copy().wait()
        weights_copy().wait()
        tables(peers, r)

    settle = attend(zs, peers, side, r, prepare)
    settle = project(zs, peers, side, r, settle)
    route(zs, peers, features, r, settle)


def local(
    zs,
    peers,
    queries,
    latents,
    cache,
    prefix_len,
    value_up,
    out_proj,
    residual,
    norm_gain,
    w_gate,
    w_up,
    w_down,
    routes,
    route_weights,
):
    bf16, f32 = jnp.bfloat16, jnp.float32
    dma = pltpu.SemaphoreType.DMA
    tok, heads, qwidth = queries.shape
    slots = cache.shape[0]
    block, width = residual.shape
    inner = out_proj.shape[0]
    cap = SRC_CAP * min(peers, 6)
    half = cap // 2
    wide = -(-(width + 3) // 128) * 128
    cols = w_gate.shape[2] // zs
    up, down = zs // 2, zs // 2 - 1
    features = width * 2 * zs
    rows = tok * heads
    side = math.isqrt(peers)

    operands = dict(
        queries_hbm=(jnp.transpose(queries, (1, 2, 0)), pl.ANY),
        latents_hbm=(latents.T, pl.ANY),
        cache_hbm=(cache, pl.ANY),
        live=(prefix_len, pltpu.SMEM),
        residual_hbm=(residual.T, pl.ANY),
        gain=(norm_gain.reshape(1, width), VMEM),
        routes_hbm=(routes.T, pl.ANY),
        weights_hbm=(route_weights.T, pl.ANY),
        vup_hbm=(value_up, pl.ANY),
        proj_hbm=(out_proj.T, pl.ANY),
        wg_hbm=(w_gate[0], pl.ANY),
        wu_hbm=(w_up[0], pl.ANY),
        wd_hbm=(w_down[0].T, pl.ANY),
    )
    scratch = dict(
        queries=VMEM((heads, qwidth, tok), bf16),
        latents=VMEM((qwidth, tok), bf16),
        residual=VMEM((width, block), bf16),
        routes=VMEM(routes.shape[::-1], jnp.int32),
        weights=VMEM(routes.shape[::-1], bf16),
        q=VMEM((rows, qwidth), bf16),
        keys=VMEM((2 * zs, tok, qwidth), bf16),
        prefix=VMEM((2, zs, slots, qwidth), bf16),
        best=VMEM((rows, 128), f32),
        total=VMEM((rows, 128), f32),
        acc=VMEM((rows, LAT), f32),
        vup=VMEM(value_up.shape, bf16),
        rs=dma((zs,)),
        rr=dma((zs,)),
        cs=dma((zs,)),
        cr=dma((zs,)),
        ls=dma((zs, side)),
        lr=dma((zs, side)),
        ms=dma((zs, side)),
        mr=dma((zs,)),
        ts=dma((zs,)),
        tr=dma((zs,)),
        ns=dma((1,)),
        nr=dma((1,)),
        heads=VMEM((2 * zs, tok, inner), bf16),
        proj=VMEM((width, inner), bf16),
        terms=VMEM((peers, block, width), bf16),
        row_in=VMEM((side, side, block, width), bf16),
        sums=VMEM((side, block, width), bf16),
        col_in=VMEM((side, block, width), bf16),
        hid=VMEM((block, wide), f32),
        x_send=dma((peers,)),
        x_recv=dma((side, side)),
        y_send=dma((side,)),
        y_recv=dma((side,)),
        **dict(zip(("hs", "hr", "hts", "htr"), ring_sems(zs, 4))),
        pick=VMEM((peers * SRC_CAP, block), bf16),
        mix=VMEM((peers * SRC_CAP, block), bf16),
        pack=VMEM((cap, peers * SRC_CAP), bf16),
        wgu=VMEM((zs, width, 2 * cols), bf16),
        wd=VMEM((width, w_down.shape[1]), bf16),
        d_send=VMEM((peers, SRC_CAP, wide), bf16),
        d_recv=VMEM((peers, SRC_CAP, wide), bf16),
        xs=VMEM((cap, wide), bf16),
        xo=VMEM((cap, width), bf16),
        sqv=VMEM((2, 16, cols), f32),
        mine=VMEM((zs, 2, half, cols), f32),
        other=VMEM((zs, 2, half + 16, cols), bf16),
        theirs=VMEM((zs, 2, half + 16, cols), bf16),
        up_out=VMEM((up, 2, half + 16, cols), bf16),
        up_in=VMEM((up, 2, half + 16, cols), bf16),
        dn_out=VMEM((down, 2, half + 16, cols), bf16),
        dn_in=VMEM((down, 2, half + 16, cols), bf16),
        ibuf=VMEM((2 * zs, half, cols), bf16),
        produced=VMEM((cap, width), f32),
        c_send=VMEM((peers, SRC_CAP, width), bf16),
        c_recv=VMEM((peers, SRC_CAP, width), bf16),
        w_sem=dma((zs, 2)),
        b_sem=dma((9,)),
        ds_sem=dma((peers,)),
        dr_sem=dma((peers,)),
        ps_sem=dma((zs,)),
        pr_sem=dma((zs,)),
        us_sem=dma((up, 2)),
        ur_sem=dma((up, 2)),
        ls_sem=dma((down, 2)),
        lr_sem=dma((down, 2)),
        cs_sem=dma((peers,)),
        cr_sem=dma((peers,)),
        **dict(zip(("is_", "ir", "its", "itr"), ring_sems(zs, 1))),
    )
    names = [*operands, "out", *scratch]
    return pl.pallas_call(
        functools.partial(layer_kernel, zs, peers, side, features, names),
        out_shape=jax.ShapeDtypeStruct((block, width), bf16),
        in_specs=[pl.BlockSpec(memory_space=space) for _, space in operands.values()],
        out_specs=pl.BlockSpec(memory_space=VMEM),
        scratch_shapes=list(scratch.values()),
        compiler_params=pltpu.CompilerParams(
            collective_id=1, has_side_effects=True, vmem_limit_bytes=VMEM_BYTES
        ),
    )(*[value for value, _ in operands.values()])


def solution(mesh):
    in_specs = (
        P("seq", "exp", None),
        P("seq", None),
        P("seq", None),
        P(),
        P("exp", None, None),
        P("exp", "seq"),
        P("exp", "seq"),
        P("seq"),
        P("exp", "seq", None),
        P("exp", "seq", None),
        P("exp", None, "seq"),
        P(),
        P(),
    )
    zs, peers = mesh.shape["seq"] // 2, mesh.shape["exp"]
    return jax.shard_map(
        functools.partial(local, zs, peers),
        mesh=mesh,
        in_specs=in_specs,
        out_specs=P("exp", "seq"),
        check_vma=False,
    )
```

```python
import functools
import math
import types

import jax
import jax.numpy as jnp
from jax import lax
from jax.experimental import pallas as pl
from jax.experimental.pallas import tpu as pltpu
from jax.sharding import PartitionSpec as P

LAT = 512
ROPE = 64
QK_NOPE = 128
SRC_CAP = 32

EPS = 1e-06
FLOOR = -1e30
SCALE2 = (QK_NOPE + ROPE) ** (-0.5) * math.log2(math.e)
MESH = pl.DeviceIdType.MESH
VMEM = pltpu.VMEM
VMEM_BYTES = 60 * 1024 * 1024


def rdot(a, b):
    return jnp.dot(a, b, preferred_element_type=jnp.float32)


def rdot_t(a, b):
    return lax.dot_general(
        a, b, (((1,), (1,)), ((), ())), preferred_element_type=jnp.float32
    )


def rdot_tn(a, b):
    return lax.dot_general(
        a, b, (((0,), (0,)), ((), ())), preferred_element_type=jnp.float32
    )


def turn(x):
    return x.astype(jnp.float32).T.astype(jnp.bfloat16)


def place(zs):
    s = lax.axis_index("seq")
    z, c = s // 2, lax.rem(s, 2)
    above = lax.rem(z + 1, zs) * 2 + c
    below = lax.rem(z + zs - 1, zs) * 2 + c
    twin = 2 * z + 1 - c
    return z, c, above, below, twin


def greet(zs, reach, peers, side):
    z, c, _, _, twin = place(zs)
    s = 2 * z + c
    e = lax.axis_index("exp")
    barrier = pltpu.get_barrier_semaphore()

    def hello(seq, exp):
        pl.semaphore_signal(
            barrier, inc=1, device_id={"seq": seq, "exp": exp}, device_id_type=MESH
        )

    def along(j, carry):
        hello(s, lax.rem(e + j, peers))
        return carry

    lax.fori_loop(1, peers, along, 0)
    for k in range(1, reach + 1):
        hello(lax.rem(z + k, zs) * 2 + c, e)
        hello(lax.rem(z + zs - k, zs) * 2 + c, e)
    ey, ex = e // side, lax.rem(e, side)
    for j in range(1, side):
        hello(twin, ey * side + lax.rem(ex + j, side))
        hello(twin, lax.rem(ey + j, side) * side + ex)
    hello(twin, e)
    return lambda: pl.semaphore_wait(barrier, 1 + 2 * reach + peers - 1 + 2 * (side - 1))


def remote(src, dst, ssem, rsem, seq, exp):
    return pltpu.make_async_remote_copy(
        src_ref=src,
        dst_ref=dst,
        send_sem=ssem,
        recv_sem=rsem,
        device_id={"seq": seq, "exp": exp},
        device_id_type=MESH,
    )


def ring_sems(zs, parts):
    dma = pltpu.SemaphoreType.DMA
    return [dma((zs, parts)), dma((zs, parts)), dma((zs,)), dma((zs,))]


def ring_gather(
    zs, buf, sems, own, visit, stride=1, parts=1, after=None, delay=0, meanwhile=None, shared=True
):
    rs, rr, ts, tr = sems
    up, down = zs // 2, zs // 2 - 1
    z, c, _, _, twin = place(zs)
    e = lax.axis_index("exp")
    size = buf.shape[1] // parts
    lag = 1 if shared else 0

    def far(side, k):
        return lax.rem(z + (zs - k if side == 0 else k), zs)

    def index(side, k):
        return k if side == 0 else up + k

    def hop(side, k, p, step):
        slot = buf.at[2 * far(side, k) + c, pl.ds(p * size, size)]
        i = index(side, k + step)
        to = lax.rem(z + (step if side == 0 else zs - step), zs) * 2 + c
        return remote(slot, slot, rs.at[i, p], rr.at[i, p], to, e)

    def came(side, k, p):
        slot = buf.at[2 * far(side, k) + c, pl.ds(p * size, size)]
        i = index(side, k)
        return remote(slot, slot, rs.at[i, p], rr.at[i, p], twin, e)

    def share(i, zb, core):
        slot = buf.at[2 * zb + core]
        return remote(slot, slot, ts.at[i], tr.at[i], twin, e)

    limits = (up, down)
    for p in range(parts):
        for k in range(1, stride + 1):
            for side in range(2):
                if k <= limits[side]:
                    hop(side, 0, p, k).start()
    if shared:
        share(0, z, c).start()
    if meanwhile is not None:
        meanwhile()

    def step(k, carry):
        for p in range(parts):
            for side in range(2):

                @pl.when(k <= limits[side])
                def _():
                    came(side, k, p).wait_recv()

                    @pl.when(k + stride <= limits[side])
                    def _():
                        hop(side, k, p, stride).start()

                    if shared and p == parts - 1:
                        share(index(side, k), far(side, k), c).start()

        @pl.when(k == 1)
        def _():
            if shared:
                share(0, z, 1 - c).wait_recv()
            own()

        def both(j, act):
            def one(side, inner):
                @pl.when((side == 0) | (j <= down))
                def _():
                    zb = lax.rem(z + jnp.where(side == 0, zs - j, j), zs)
                    act(zb, jnp.where(side == 0, j, up + j))

                return inner

            lax.fori_loop(0, 2, one, 0)

        def arrive(zb, i):
            if shared:
                share(i, zb, 1 - c).wait_recv()
            visit(zb)

        @pl.when((k > lag) & (k <= up + lag))
        def _():
            both(k - lag, arrive)

        if after is not None:

            @pl.when(k == delay + lag)
            def _():
                after(z)

            @pl.when(k > delay + lag)
            def _():
                both(k - lag - delay, lambda zb, i: after(zb))

        return carry

    lax.fori_loop(1, up + 1 + lag + delay, step, 0)

    def settle():
        def drain(k, carry):
            for side in range(2):

                @pl.when(k <= limits[side])
                def _():
                    for p in range(parts):
                        came(side, k, p).wait_send()
                    if shared:
                        share(index(side, k), far(side, k), c).wait_send()

            return carry

        lax.fori_loop(1, up + 1, drain, 0)
        if shared:
            share(0, z, c).wait_send()

    return settle


def attend(zs, peers, side, r, meanwhile):
    q_ref, buf, cbuf = r.q, r.keys, r.prefix
    best, total, acc = r.best, r.total, r.acc
    tok, width = buf.shape[1:]
    slots = cbuf.shape[2]
    rows = q_ref.shape[0]
    heads = rows // tok
    hand, use = 2, 3
    stride = 2
    up, down = zs // 2, zs // 2 - 1
    limits = (up, down)
    z, c, _, _, twin = place(zs)
    s = 2 * z + c
    e = lax.axis_index("exp")
    ey, ex = e // side, lax.rem(e, side)
    q = jnp.where(c == 0, ex, ey)
    size = tok // side

    def line(j):
        p = lax.rem(q + j, side)
        return jnp.where(c == 0, ey * side + p, p * side + ex)

    def lanes(x, fold):
        parts = [x[:, i * 128 : (i + 1) * 128] for i in range(x.shape[1] // 128)]
        return functools.reduce(fold, parts)

    def wide(x, like):
        return jnp.concatenate([x] * (like // 128), axis=1)

    def absorb(blocks, first=False):
        scores = []
        for keys, visible in blocks:
            raw = rdot_t(q_ref[...], keys)
            scores.append(raw if visible is None else jnp.where(visible, raw, FLOOR))
        top = functools.reduce(jnp.maximum, [lanes(x, jnp.maximum) for x in scores])
        top = jnp.max(top, axis=1, keepdims=True) * SCALE2
        newest = jnp.broadcast_to(top, best.shape)
        if not first:
            before = best[...]
            newest = jnp.maximum(before, newest)
            fade = jnp.exp2(before - newest)
        best[...] = newest
        weights = [jnp.exp2(x * SCALE2 - wide(newest, x.shape[1])) for x in scores]
        added = functools.reduce(jnp.add, [lanes(x, jnp.add) for x in weights])
        total[...] = added if first else total[...] * fade + added
        summed = functools.reduce(
            jnp.add,
            [
                rdot(x.astype(jnp.bfloat16), keys[:, :LAT])
                for x, (keys, _) in zip(weights, blocks)
            ],
        )
        acc[...] = summed if first else acc[...] * wide(fade, LAT) + summed

    def pair(zb):
        return buf[pl.ds(2 * zb, 2)].reshape(2 * tok, width)

    def far(way, k):
        return lax.rem(z + (zs - k if way == 0 else k), zs)

    def index(way, k):
        return k if way == 0 else up + k

    def piece(zb, p):
        return buf.at[2 * zb + c, pl.ds(pl.multiple_of(p * size, size), size)]

    def hop(way, k, step):
        i = index(way, k + step)
        to = lax.rem(z + (step if way == 0 else zs - step), zs) * 2 + c
        slot = piece(far(way, k), q)
        return remote(slot, slot, r.rs.at[i], r.rr.at[i], to, e)

    def cache_hop(way, k, step):
        i = index(way, k + step)
        to = lax.rem(z + (step if way == 0 else zs - step), zs) * 2 + c
        slot = cbuf.at[c, far(way, k)]
        return remote(slot, slot, r.cs.at[i], r.cr.at[i], to, e)

    def came(way, k):
        i = index(way, k)
        slot = piece(far(way, k), q)
        return remote(slot, slot, r.rs.at[i], r.rr.at[i], twin, e)

    def cache_came(way, k):
        i = index(way, k)
        slot = cbuf.at[c, far(way, k)]
        return remote(slot, slot, r.cs.at[i], r.cr.at[i], twin, e)

    def spread(i, zb, j):
        slot = piece(zb, q)
        return remote(slot, slot, r.ls.at[i, j], r.lr.at[i, j], s, line(j))

    def spread_in(i, zb, j):
        slot = piece(zb, lax.rem(q + side - j, side))
        return remote(slot, slot, r.ls.at[i, j], r.lr.at[i, j], s, line(j))

    def cache_spread(i, zb, j):
        slot = cbuf.at[c, zb]
        return remote(slot, slot, r.ms.at[i, j], r.mr.at[i], s, line(j))

    def share(i, zb, core):
        slot = buf.at[2 * zb + core]
        return remote(slot, slot, r.ts.at[i], r.tr.at[i], twin, e)

    def cache_share(core):
        slot = cbuf.at[core]
        return remote(slot, slot, r.ns.at[0], r.nr.at[0], twin, e)

    def carries(zb):
        return lax.rem(zb, side) == q

    for k in range(1, stride + 1):
        for way in range(2):
            if k <= limits[way]:
                hop(way, 0, k).start()

                @pl.when(carries(z))
                def _():
                    cache_hop(way, 0, k).start()

    share(0, z, c).start()
    meanwhile()

    def step(k, carry):
        for way in range(2):
            zb, i = far(way, k), index(way, k)

            @pl.when(k <= limits[way])
            def _():
                came(way, k).wait_recv()

                @pl.when(k + stride <= limits[way])
                def _():
                    hop(way, k, stride).start()

                @pl.when(zb < z)
                def _():
                    for j in range(1, side):
                        spread(i, zb, j).start()

                @pl.when(carries(zb))
                def _():
                    cache_came(way, k).wait_recv()

                    @pl.when(k + stride <= limits[way])
                    def _():
                        cache_hop(way, k, stride).start()

                    for j in range(1, side):
                        cache_spread(i, zb, j).start()

        for way in range(2):
            zl, il = far(way, k - hand), index(way, k - hand)

            @pl.when((k > hand) & (k - hand <= limits[way]))
            def _():
                @pl.when(zl < z)
                def _():
                    for j in range(1, side):
                        spread_in(il, zl, j).wait_recv()
                    share(il, zl, c).start()

                @pl.when(jnp.logical_not(carries(zl)))
                def _():
                    cache_spread(il, zl, 1).wait_recv()

        @pl.when(k == up + hand)
        def _():
            cache_share(c).start()

        @pl.when(k == 2)
        def _():
            share(0, z, 1 - c).wait_recv()
            row = lax.broadcasted_iota(jnp.int32, (rows, 2 * tok), 0)
            key = lax.broadcasted_iota(jnp.int32, (rows, 2 * tok), 1)
            absorb([(pair(z), key <= lax.rem(row, tok) + c * tok)], True)

        j = k - use
        lower, upper = far(0, j), far(1, j)
        has_lower = (j >= 1) & (lower < z)
        has_upper = (j >= 1) & (j <= down) & (upper < z)

        @pl.when(has_lower)
        def _():
            share(j, lower, 1 - c).wait_recv()

        @pl.when(has_upper)
        def _():
            share(up + j, upper, 1 - c).wait_recv()

        @pl.when(has_lower & has_upper)
        def _():
            absorb([(pair(lower), None), (pair(upper), None)])

        @pl.when(has_lower != has_upper)
        def _():
            absorb([(pair(jnp.where(has_lower, lower, upper)), None)])

        return carry

    lax.fori_loop(1, up + use + 1, step, 0)

    cache_share(1 - c).wait_recv()
    live = r.live[0]
    prefix = []
    cores = 1 if zs * slots % 128 == 0 else 2
    for core in range(0, 2, cores):
        count = cores * zs * slots
        at = lax.broadcasted_iota(jnp.int32, (rows, count), 1)
        own_core, rest = core + at // (zs * slots), lax.rem(at, zs * slots)
        at = (rest // slots * 2 + own_core) * slots + lax.rem(rest, slots)
        prefix.append((cbuf[core : core + cores].reshape(count, width), at < live))
    absorb(prefix)

    r.vup_copy().wait()
    for h in range(heads):
        part = pl.ds(h * tok, tok)
        weight = jnp.sum(total[part, :], axis=1, keepdims=True)
        context = (acc[part, :] / weight).astype(jnp.bfloat16)
        vh = r.vup.shape[2]
        r.heads[s, :, h * vh : (h + 1) * vh] = rdot(context, r.vup[h]).astype(jnp.bfloat16)

    def settle():
        def drain(k, carry):
            for way in range(2):
                zb, i = far(way, k), index(way, k)

                @pl.when(k <= limits[way])
                def _():
                    came(way, k).wait_send()

                    @pl.when(zb < z)
                    def _():
                        for j in range(1, side):
                            spread(i, zb, j).wait_send()
                        share(i, zb, c).wait_send()

                    origin = jnp.maximum(k - stride, 0)
                    source = lax.rem(z + (zs - origin if way == 0 else origin), zs)

                    @pl.when(carries(source))
                    def _():
                        cache_came(way, k).wait_send()

                    @pl.when(carries(zb))
                    def _():
                        for j in range(1, side):
                            cache_spread(i, zb, j).wait_send()

            return carry

        lax.fori_loop(1, up + 1, drain, 0)
        share(0, z, c).wait_send()
        cache_share(c).wait_send()

    return settle


def project(zs, peers, side, r, meanwhile):
    buf, terms = r.heads, r.terms
    _, tok, inner = buf.shape
    width = r.proj.shape[1]
    z, c, _, _, twin = place(zs)
    s = 2 * z + c
    e = lax.axis_index("exp")
    ey, ex = e // side, lax.rem(e, side)
    one, two = jnp.where(c == 0, ex, ey), jnp.where(c == 0, ey, ex)
    cross = (ey, ex)

    def split(zb):
        to_y, to_x = zb // side, lax.rem(zb, side)
        return jnp.where(c == 0, to_x, to_y), jnp.where(c == 0, to_y, to_x)

    def column(to_one, to_two):
        return jnp.where(c == 0, to_two * side + to_one, to_one * side + to_two)

    def along_one(zb):
        to_one, to_two = split(zb)
        return remote(
            terms.at[zb],
            r.row_in.at[to_two, one],
            r.x_send.at[zb],
            r.x_recv.at[to_two, one],
            s,
            column(to_one, two),
        )

    def along_two(to_two, core):
        return remote(
            r.sums.at[to_two, core],
            r.col_in.at[c, two],
            r.y_send.at[to_two, core],
            r.y_recv.at[c, two],
            2 * z + core,
            column(one, to_two),
        )

    def visit(zb):
        rows = buf[2 * zb + c]
        for core in range(2):
            terms[zb, core] = rdot_t(rows, r.proj[core]).astype(jnp.bfloat16)

        @pl.when(split(zb)[0] != one)
        def _():
            along_one(zb).start()

    def after(zb):
        to_one, to_two = split(zb)

        @pl.when(to_one == one)
        def _():
            for j in range(1, side):
                g = lax.rem(one + j, side)
                slot = r.row_in.at[to_two, g]
                remote(
                    slot, slot, r.x_send.at[zb], r.x_recv.at[to_two, g], s, column(g, two)
                ).wait_recv()
            for core in range(2):
                part = terms[zb, core].astype(jnp.float32)
                for j in range(1, side):
                    part = part + r.row_in[to_two, lax.rem(one + j, side), core].astype(
                        jnp.float32
                    )

                @pl.when((to_two == two) & (core == c))
                def _():
                    span = pl.ds(pl.multiple_of(c * tok, tok), tok)
                    r.hid[span, 0:width] += part

                @pl.when((to_two != two) | (core != c))
                def _():
                    r.sums[to_two, core] = part.astype(jnp.bfloat16)
                    along_two(to_two, core).start()

    def first():
        r.proj_swap(1 - c).wait_recv()
        r.res_copy().wait()
        r.hid[...] = jnp.zeros_like(r.hid)
        r.hid[:, 0:width] = r.residual[...].astype(jnp.float32).T
        meanwhile()

    sems = (r.hs, r.hr, r.hts, r.htr)
    settle_ring = ring_gather(
        zs,
        buf,
        sems,
        lambda: visit(z),
        visit,
        parts=4,
        after=after,
        delay=2,
        meanwhile=first,
        shared=False,
    )

    for core in range(2):
        for j in range(side):
            g = lax.rem(cross[core] + j, side)

            def collect():
                slot = r.col_in.at[core, g]
                remote(
                    slot, slot, r.y_send.at[0, 0], r.y_recv.at[core, g], 2 * z + core, e
                ).wait_recv()
                r.hid[core * tok : (core + 1) * tok, 0:width] += r.col_in[core, g].astype(
                    jnp.float32
                )

            if j == 0:
                pl.when(core != c)(collect)
            else:
                collect()

    def settle():
        settle_ring()
        r.proj_swap(c).wait_send()

        def drain(zb, carry):
            @pl.when(split(zb)[0] != one)
            def _():
                along_one(zb).wait_send()

            return carry

        lax.fori_loop(0, zs, drain, 0)
        for j in range(side):
            for core in range(2):
                to_two = lax.rem(two + j, side)

                @pl.when((to_two != two) | (core != c))
                def _():
                    along_two(to_two, core).wait_send()

    return settle


def swap_exp(peers, send, recv, s_sem, r_sem, meanwhile):
    s = lax.axis_index("seq")
    e = lax.axis_index("exp")

    def copy(j, to, slot):
        return remote(send.at[to], recv.at[slot], s_sem.at[j], r_sem.at[j], s, to)

    def start(j, carry):
        copy(j, lax.rem(e + j, peers), e).start()
        return carry

    lax.fori_loop(1, peers, start, 0)
    recv[e] = send[e]
    meanwhile()

    def finish(j, carry):
        copy(j, lax.rem(e + j, peers), lax.rem(e + peers - j, peers)).wait_recv()
        return carry

    lax.fori_loop(1, peers, finish, 0)

    def settle():
        def drain(j, carry):
            copy(j, lax.rem(e + j, peers), e).wait_send()
            return carry

        lax.fori_loop(1, peers, drain, 0)

    return settle


def tables(peers, r):
    e = lax.axis_index("exp")
    block = r.pick.shape[1]
    cap = r.pack.shape[0]
    span = pl.ds(pl.multiple_of(e * block, block), block)
    named, weights = r.routes[:, span], r.weights[:, span].astype(jnp.float32)
    hits, scaled = [], []
    for x in range(peers):
        hit = named == x
        hits.append(jnp.max(jnp.where(hit, 1.0, 0.0), axis=0, keepdims=True))
        scaled.append(jnp.sum(jnp.where(hit, weights, 0.0), axis=0, keepdims=True))
    chosen = jnp.concatenate(hits, axis=0)
    before = lax.broadcasted_iota(jnp.int32, (block, block), 0)
    order = lax.broadcasted_iota(jnp.int32, (block, block), 1)
    earlier = jnp.where(before < order, 1.0, 0.0).astype(jnp.bfloat16)
    rank = rdot(chosen.astype(jnp.bfloat16), earlier)
    slot = lax.broadcasted_iota(jnp.int32, (SRC_CAP, block), 0).astype(jnp.float32)
    for x in range(peers):
        part = pl.ds(x * SRC_CAP, SRC_CAP)
        here = jnp.where((rank[x : x + 1] == slot) & (hits[x] > 0.0), 1.0, 0.0)
        r.pick[part, :] = here.astype(jnp.bfloat16)
        r.mix[part, :] = (here * scaled[x]).astype(jnp.bfloat16)
    mine = jnp.sum(jnp.where(r.routes[...] == e, 1.0, 0.0), axis=0, keepdims=True)
    mine = [mine[:, x * block : (x + 1) * block] for x in range(peers)]
    count = jnp.sum(jnp.concatenate(mine, axis=0), axis=1, keepdims=True)
    spots = peers * SRC_CAP
    lane = lax.broadcasted_iota(jnp.int32, (peers, spots), 1) // SRC_CAP
    source = lax.broadcasted_iota(jnp.int32, (peers, spots), 0)
    own = jnp.sum(jnp.where(lane == source, count, 0.0), axis=0, keepdims=True)
    start = jnp.sum(jnp.where(lane > source, count, 0.0), axis=0, keepdims=True)
    turn = lax.rem(lax.broadcasted_iota(jnp.int32, (1, spots), 1), SRC_CAP).astype(jnp.float32)
    at = jnp.where(turn < own, start + turn, -1.0)
    row = lax.broadcasted_iota(jnp.int32, (cap, spots), 0).astype(jnp.float32)
    r.pack[...] = jnp.where(row == at, 1.0, 0.0).astype(jnp.bfloat16)


def split_rows(v):
    row = lax.broadcasted_iota(jnp.int32, v.shape, 0)
    high = v.astype(jnp.bfloat16).astype(jnp.float32)
    rest = v - high
    mid = rest.astype(jnp.bfloat16).astype(jnp.float32)
    low = rest - mid
    parts = jnp.where(row == 0, high, jnp.where(row == 1, mid, jnp.where(row == 2, low, 0.0)))
    return parts.astype(jnp.bfloat16)


def join_rows(block):
    return jnp.sum(block.astype(jnp.float32), axis=0, keepdims=True)


def route(zs, peers, features, r, meanwhile):
    width, tokens = r.residual.shape
    wide = r.hid.shape[1]
    cap = r.pack.shape[0]
    half = cap // 2
    cols = r.ibuf.shape[2]
    up, down = zs // 2, zs // 2 - 1
    z, c, above, below, twin = place(zs)
    e = lax.axis_index("exp")

    gain = jnp.concatenate([r.gain[...], jnp.zeros((1, wide - width), jnp.float32)], axis=1)
    hidden = r.hid[...]
    squares = jnp.sum(hidden * hidden, axis=1, keepdims=True)
    high = squares.astype(jnp.bfloat16).astype(jnp.float32)
    rest = squares - high
    mid = rest.astype(jnp.bfloat16).astype(jnp.float32)
    low = rest - mid
    lane = lax.broadcasted_iota(jnp.int32, (tokens, wide), 1)
    ext = jnp.where(
        lane < width,
        hidden * gain,
        jnp.where(
            lane == width,
            high,
            jnp.where(lane == width + 1, mid, jnp.where(lane == width + 2, low, 0.0)),
        ),
    ).astype(jnp.bfloat16)
    r.d_send[...] = rdot(r.pick[...], ext).astype(jnp.bfloat16).reshape(r.d_send.shape)
    settle_rows = swap_exp(peers, r.d_send, r.d_recv, r.ds_sem, r.dr_sem, meanwhile)

    arrived = r.d_recv[...].reshape(peers * SRC_CAP, wide)
    packed = rdot(r.pack[...], arrived).astype(jnp.bfloat16)
    r.xs[...] = packed
    mark = lax.broadcasted_iota(jnp.int32, (16, wide), 1)
    ones = jnp.where((mark >= width) & (mark < width + 3), 1.0, 0.0).astype(jnp.bfloat16)
    r.sqv[...] = jnp.zeros_like(r.sqv)
    for h in range(2):
        span = pl.ds(pl.multiple_of((c if h == 0 else 1 - c) * half, 16), half)
        r.xo[h * half : (h + 1) * half, :] = r.xs[span, 0:width]
        r.sqv[h, :, 0:half] = rdot_t(ones, r.xs[span, :])
    own_sq = r.sqv[0]
    tail = split_rows(r.sqv[1])

    def to_twin(d):
        return pltpu.make_async_remote_copy(
            src_ref=r.other.at[d],
            dst_ref=r.theirs.at[d],
            send_sem=r.ps_sem.at[d],
            recv_sem=r.pr_sem.at[d],
            device_id={"seq": twin, "exp": e},
            device_id_type=MESH,
        )

    def partial(d):
        r.load(d, 0).wait()
        r.load(d, 1).wait()
        both = rdot(r.xo[...], r.wgu[d])
        for p in range(2):
            part = both[:, p * cols : (p + 1) * cols]
            r.other[d, p, 0:half, :] = part[half:].astype(jnp.bfloat16)
            r.other[d, p, half : half + 16, :] = tail
            r.mine[d, p] = part[:half]
        to_twin(d).start()

    def sent_rows(p):
        return pl.ds(0, half + 16 if p == 0 else half)

    def up_copy(t, p):
        return remote(
            r.up_out.at[t, p, sent_rows(p)],
            r.up_in.at[t, p, sent_rows(p)],
            r.us_sem.at[t, p],
            r.ur_sem.at[t, p],
            above,
            e,
        )

    def dn_copy(t, p):
        return remote(
            r.dn_out.at[t, p, sent_rows(p)],
            r.dn_in.at[t, p, sent_rows(p)],
            r.ls_sem.at[t, p],
            r.lr_sem.at[t, p],
            below,
            e,
        )

    def pair_sum(d, p):
        if p == 0:
            to_twin(d).wait_recv()
        body = r.mine[d, p] + r.theirs[d, p, 0:half, :].astype(jnp.float32)
        sq = own_sq + join_rows(r.theirs[d, 0, half : half + 16, :]) if p == 0 else None
        return body, sq

    def relay(d, out, into, copy, t, p, first):
        body, sq = pair_sum(d, p)
        if not first:
            copy(t - 1, p).wait_recv()
            body = body + into[t - 1, p, 0:half, :].astype(jnp.float32)
            if p == 0:
                sq = sq + join_rows(into[t - 1, p, half : half + 16, :])
        out[t, p, 0:half, :] = body.astype(jnp.bfloat16)
        if p == 0:
            out[t, p, half : half + 16, :] = split_rows(sq)
        copy(t, p).start()

    def up_dest(t):
        return lax.rem(z + up - t, zs)

    def dn_dest(t):
        return lax.rem(z + zs - down + t, zs)

    partial(up_dest(0))
    partial(dn_dest(0))
    partial(up_dest(1))
    partial(dn_dest(1))
    for p in range(2):
        relay(up_dest(0), r.up_out, r.up_in, up_copy, 0, p, True)
        relay(dn_dest(0), r.dn_out, r.dn_in, dn_copy, 0, p, True)

    def ring(t, carry):
        @pl.when(t < up - 1)
        def _():
            partial(up_dest(t + 1))
            partial(dn_dest(t + 1))

        for p in range(2):
            relay(up_dest(t), r.up_out, r.up_in, up_copy, t, p, False)

            @pl.when(t < down)
            def _():
                relay(dn_dest(t), r.dn_out, r.dn_in, dn_copy, t, p, False)

        return carry

    lax.fori_loop(1, up, ring, 0)

    sums = []
    for p in range(2):
        body, added = pair_sum(z, p)
        up_copy(up - 1, p).wait_recv()
        dn_copy(down - 1, p).wait_recv()
        sums.append(
            body
            + r.up_in[up - 1, p, 0:half, :].astype(jnp.float32)
            + r.dn_in[down - 1, p, 0:half, :].astype(jnp.float32)
        )
        if p == 0:
            sq = (
                added
                + join_rows(r.up_in[up - 1, p, half : half + 16, :])
                + join_rows(r.dn_in[down - 1, p, half : half + 16, :])
            )
    factor = lax.rsqrt(sq[0:1, :] / features + EPS)
    row = lax.broadcasted_iota(jnp.int32, (half, cols), 0)
    lane = lax.broadcasted_iota(jnp.int32, (half, cols), 1)
    factor = jnp.sum(jnp.where(row == lane, factor, 0.0), axis=1, keepdims=True)
    gate = sums[0] * factor
    lift = sums[1] * factor
    r.ibuf[2 * z + c] = (gate / (1.0 + jnp.exp(-gate)) * lift).astype(jnp.bfloat16)

    r.produced[...] = jnp.zeros_like(r.produced)

    def visit(zb):
        block = r.ibuf[pl.ds(2 * zb, 2)].reshape(cap, cols)
        span = pl.ds(pl.multiple_of(zb * cols, cols), cols)
        r.produced[...] += rdot_t(block, r.wd[:, span])

    def settle_sums():
        settle_rows()

        def drain(d, carry):
            to_twin(d).wait_send()
            return carry

        lax.fori_loop(0, zs, drain, 0)

        def drain_ring(t, carry):
            for p in range(2):
                up_copy(t, p).wait_send()

                @pl.when(t < down)
                def _():
                    dn_copy(t, p).wait_send()

            return carry

        lax.fori_loop(0, up, drain_ring, 0)
        r.wd_copy().wait()

    sems = (r.is_, r.ir, r.its, r.itr)
    settle_ring = ring_gather(
        zs, r.ibuf, sems, lambda: visit(z), visit, stride=2, meanwhile=settle_sums
    )

    produced = r.produced[...].astype(jnp.bfloat16)
    r.c_send[...] = rdot_tn(r.pack[...], produced).astype(jnp.bfloat16).reshape(r.c_send.shape)
    settle_back = swap_exp(peers, r.c_send, r.c_recv, r.cs_sem, r.cr_sem, settle_ring)
    back = r.c_recv[...].reshape(peers * SRC_CAP, width)
    r.out[...] = (r.hid[:, 0:width] + rdot_tn(r.mix[...], back)).astype(jnp.bfloat16)
    settle_back()


def layer_kernel(zs, peers, side, features, names, *refs):
    r = types.SimpleNamespace(**dict(zip(names, refs)))
    z, c, _, _, _ = place(zs)
    s = 2 * z + c
    cols = r.ibuf.shape[2]
    up, down = zs // 2, zs // 2 - 1

    def load(d, which):
        span = pl.ds(pl.multiple_of(d * cols, cols), cols)
        return pltpu.make_async_copy(
            (r.wg_hbm, r.wu_hbm)[which].at[:, span],
            r.wgu.at[d, :, pl.ds(which * cols, cols)],
            r.w_sem.at[d, which],
        )

    def load_all(d, carry):
        load(d, 0).start()
        load(d, 1).start()
        return carry

    r.load = load

    def whole(src, dst, i):
        return lambda: pltpu.make_async_copy(src, dst, r.b_sem.at[i])

    latents_copy = whole(r.latents_hbm, r.latents, 0)
    cache_copy = whole(r.cache_hbm, r.prefix.at[c, z], 1)
    queries_copy = whole(r.queries_hbm, r.queries, 2)
    routes_copy = whole(r.routes_hbm, r.routes, 3)
    weights_copy = whole(r.weights_hbm, r.weights, 4)
    r.res_copy = whole(r.residual_hbm, r.residual, 5)
    r.vup_copy = whole(r.vup_hbm, r.vup, 6)
    r.proj_copy = whole(r.proj_hbm, r.proj.at[c], 7)
    r.proj_swap = lambda core: remote(
        r.proj.at[core],
        r.proj.at[core],
        r.o_sem.at[0],
        r.o_sem.at[1],
        2 * z + 1 - c,
        lax.axis_index("exp"),
    )
    r.wd_copy = whole(r.wd_hbm, r.wd, 8)
    latents_copy().start()
    cache_copy().start()
    greeted = greet(zs, 2, peers, side)
    for copy in (queries_copy, routes_copy, weights_copy, r.res_copy, r.vup_copy):
        copy().start()
    r.proj_copy().start()
    r.wd_copy().start()
    lax.fori_loop(0, zs, load_all, 0)
    latents_copy().wait()
    r.keys[s] = turn(r.latents[...])
    cache_copy().wait()
    greeted()

    def prepare():
        tok = r.keys.shape[1]
        queries_copy().wait()
        for h in range(r.queries.shape[0]):
            r.q[h * tok : (h + 1) * tok, :] = turn(r.queries[h])
        r.proj_copy().wait()
        r.proj_swap(c).start()
        routes_copy().wait()
        weights_copy().wait()
        tables(peers, r)

    settle = attend(zs, peers, side, r, prepare)
    settle = project(zs, peers, side, r, settle)
    route(zs, peers, features, r, settle)


def local(
    zs,
    peers,
    queries,
    latents,
    cache,
    prefix_len,
    value_up,
    out_proj,
    residual,
    norm_gain,
    w_gate,
    w_up,
    w_down,
    routes,
    route_weights,
):
    bf16, f32 = jnp.bfloat16, jnp.float32
    dma = pltpu.SemaphoreType.DMA
    tok, heads, qwidth = queries.shape
    slots = cache.shape[0]
    block, width = residual.shape
    inner = out_proj.shape[0]
    cap = SRC_CAP * min(peers, 6)
    half = cap // 2
    wide = -(-(width + 3) // 128) * 128
    cols = w_gate.shape[2] // zs
    up, down = zs // 2, zs // 2 - 1
    features = width * 2 * zs
    rows = tok * heads
    side = math.isqrt(peers)

    operands = dict(
        queries_hbm=(jnp.transpose(queries, (1, 2, 0)), pl.ANY),
        latents_hbm=(latents.T, pl.ANY),
        cache_hbm=(cache, pl.ANY),
        live=(prefix_len, pltpu.SMEM),
        residual_hbm=(residual.T, pl.ANY),
        gain=(norm_gain.reshape(1, width), VMEM),
        routes_hbm=(routes.T, pl.ANY),
        weights_hbm=(route_weights.T, pl.ANY),
        vup_hbm=(value_up, pl.ANY),
        proj_hbm=(out_proj.T, pl.ANY),
        wg_hbm=(w_gate[0], pl.ANY),
        wu_hbm=(w_up[0], pl.ANY),
        wd_hbm=(w_down[0].T, pl.ANY),
    )
    scratch = dict(
        queries=VMEM((heads, qwidth, tok), bf16),
        latents=VMEM((qwidth, tok), bf16),
        residual=VMEM((width, block), bf16),
        routes=VMEM(routes.shape[::-1], jnp.int32),
        weights=VMEM(routes.shape[::-1], bf16),
        q=VMEM((rows, qwidth), bf16),
        keys=VMEM((2 * zs, tok, qwidth), bf16),
        prefix=VMEM((2, zs, slots, qwidth), bf16),
        best=VMEM((rows, 128), f32),
        total=VMEM((rows, 128), f32),
        acc=VMEM((rows, LAT), f32),
        vup=VMEM(value_up.shape, bf16),
        rs=dma((zs,)),
        rr=dma((zs,)),
        cs=dma((zs,)),
        cr=dma((zs,)),
        ls=dma((zs, side)),
        lr=dma((zs, side)),
        ms=dma((zs, side)),
        mr=dma((zs,)),
        ts=dma((zs,)),
        tr=dma((zs,)),
        ns=dma((1,)),
        nr=dma((1,)),
        heads=VMEM((2 * zs, tok, inner), bf16),
        proj=VMEM((2, width, inner), bf16),
        terms=VMEM((peers, 2, tok, width), bf16),
        row_in=VMEM((side, side, 2, tok, width), bf16),
        sums=VMEM((side, 2, tok, width), bf16),
        col_in=VMEM((2, side, tok, width), bf16),
        hid=VMEM((block, wide), f32),
        x_send=dma((peers,)),
        x_recv=dma((side, side)),
        y_send=dma((side, 2)),
        y_recv=dma((2, side)),
        **dict(zip(("hs", "hr", "hts", "htr"), ring_sems(zs, 4))),
        pick=VMEM((peers * SRC_CAP, block), bf16),
        mix=VMEM((peers * SRC_CAP, block), bf16),
        pack=VMEM((cap, peers * SRC_CAP), bf16),
        wgu=VMEM((zs, width, 2 * cols), bf16),
        wd=VMEM((width, w_down.shape[1]), bf16),
        d_send=VMEM((peers, SRC_CAP, wide), bf16),
        d_recv=VMEM((peers, SRC_CAP, wide), bf16),
        xs=VMEM((cap, wide), bf16),
        xo=VMEM((cap, width), bf16),
        sqv=VMEM((2, 16, cols), f32),
        mine=VMEM((zs, 2, half, cols), f32),
        other=VMEM((zs, 2, half + 16, cols), bf16),
        theirs=VMEM((zs, 2, half + 16, cols), bf16),
        up_out=VMEM((up, 2, half + 16, cols), bf16),
        up_in=VMEM((up, 2, half + 16, cols), bf16),
        dn_out=VMEM((down, 2, half + 16, cols), bf16),
        dn_in=VMEM((down, 2, half + 16, cols), bf16),
        ibuf=VMEM((2 * zs, half, cols), bf16),
        produced=VMEM((cap, width), f32),
        c_send=VMEM((peers, SRC_CAP, width), bf16),
        c_recv=VMEM((peers, SRC_CAP, width), bf16),
        w_sem=dma((zs, 2)),
        b_sem=dma((9,)),
        o_sem=dma((2,)),
        ds_sem=dma((peers,)),
        dr_sem=dma((peers,)),
        ps_sem=dma((zs,)),
        pr_sem=dma((zs,)),
        us_sem=dma((up, 2)),
        ur_sem=dma((up, 2)),
        ls_sem=dma((down, 2)),
        lr_sem=dma((down, 2)),
        cs_sem=dma((peers,)),
        cr_sem=dma((peers,)),
        **dict(zip(("is_", "ir", "its", "itr"), ring_sems(zs, 1))),
    )
    names = [*operands, "out", *scratch]
    return pl.pallas_call(
        functools.partial(layer_kernel, zs, peers, side, features, names),
        out_shape=jax.ShapeDtypeStruct((block, width), bf16),
        in_specs=[pl.BlockSpec(memory_space=space) for _, space in operands.values()],
        out_specs=pl.BlockSpec(memory_space=VMEM),
        scratch_shapes=list(scratch.values()),
        compiler_params=pltpu.CompilerParams(
            collective_id=1, has_side_effects=True, vmem_limit_bytes=VMEM_BYTES
        ),
    )(*[value for value, _ in operands.values()])


def solution(mesh):
    in_specs = (
        P("seq", "exp", None),
        P("seq", None),
        P("seq", None),
        P(),
        P("exp", None, None),
        P("exp", "seq"),
        P("exp", "seq"),
        P("seq"),
        P("exp", "seq", None),
        P("exp", "seq", None),
        P("exp", None, "seq"),
        P(),
        P(),
    )
    zs, peers = mesh.shape["seq"] // 2, mesh.shape["exp"]
    return jax.shard_map(
        functools.partial(local, zs, peers),
        mesh=mesh,
        in_specs=in_specs,
        out_specs=P("exp", "seq"),
        check_vma=False,
    )
```

```python
import functools
import math
import types

import jax
import jax.numpy as jnp
from jax import lax
from jax.experimental import pallas as pl
from jax.experimental.pallas import tpu as pltpu
from jax.sharding import PartitionSpec as P

LAT = 512
ROPE = 64
QK_NOPE = 128
SRC_CAP = 32

EPS = 1e-06
FLOOR = -1e30
SCALE2 = (QK_NOPE + ROPE) ** (-0.5) * math.log2(math.e)
MESH = pl.DeviceIdType.MESH
VMEM = pltpu.VMEM
VMEM_BYTES = 60 * 1024 * 1024


def rdot(a, b):
    return jnp.dot(a, b, preferred_element_type=jnp.float32)


def rdot_t(a, b):
    return lax.dot_general(
        a, b, (((1,), (1,)), ((), ())), preferred_element_type=jnp.float32
    )


def rdot_tn(a, b):
    return lax.dot_general(
        a, b, (((0,), (0,)), ((), ())), preferred_element_type=jnp.float32
    )


def turn(x):
    return x.astype(jnp.float32).T.astype(jnp.bfloat16)


def place(zs):
    s = lax.axis_index("seq")
    z, c = s // 2, lax.rem(s, 2)
    above = lax.rem(z + 1, zs) * 2 + c
    below = lax.rem(z + zs - 1, zs) * 2 + c
    twin = 2 * z + 1 - c
    return z, c, above, below, twin


def greet(zs, reach, peers, side):
    z, c, _, _, twin = place(zs)
    s = 2 * z + c
    e = lax.axis_index("exp")
    barrier = pltpu.get_barrier_semaphore()

    def hello(seq, exp):
        pl.semaphore_signal(
            barrier, inc=1, device_id={"seq": seq, "exp": exp}, device_id_type=MESH
        )

    def along(j, carry):
        hello(s, lax.rem(e + j, peers))
        return carry

    lax.fori_loop(1, peers, along, 0)
    for k in range(1, reach + 1):
        hello(lax.rem(z + k, zs) * 2 + c, e)
        hello(lax.rem(z + zs - k, zs) * 2 + c, e)
    ey, ex = e // side, lax.rem(e, side)
    for j in range(1, side):
        hello(twin, ey * side + lax.rem(ex + j, side))
        hello(twin, lax.rem(ey + j, side) * side + ex)
    hello(twin, e)
    return lambda: pl.semaphore_wait(barrier, 1 + 2 * reach + peers - 1 + 2 * (side - 1))


def remote(src, dst, ssem, rsem, seq, exp):
    return pltpu.make_async_remote_copy(
        src_ref=src,
        dst_ref=dst,
        send_sem=ssem,
        recv_sem=rsem,
        device_id={"seq": seq, "exp": exp},
        device_id_type=MESH,
    )


def ring_sems(zs, parts):
    dma = pltpu.SemaphoreType.DMA
    return [dma((zs, parts)), dma((zs, parts)), dma((zs,)), dma((zs,))]


def ring_gather(
    zs, buf, sems, own, visit, stride=1, parts=1, after=None, delay=0, meanwhile=None, shared=True
):
    rs, rr, ts, tr = sems
    up, down = zs // 2, zs // 2 - 1
    z, c, _, _, twin = place(zs)
    e = lax.axis_index("exp")
    size = buf.shape[1] // parts
    lag = 1 if shared else 0

    def far(side, k):
        return lax.rem(z + (zs - k if side == 0 else k), zs)

    def index(side, k):
        return k if side == 0 else up + k

    def hop(side, k, p, step):
        slot = buf.at[2 * far(side, k) + c, pl.ds(p * size, size)]
        i = index(side, k + step)
        to = lax.rem(z + (step if side == 0 else zs - step), zs) * 2 + c
        return remote(slot, slot, rs.at[i, p], rr.at[i, p], to, e)

    def came(side, k, p):
        slot = buf.at[2 * far(side, k) + c, pl.ds(p * size, size)]
        i = index(side, k)
        return remote(slot, slot, rs.at[i, p], rr.at[i, p], twin, e)

    def share(i, zb, core):
        slot = buf.at[2 * zb + core]
        return remote(slot, slot, ts.at[i], tr.at[i], twin, e)

    limits = (up, down)
    for p in range(parts):
        for k in range(1, stride + 1):
            for side in range(2):
                if k <= limits[side]:
                    hop(side, 0, p, k).start()
    if shared:
        share(0, z, c).start()
    if meanwhile is not None:
        meanwhile()

    def step(k, carry):
        for p in range(parts):
            for side in range(2):

                @pl.when(k <= limits[side])
                def _():
                    came(side, k, p).wait_recv()

                    @pl.when(k + stride <= limits[side])
                    def _():
                        hop(side, k, p, stride).start()

                    if shared and p == parts - 1:
                        share(index(side, k), far(side, k), c).start()

        @pl.when(k == 1)
        def _():
            if shared:
                share(0, z, 1 - c).wait_recv()
            own()

        def both(j, act):
            def one(side, inner):
                @pl.when((side == 0) | (j <= down))
                def _():
                    zb = lax.rem(z + jnp.where(side == 0, zs - j, j), zs)
                    act(zb, jnp.where(side == 0, j, up + j))

                return inner

            lax.fori_loop(0, 2, one, 0)

        def arrive(zb, i):
            if shared:
                share(i, zb, 1 - c).wait_recv()
            visit(zb)

        @pl.when((k > lag) & (k <= up + lag))
        def _():
            both(k - lag, arrive)

        if after is not None:

            @pl.when(k == delay + lag)
            def _():
                after(z)

            @pl.when(k > delay + lag)
            def _():
                both(k - lag - delay, lambda zb, i: after(zb))

        return carry

    lax.fori_loop(1, up + 1 + lag + delay, step, 0)

    def settle():
        def drain(k, carry):
            for side in range(2):

                @pl.when(k <= limits[side])
                def _():
                    for p in range(parts):
                        came(side, k, p).wait_send()
                    if shared:
                        share(index(side, k), far(side, k), c).wait_send()

            return carry

        lax.fori_loop(1, up + 1, drain, 0)
        if shared:
            share(0, z, c).wait_send()

    return settle


def attend(zs, peers, side, r, meanwhile):
    q_ref, buf, cbuf = r.q, r.keys, r.prefix
    best, total, acc = r.best, r.total, r.acc
    tok, width = buf.shape[1:]
    slots = cbuf.shape[2]
    rows = q_ref.shape[0]
    heads = rows // tok
    hand, use = 2, 3
    stride = 2
    up, down = zs // 2, zs // 2 - 1
    limits = (up, down)
    z, c, _, _, twin = place(zs)
    s = 2 * z + c
    e = lax.axis_index("exp")
    ey, ex = e // side, lax.rem(e, side)
    q = jnp.where(c == 0, ex, ey)
    size = tok // side

    def line(j):
        p = lax.rem(q + j, side)
        return jnp.where(c == 0, ey * side + p, p * side + ex)

    def lanes(x, fold):
        parts = [x[:, i * 128 : (i + 1) * 128] for i in range(x.shape[1] // 128)]
        return functools.reduce(fold, parts)

    def wide(x, like):
        return jnp.concatenate([x] * (like // 128), axis=1)

    def absorb(blocks, first=False):
        scores = []
        for keys, visible in blocks:
            raw = rdot_t(q_ref[...], keys)
            scores.append(raw if visible is None else jnp.where(visible, raw, FLOOR))
        top = functools.reduce(jnp.maximum, [lanes(x, jnp.maximum) for x in scores])
        top = jnp.max(top, axis=1, keepdims=True) * SCALE2
        newest = jnp.broadcast_to(top, best.shape)
        if not first:
            before = best[...]
            newest = jnp.maximum(before, newest)
            fade = jnp.exp2(before - newest)
        best[...] = newest
        weights = [jnp.exp2(x * SCALE2 - wide(newest, x.shape[1])) for x in scores]
        added = functools.reduce(jnp.add, [lanes(x, jnp.add) for x in weights])
        total[...] = added if first else total[...] * fade + added
        summed = functools.reduce(
            jnp.add,
            [
                rdot(x.astype(jnp.bfloat16), keys[:, :LAT])
                for x, (keys, _) in zip(weights, blocks)
            ],
        )
        acc[...] = summed if first else acc[...] * wide(fade, LAT) + summed

    def pair(zb):
        return buf[pl.ds(2 * zb, 2)].reshape(2 * tok, width)

    def far(way, k):
        return lax.rem(z + (zs - k if way == 0 else k), zs)

    def index(way, k):
        return k if way == 0 else up + k

    def piece(zb, p):
        return buf.at[2 * zb + c, pl.ds(pl.multiple_of(p * size, size), size)]

    def hop(way, k, step):
        i = index(way, k + step)
        to = lax.rem(z + (step if way == 0 else zs - step), zs) * 2 + c
        slot = piece(far(way, k), q)
        return remote(slot, slot, r.rs.at[i], r.rr.at[i], to, e)

    def cache_hop(way, k, step):
        i = index(way, k + step)
        to = lax.rem(z + (step if way == 0 else zs - step), zs) * 2 + c
        slot = cbuf.at[c, far(way, k)]
        return remote(slot, slot, r.cs.at[i], r.cr.at[i], to, e)

    def came(way, k):
        i = index(way, k)
        slot = piece(far(way, k), q)
        return remote(slot, slot, r.rs.at[i], r.rr.at[i], twin, e)

    def cache_came(way, k):
        i = index(way, k)
        slot = cbuf.at[c, far(way, k)]
        return remote(slot, slot, r.cs.at[i], r.cr.at[i], twin, e)

    def spread(i, zb, j):
        slot = piece(zb, q)
        return remote(slot, slot, r.ls.at[i, j], r.lr.at[i, j], s, line(j))

    def spread_in(i, zb, j):
        slot = piece(zb, lax.rem(q + side - j, side))
        return remote(slot, slot, r.ls.at[i, j], r.lr.at[i, j], s, line(j))

    def cache_spread(i, zb, j):
        slot = cbuf.at[c, zb]
        return remote(slot, slot, r.ms.at[i, j], r.mr.at[i], s, line(j))

    def share(i, zb, core):
        slot = buf.at[2 * zb + core]
        return remote(slot, slot, r.ts.at[i], r.tr.at[i], twin, e)

    def cache_share(core):
        slot = cbuf.at[core]
        return remote(slot, slot, r.ns.at[0], r.nr.at[0], twin, e)

    def carries(zb):
        return lax.rem(zb, side) == q

    for k in range(1, stride + 1):
        for way in range(2):
            if k <= limits[way]:
                hop(way, 0, k).start()

                @pl.when(carries(z))
                def _():
                    cache_hop(way, 0, k).start()

    share(0, z, c).start()
    meanwhile()

    def step(k, carry):
        for way in range(2):
            zb, i = far(way, k), index(way, k)

            @pl.when(k <= limits[way])
            def _():
                came(way, k).wait_recv()

                @pl.when(k + stride <= limits[way])
                def _():
                    hop(way, k, stride).start()

                @pl.when(zb < z)
                def _():
                    for j in range(1, side):
                        spread(i, zb, j).start()

                @pl.when(carries(zb))
                def _():
                    cache_came(way, k).wait_recv()

                    @pl.when(k + stride <= limits[way])
                    def _():
                        cache_hop(way, k, stride).start()

                    for j in range(1, side):
                        cache_spread(i, zb, j).start()

        for way in range(2):
            zl, il = far(way, k - hand), index(way, k - hand)

            @pl.when((k > hand) & (k - hand <= limits[way]))
            def _():
                @pl.when(zl < z)
                def _():
                    for j in range(1, side):
                        spread_in(il, zl, j).wait_recv()
                    share(il, zl, c).start()

                @pl.when(jnp.logical_not(carries(zl)))
                def _():
                    cache_spread(il, zl, 1).wait_recv()

        @pl.when(k == up + hand)
        def _():
            cache_share(c).start()

        @pl.when(k == 2)
        def _():
            share(0, z, 1 - c).wait_recv()
            row = lax.broadcasted_iota(jnp.int32, (rows, 2 * tok), 0)
            key = lax.broadcasted_iota(jnp.int32, (rows, 2 * tok), 1)
            absorb([(pair(z), key <= lax.rem(row, tok) + c * tok)], True)

        j = k - use
        lower, upper = far(0, j), far(1, j)
        has_lower = (j >= 1) & (lower < z)
        has_upper = (j >= 1) & (j <= down) & (upper < z)

        @pl.when(has_lower)
        def _():
            share(j, lower, 1 - c).wait_recv()

        @pl.when(has_upper)
        def _():
            share(up + j, upper, 1 - c).wait_recv()

        @pl.when(has_lower & has_upper)
        def _():
            absorb([(pair(lower), None), (pair(upper), None)])

        @pl.when(has_lower != has_upper)
        def _():
            absorb([(pair(jnp.where(has_lower, lower, upper)), None)])

        return carry

    lax.fori_loop(1, up + use + 1, step, 0)

    cache_share(1 - c).wait_recv()
    live = r.live[0]
    prefix = []
    cores = 1 if zs * slots % 128 == 0 else 2
    for core in range(0, 2, cores):
        count = cores * zs * slots
        at = lax.broadcasted_iota(jnp.int32, (rows, count), 1)
        own_core, rest = core + at // (zs * slots), lax.rem(at, zs * slots)
        at = (rest // slots * 2 + own_core) * slots + lax.rem(rest, slots)
        prefix.append((cbuf[core : core + cores].reshape(count, width), at < live))
    absorb(prefix)

    r.vup_copy().wait()
    for h in range(heads):
        part = pl.ds(h * tok, tok)
        weight = jnp.sum(total[part, :], axis=1, keepdims=True)
        context = (acc[part, :] / weight).astype(jnp.bfloat16)
        vh = r.vup.shape[2]
        r.heads[s, :, h * vh : (h + 1) * vh] = rdot(context, r.vup[h]).astype(jnp.bfloat16)

    def settle():
        def drain(k, carry):
            for way in range(2):
                zb, i = far(way, k), index(way, k)

                @pl.when(k <= limits[way])
                def _():
                    came(way, k).wait_send()

                    @pl.when(zb < z)
                    def _():
                        for j in range(1, side):
                            spread(i, zb, j).wait_send()
                        share(i, zb, c).wait_send()

                    origin = jnp.maximum(k - stride, 0)
                    source = lax.rem(z + (zs - origin if way == 0 else origin), zs)

                    @pl.when(carries(source))
                    def _():
                        cache_came(way, k).wait_send()

                    @pl.when(carries(zb))
                    def _():
                        for j in range(1, side):
                            cache_spread(i, zb, j).wait_send()

            return carry

        lax.fori_loop(1, up + 1, drain, 0)
        share(0, z, c).wait_send()
        cache_share(c).wait_send()

    return settle


def project(zs, peers, side, r, meanwhile):
    buf, terms = r.heads, r.terms
    _, tok, inner = buf.shape
    width = r.proj.shape[1]
    z, c, _, _, twin = place(zs)
    s = 2 * z + c
    e = lax.axis_index("exp")
    ey, ex = e // side, lax.rem(e, side)
    one, two = jnp.where(c == 0, ex, ey), jnp.where(c == 0, ey, ex)
    cross = (ey, ex)

    def split(zb):
        to_y, to_x = zb // side, lax.rem(zb, side)
        return jnp.where(c == 0, to_x, to_y), jnp.where(c == 0, to_y, to_x)

    def column(to_one, to_two):
        return jnp.where(c == 0, to_two * side + to_one, to_one * side + to_two)

    def along_one(zb):
        to_one, to_two = split(zb)
        return remote(
            terms.at[zb],
            r.row_in.at[to_two, one],
            r.x_send.at[zb],
            r.x_recv.at[to_two, one],
            s,
            column(to_one, two),
        )

    def along_two(to_two, core):
        return remote(
            r.sums.at[to_two, core],
            r.col_in.at[c, two],
            r.y_send.at[to_two, core],
            r.y_recv.at[c, two],
            2 * z + core,
            column(one, to_two),
        )

    def visit(zb):
        rows = buf[2 * zb + c]
        for core in range(2):
            terms[zb, core] = rdot_t(rows, r.proj[core]).astype(jnp.bfloat16)

        @pl.when(split(zb)[0] != one)
        def _():
            along_one(zb).start()

    def after(zb):
        to_one, to_two = split(zb)

        @pl.when(to_one == one)
        def _():
            for j in range(1, side):
                g = lax.rem(one + j, side)
                slot = r.row_in.at[to_two, g]
                remote(
                    slot, slot, r.x_send.at[zb], r.x_recv.at[to_two, g], s, column(g, two)
                ).wait_recv()
            for core in range(2):
                part = terms[zb, core].astype(jnp.float32)
                for j in range(1, side):
                    part = part + r.row_in[to_two, lax.rem(one + j, side), core].astype(
                        jnp.float32
                    )

                @pl.when((to_two == two) & (core == c))
                def _():
                    span = pl.ds(pl.multiple_of(c * tok, tok), tok)
                    r.hid[span, 0:width] += part

                @pl.when((to_two != two) | (core != c))
                def _():
                    r.sums[to_two, core] = part.astype(jnp.bfloat16)
                    along_two(to_two, core).start()

    def first():
        r.proj_swap(1 - c).wait_recv()
        r.res_copy().wait()
        r.hid[...] = jnp.zeros_like(r.hid)
        r.hid[:, 0:width] = r.residual[...].astype(jnp.float32).T
        meanwhile()

    sems = (r.hs, r.hr, r.hts, r.htr)
    settle_ring = ring_gather(
        zs,
        buf,
        sems,
        lambda: visit(z),
        visit,
        parts=4,
        after=after,
        delay=2,
        meanwhile=first,
        shared=False,
    )

    for core in range(2):
        for j in range(side):
            g = lax.rem(cross[core] + j, side)

            def collect():
                slot = r.col_in.at[core, g]
                remote(
                    slot, slot, r.y_send.at[0, 0], r.y_recv.at[core, g], 2 * z + core, e
                ).wait_recv()
                r.hid[core * tok : (core + 1) * tok, 0:width] += r.col_in[core, g].astype(
                    jnp.float32
                )

            if j == 0:
                pl.when(core != c)(collect)
            else:
                collect()

    def settle():
        settle_ring()
        r.proj_swap(c).wait_send()

        def drain(zb, carry):
            @pl.when(split(zb)[0] != one)
            def _():
                along_one(zb).wait_send()

            return carry

        lax.fori_loop(0, zs, drain, 0)
        for j in range(side):
            for core in range(2):
                to_two = lax.rem(two + j, side)

                @pl.when((to_two != two) | (core != c))
                def _():
                    along_two(to_two, core).wait_send()

    return settle


def swap_exp(peers, send, recv, s_sem, r_sem, meanwhile):
    s = lax.axis_index("seq")
    e = lax.axis_index("exp")

    def copy(j, to, slot):
        return remote(send.at[to], recv.at[slot], s_sem.at[j], r_sem.at[j], s, to)

    def start(j, carry):
        copy(j, lax.rem(e + j, peers), e).start()
        return carry

    lax.fori_loop(1, peers, start, 0)
    recv[e] = send[e]
    meanwhile()

    def finish(j, carry):
        copy(j, lax.rem(e + j, peers), lax.rem(e + peers - j, peers)).wait_recv()
        return carry

    lax.fori_loop(1, peers, finish, 0)

    def settle():
        def drain(j, carry):
            copy(j, lax.rem(e + j, peers), e).wait_send()
            return carry

        lax.fori_loop(1, peers, drain, 0)

    return settle


def tables(peers, r):
    e = lax.axis_index("exp")
    block = r.pick.shape[1]
    cap = r.pack.shape[0]
    span = pl.ds(pl.multiple_of(e * block, block), block)
    named, weights = r.routes[:, span], r.weights[:, span].astype(jnp.float32)
    hits, scaled = [], []
    for x in range(peers):
        hit = named == x
        hits.append(jnp.max(jnp.where(hit, 1.0, 0.0), axis=0, keepdims=True))
        scaled.append(jnp.sum(jnp.where(hit, weights, 0.0), axis=0, keepdims=True))
    chosen = jnp.concatenate(hits, axis=0)
    before = lax.broadcasted_iota(jnp.int32, (block, block), 0)
    order = lax.broadcasted_iota(jnp.int32, (block, block), 1)
    earlier = jnp.where(before < order, 1.0, 0.0).astype(jnp.bfloat16)
    rank = rdot(chosen.astype(jnp.bfloat16), earlier)
    slot = lax.broadcasted_iota(jnp.int32, (SRC_CAP, block), 0).astype(jnp.float32)
    for x in range(peers):
        part = pl.ds(x * SRC_CAP, SRC_CAP)
        here = jnp.where((rank[x : x + 1] == slot) & (hits[x] > 0.0), 1.0, 0.0)
        r.pick[part, :] = here.astype(jnp.bfloat16)
        r.mix[part, :] = (here * scaled[x]).astype(jnp.bfloat16)
    mine = jnp.sum(jnp.where(r.routes[...] == e, 1.0, 0.0), axis=0, keepdims=True)
    mine = [mine[:, x * block : (x + 1) * block] for x in range(peers)]
    count = jnp.sum(jnp.concatenate(mine, axis=0), axis=1, keepdims=True)
    spots = peers * SRC_CAP
    lane = lax.broadcasted_iota(jnp.int32, (peers, spots), 1) // SRC_CAP
    source = lax.broadcasted_iota(jnp.int32, (peers, spots), 0)
    own = jnp.sum(jnp.where(lane == source, count, 0.0), axis=0, keepdims=True)
    start = jnp.sum(jnp.where(lane > source, count, 0.0), axis=0, keepdims=True)
    turn = lax.rem(lax.broadcasted_iota(jnp.int32, (1, spots), 1), SRC_CAP).astype(jnp.float32)
    at = jnp.where(turn < own, start + turn, -1.0)
    row = lax.broadcasted_iota(jnp.int32, (cap, spots), 0).astype(jnp.float32)
    r.pack[...] = jnp.where(row == at, 1.0, 0.0).astype(jnp.bfloat16)


def split_rows(v):
    row = lax.broadcasted_iota(jnp.int32, v.shape, 0)
    high = v.astype(jnp.bfloat16).astype(jnp.float32)
    rest = v - high
    mid = rest.astype(jnp.bfloat16).astype(jnp.float32)
    low = rest - mid
    parts = jnp.where(row == 0, high, jnp.where(row == 1, mid, jnp.where(row == 2, low, 0.0)))
    return parts.astype(jnp.bfloat16)


def join_rows(block):
    return jnp.sum(block.astype(jnp.float32), axis=0, keepdims=True)


def route(zs, peers, features, r, meanwhile):
    width, tokens = r.residual.shape
    wide = r.hid.shape[1]
    cap = r.pack.shape[0]
    half = cap // 2
    cols = r.ibuf.shape[2]
    up, down = zs // 2, zs // 2 - 1
    z, c, _, _, twin = place(zs)
    e = lax.axis_index("exp")

    gain = jnp.concatenate([r.gain[...], jnp.zeros((1, wide - width), jnp.float32)], axis=1)
    hidden = r.hid[...]
    squares = jnp.sum(hidden * hidden, axis=1, keepdims=True)
    high = squares.astype(jnp.bfloat16).astype(jnp.float32)
    rest = squares - high
    mid = rest.astype(jnp.bfloat16).astype(jnp.float32)
    low = rest - mid
    lane = lax.broadcasted_iota(jnp.int32, (tokens, wide), 1)
    ext = jnp.where(
        lane < width,
        hidden * gain,
        jnp.where(
            lane == width,
            high,
            jnp.where(lane == width + 1, mid, jnp.where(lane == width + 2, low, 0.0)),
        ),
    ).astype(jnp.bfloat16)
    r.d_send[...] = rdot(r.pick[...], ext).astype(jnp.bfloat16).reshape(r.d_send.shape)
    settle_rows = swap_exp(peers, r.d_send, r.d_recv, r.ds_sem, r.dr_sem, meanwhile)

    arrived = r.d_recv[...].reshape(peers * SRC_CAP, wide)
    packed = rdot(r.pack[...], arrived).astype(jnp.bfloat16)
    r.xs[...] = packed
    mark = lax.broadcasted_iota(jnp.int32, (16, wide), 1)
    ones = jnp.where((mark >= width) & (mark < width + 3), 1.0, 0.0).astype(jnp.bfloat16)
    r.sqv[...] = jnp.zeros_like(r.sqv)
    for h in range(2):
        span = pl.ds(pl.multiple_of((c if h == 0 else 1 - c) * half, 16), half)
        r.xo[h * half : (h + 1) * half, :] = r.xs[span, 0:width]
        r.sqv[h, :, 0:half] = rdot_t(ones, r.xs[span, :])
    own_sq = r.sqv[0]
    tail = split_rows(r.sqv[1])

    def to_twin(d):
        return pltpu.make_async_remote_copy(
            src_ref=r.other.at[d],
            dst_ref=r.theirs.at[d],
            send_sem=r.ps_sem.at[d],
            recv_sem=r.pr_sem.at[d],
            device_id={"seq": twin, "exp": e},
            device_id_type=MESH,
        )

    def partial(d):
        r.load(d, 0).wait()
        r.load(d, 1).wait()
        both = rdot(r.xo[...], r.wgu[d])
        for p in range(2):
            part = both[:, p * cols : (p + 1) * cols]
            r.other[d, p, 0:half, :] = part[half:].astype(jnp.bfloat16)
            r.other[d, p, half : half + 16, :] = tail
            r.mine[d, p] = part[:half]
        to_twin(d).start()

    def sent_rows(p):
        return pl.ds(0, half + 16 if p == 0 else half)

    def chunk_copy(way, d, p):
        out, into, ssem, rsem = chains[way]
        ahead = jnp.minimum(d, 2)
        to = lax.rem(z + (ahead if way == 0 else zs - ahead), zs) * 2 + c
        return remote(
            out.at[d - 1, p, sent_rows(p)],
            into.at[d - 1, p, sent_rows(p)],
            ssem.at[d - 1, p],
            rsem.at[d - 1, p],
            to,
            e,
        )

    chains = (
        (r.up_out, r.up_in, r.us_sem, r.ur_sem),
        (r.dn_out, r.dn_in, r.ls_sem, r.lr_sem),
    )
    limits = (up, down)

    def end(way, d):
        return lax.rem(z + (d if way == 0 else zs - d), zs)

    def pair_sum(d, p):
        if p == 0:
            to_twin(d).wait_recv()
        body = r.mine[d, p] + r.theirs[d, p, 0:half, :].astype(jnp.float32)
        sq = own_sq + join_rows(r.theirs[d, 0, half : half + 16, :]) if p == 0 else None
        return body, sq

    def relay(way, d, p, first):
        out, into, _, _ = chains[way]
        body, sq = pair_sum(end(way, d), p)
        if not first:
            chunk_copy(way, d + 2, p).wait_recv()
            body = body + into[d + 1, p, 0:half, :].astype(jnp.float32)
            if p == 0:
                sq = sq + join_rows(into[d + 1, p, half : half + 16, :])
        out[d - 1, p, 0:half, :] = body.astype(jnp.bfloat16)
        if p == 0:
            out[d - 1, p, half : half + 16, :] = split_rows(sq)
        chunk_copy(way, d, p).start()

    def order(t):
        return [(way, limits[way] - 2 * t - x) for x in range(2) for way in range(2)]

    for way, d in order(0):
        partial(end(way, d))
    for way, d in order(0):
        if d >= 1:
            for p in range(2):
                relay(way, d, p, True)

    def ring(t, carry):
        for way, d in order(t):
            partial(end(way, d))
        for way, d in order(t):

            @pl.when(d >= 1)
            def _():
                for p in range(2):
                    relay(way, d, p, False)

        return carry

    lax.fori_loop(1, up // 2, ring, 0)

    sums = []
    for p in range(2):
        total, added = pair_sum(z, p)
        for way in range(2):
            for d in range(1, min(2, limits[way]) + 1):
                into = chains[way][1]
                chunk_copy(way, d, p).wait_recv()
                total = total + into[d - 1, p, 0:half, :].astype(jnp.float32)
                if p == 0:
                    added = added + join_rows(into[d - 1, p, half : half + 16, :])
        sums.append(total)
        if p == 0:
            sq = added
    factor = lax.rsqrt(sq[0:1, :] / features + EPS)
    row = lax.broadcasted_iota(jnp.int32, (half, cols), 0)
    lane = lax.broadcasted_iota(jnp.int32, (half, cols), 1)
    factor = jnp.sum(jnp.where(row == lane, factor, 0.0), axis=1, keepdims=True)
    gate = sums[0] * factor
    lift = sums[1] * factor
    r.ibuf[2 * z + c] = (gate / (1.0 + jnp.exp(-gate)) * lift).astype(jnp.bfloat16)

    r.produced[...] = jnp.zeros_like(r.produced)

    def visit(zb):
        block = r.ibuf[pl.ds(2 * zb, 2)].reshape(cap, cols)
        span = pl.ds(pl.multiple_of(zb * cols, cols), cols)
        r.produced[...] += rdot_t(block, r.wd[:, span])

    def settle_sums():
        settle_rows()

        def drain(d, carry):
            to_twin(d).wait_send()
            return carry

        lax.fori_loop(0, zs, drain, 0)

        def drain_ring(t, carry):
            for p in range(2):
                chunk_copy(0, t, p).wait_send()

                @pl.when(t <= down)
                def _():
                    chunk_copy(1, t, p).wait_send()

            return carry

        lax.fori_loop(1, up + 1, drain_ring, 0)
        r.wd_copy().wait()

    sems = (r.is_, r.ir, r.its, r.itr)
    settle_ring = ring_gather(
        zs, r.ibuf, sems, lambda: visit(z), visit, stride=2, meanwhile=settle_sums
    )

    produced = r.produced[...].astype(jnp.bfloat16)
    r.c_send[...] = rdot_tn(r.pack[...], produced).astype(jnp.bfloat16).reshape(r.c_send.shape)
    settle_back = swap_exp(peers, r.c_send, r.c_recv, r.cs_sem, r.cr_sem, settle_ring)
    back = r.c_recv[...].reshape(peers * SRC_CAP, width)
    r.out[...] = (r.hid[:, 0:width] + rdot_tn(r.mix[...], back)).T.astype(jnp.bfloat16)
    settle_back()


def layer_kernel(zs, peers, side, features, names, *refs):
    r = types.SimpleNamespace(**dict(zip(names, refs)))
    z, c, _, _, _ = place(zs)
    s = 2 * z + c
    cols = r.ibuf.shape[2]
    up, down = zs // 2, zs // 2 - 1

    def load(d, which):
        span = pl.ds(pl.multiple_of(d * cols, cols), cols)
        return pltpu.make_async_copy(
            (r.wg_hbm, r.wu_hbm)[which].at[:, span],
            r.wgu.at[d, :, pl.ds(which * cols, cols)],
            r.w_sem.at[d, which],
        )

    def load_all(d, carry):
        load(d, 0).start()
        load(d, 1).start()
        return carry

    r.load = load

    def whole(src, dst, i):
        return lambda: pltpu.make_async_copy(src, dst, r.b_sem.at[i])

    latents_copy = whole(r.latents_hbm, r.latents, 0)
    cache_copy = whole(r.cache_hbm, r.prefix.at[c, z], 1)
    queries_copy = whole(r.queries_hbm, r.queries, 2)
    routes_copy = whole(r.routes_hbm, r.routes, 3)
    weights_copy = whole(r.weights_hbm, r.weights, 4)
    r.res_copy = whole(r.residual_hbm, r.residual, 5)
    r.vup_copy = whole(r.vup_hbm, r.vup, 6)
    r.proj_copy = whole(r.proj_hbm, r.proj.at[c], 7)
    r.proj_swap = lambda core: remote(
        r.proj.at[core],
        r.proj.at[core],
        r.o_sem.at[0],
        r.o_sem.at[1],
        2 * z + 1 - c,
        lax.axis_index("exp"),
    )
    r.wd_copy = whole(r.wd_hbm, r.wd, 8)
    latents_copy().start()
    cache_copy().start()
    greeted = greet(zs, 2, peers, side)
    for copy in (queries_copy, routes_copy, weights_copy, r.res_copy, r.vup_copy):
        copy().start()
    r.proj_copy().start()
    r.wd_copy().start()
    lax.fori_loop(0, zs, load_all, 0)
    latents_copy().wait()
    r.keys[s] = turn(r.latents[...])
    cache_copy().wait()
    greeted()

    def prepare():
        tok = r.keys.shape[1]
        queries_copy().wait()
        for h in range(r.queries.shape[0]):
            r.q[h * tok : (h + 1) * tok, :] = turn(r.queries[h])
        r.proj_copy().wait()
        r.proj_swap(c).start()
        routes_copy().wait()
        weights_copy().wait()
        tables(peers, r)

    settle = attend(zs, peers, side, r, prepare)
    settle = project(zs, peers, side, r, settle)
    route(zs, peers, features, r, settle)


def local(
    zs,
    peers,
    queries,
    latents,
    cache,
    prefix_len,
    value_up,
    out_proj,
    residual,
    norm_gain,
    w_gate,
    w_up,
    w_down,
    routes,
    route_weights,
):
    bf16, f32 = jnp.bfloat16, jnp.float32
    dma = pltpu.SemaphoreType.DMA
    tok, heads, qwidth = queries.shape
    slots = cache.shape[0]
    block, width = residual.shape
    inner = out_proj.shape[0]
    cap = SRC_CAP * min(peers, 6)
    half = cap // 2
    wide = -(-(width + 3) // 128) * 128
    cols = w_gate.shape[2] // zs
    up, down = zs // 2, zs // 2 - 1
    features = width * 2 * zs
    rows = tok * heads
    side = math.isqrt(peers)

    operands = dict(
        queries_hbm=(jnp.transpose(queries, (1, 2, 0)), pl.ANY),
        latents_hbm=(latents.T, pl.ANY),
        cache_hbm=(cache, pl.ANY),
        live=(prefix_len, pltpu.SMEM),
        residual_hbm=(residual.T, pl.ANY),
        gain=(norm_gain.reshape(1, width), VMEM),
        routes_hbm=(routes.T, pl.ANY),
        weights_hbm=(route_weights.T, pl.ANY),
        vup_hbm=(value_up, pl.ANY),
        proj_hbm=(out_proj.T, pl.ANY),
        wg_hbm=(w_gate[0], pl.ANY),
        wu_hbm=(w_up[0], pl.ANY),
        wd_hbm=(w_down[0].T, pl.ANY),
    )
    scratch = dict(
        queries=VMEM((heads, qwidth, tok), bf16),
        latents=VMEM((qwidth, tok), bf16),
        residual=VMEM((width, block), bf16),
        routes=VMEM(routes.shape[::-1], jnp.int32),
        weights=VMEM(routes.shape[::-1], bf16),
        q=VMEM((rows, qwidth), bf16),
        keys=VMEM((2 * zs, tok, qwidth), bf16),
        prefix=VMEM((2, zs, slots, qwidth), bf16),
        best=VMEM((rows, 128), f32),
        total=VMEM((rows, 128), f32),
        acc=VMEM((rows, LAT), f32),
        vup=VMEM(value_up.shape, bf16),
        rs=dma((zs,)),
        rr=dma((zs,)),
        cs=dma((zs,)),
        cr=dma((zs,)),
        ls=dma((zs, side)),
        lr=dma((zs, side)),
        ms=dma((zs, side)),
        mr=dma((zs,)),
        ts=dma((zs,)),
        tr=dma((zs,)),
        ns=dma((1,)),
        nr=dma((1,)),
        heads=VMEM((2 * zs, tok, inner), bf16),
        proj=VMEM((2, width, inner), bf16),
        terms=VMEM((peers, 2, tok, width), bf16),
        row_in=VMEM((side, side, 2, tok, width), bf16),
        sums=VMEM((side, 2, tok, width), bf16),
        col_in=VMEM((2, side, tok, width), bf16),
        hid=VMEM((block, wide), f32),
        x_send=dma((peers,)),
        x_recv=dma((side, side)),
        y_send=dma((side, 2)),
        y_recv=dma((2, side)),
        **dict(zip(("hs", "hr", "hts", "htr"), ring_sems(zs, 4))),
        pick=VMEM((peers * SRC_CAP, block), bf16),
        mix=VMEM((peers * SRC_CAP, block), bf16),
        pack=VMEM((cap, peers * SRC_CAP), bf16),
        wgu=VMEM((zs, width, 2 * cols), bf16),
        wd=VMEM((width, w_down.shape[1]), bf16),
        d_send=VMEM((peers, SRC_CAP, wide), bf16),
        d_recv=VMEM((peers, SRC_CAP, wide), bf16),
        xs=VMEM((cap, wide), bf16),
        xo=VMEM((cap, width), bf16),
        sqv=VMEM((2, 16, cols), f32),
        mine=VMEM((zs, 2, half, cols), f32),
        other=VMEM((zs, 2, half + 16, cols), bf16),
        theirs=VMEM((zs, 2, half + 16, cols), bf16),
        up_out=VMEM((up, 2, half + 16, cols), bf16),
        up_in=VMEM((up, 2, half + 16, cols), bf16),
        dn_out=VMEM((down, 2, half + 16, cols), bf16),
        dn_in=VMEM((down, 2, half + 16, cols), bf16),
        ibuf=VMEM((2 * zs, half, cols), bf16),
        produced=VMEM((cap, width), f32),
        c_send=VMEM((peers, SRC_CAP, width), bf16),
        c_recv=VMEM((peers, SRC_CAP, width), bf16),
        w_sem=dma((zs, 2)),
        b_sem=dma((9,)),
        o_sem=dma((2,)),
        ds_sem=dma((peers,)),
        dr_sem=dma((peers,)),
        ps_sem=dma((zs,)),
        pr_sem=dma((zs,)),
        us_sem=dma((up, 2)),
        ur_sem=dma((up, 2)),
        ls_sem=dma((down, 2)),
        lr_sem=dma((down, 2)),
        cs_sem=dma((peers,)),
        cr_sem=dma((peers,)),
        **dict(zip(("is_", "ir", "its", "itr"), ring_sems(zs, 1))),
    )
    names = [*operands, "out", *scratch]
    return pl.pallas_call(
        functools.partial(layer_kernel, zs, peers, side, features, names),
        out_shape=jax.ShapeDtypeStruct((width, block), bf16),
        in_specs=[pl.BlockSpec(memory_space=space) for _, space in operands.values()],
        out_specs=pl.BlockSpec(memory_space=VMEM),
        scratch_shapes=list(scratch.values()),
        compiler_params=pltpu.CompilerParams(
            collective_id=1, has_side_effects=True, vmem_limit_bytes=VMEM_BYTES
        ),
    )(*[value for value, _ in operands.values()]).T


def solution(mesh):
    in_specs = (
        P("seq", "exp", None),
        P("seq", None),
        P("seq", None),
        P(),
        P("exp", None, None),
        P("exp", "seq"),
        P("exp", "seq"),
        P("seq"),
        P("exp", "seq", None),
        P("exp", "seq", None),
        P("exp", None, "seq"),
        P(),
        P(),
    )
    zs, peers = mesh.shape["seq"] // 2, mesh.shape["exp"]
    return jax.shard_map(
        functools.partial(local, zs, peers),
        mesh=mesh,
        in_specs=in_specs,
        out_specs=P("exp", "seq"),
        check_vma=False,
    )
```

```python
import functools
import math
import types

import jax
import jax.numpy as jnp
from jax import lax
from jax.experimental import pallas as pl
from jax.experimental.pallas import tpu as pltpu
from jax.sharding import PartitionSpec as P

LAT = 512
ROPE = 64
QK_NOPE = 128
SRC_CAP = 32

EPS = 1e-06
FLOOR = -1e30
SCALE2 = (QK_NOPE + ROPE) ** (-0.5) * math.log2(math.e)
MESH = pl.DeviceIdType.MESH
VMEM = pltpu.VMEM
VMEM_BYTES = 60 * 1024 * 1024


def rdot(a, b):
    return jnp.dot(a, b, preferred_element_type=jnp.float32)


def rdot_t(a, b):
    return lax.dot_general(
        a, b, (((1,), (1,)), ((), ())), preferred_element_type=jnp.float32
    )


def rdot_tn(a, b):
    return lax.dot_general(
        a, b, (((0,), (0,)), ((), ())), preferred_element_type=jnp.float32
    )


def turn(x):
    return x.astype(jnp.float32).T.astype(jnp.bfloat16)


def place(zs):
    s = lax.axis_index("seq")
    z, c = s // 2, lax.rem(s, 2)
    above = lax.rem(z + 1, zs) * 2 + c
    below = lax.rem(z + zs - 1, zs) * 2 + c
    twin = 2 * z + 1 - c
    return z, c, above, below, twin


def greet(zs, reach, peers, side):
    z, c, _, _, twin = place(zs)
    s = 2 * z + c
    e = lax.axis_index("exp")
    barrier = pltpu.get_barrier_semaphore()

    def hello(seq, exp):
        pl.semaphore_signal(
            barrier, inc=1, device_id={"seq": seq, "exp": exp}, device_id_type=MESH
        )

    def along(j, carry):
        hello(s, lax.rem(e + j, peers))
        return carry

    lax.fori_loop(1, peers, along, 0)
    for k in range(1, reach + 1):
        hello(lax.rem(z + k, zs) * 2 + c, e)
        hello(lax.rem(z + zs - k, zs) * 2 + c, e)
    ey, ex = e // side, lax.rem(e, side)
    for j in range(1, side):
        hello(twin, ey * side + lax.rem(ex + j, side))
        hello(twin, lax.rem(ey + j, side) * side + ex)
    hello(twin, e)
    return lambda: pl.semaphore_wait(barrier, 1 + 2 * reach + peers - 1 + 2 * (side - 1))


def remote(src, dst, ssem, rsem, seq, exp):
    return pltpu.make_async_remote_copy(
        src_ref=src,
        dst_ref=dst,
        send_sem=ssem,
        recv_sem=rsem,
        device_id={"seq": seq, "exp": exp},
        device_id_type=MESH,
    )


def ring_sems(zs, parts):
    dma = pltpu.SemaphoreType.DMA
    return [dma((zs, parts)), dma((zs, parts)), dma((zs,)), dma((zs,))]


def ring_gather(
    zs, buf, sems, own, visit, stride=1, parts=1, after=None, delay=0, meanwhile=None, shared=True
):
    rs, rr, ts, tr = sems
    up, down = zs // 2, zs // 2 - 1
    z, c, _, _, twin = place(zs)
    e = lax.axis_index("exp")
    size = buf.shape[1] // parts
    lag = 1 if shared else 0

    def far(side, k):
        return lax.rem(z + (zs - k if side == 0 else k), zs)

    def index(side, k):
        return k if side == 0 else up + k

    def hop(side, k, p, step):
        slot = buf.at[2 * far(side, k) + c, pl.ds(p * size, size)]
        i = index(side, k + step)
        to = lax.rem(z + (step if side == 0 else zs - step), zs) * 2 + c
        return remote(slot, slot, rs.at[i, p], rr.at[i, p], to, e)

    def came(side, k, p):
        slot = buf.at[2 * far(side, k) + c, pl.ds(p * size, size)]
        i = index(side, k)
        return remote(slot, slot, rs.at[i, p], rr.at[i, p], twin, e)

    def share(i, zb, core):
        slot = buf.at[2 * zb + core]
        return remote(slot, slot, ts.at[i], tr.at[i], twin, e)

    limits = (up, down)
    for p in range(parts):
        for k in range(1, stride + 1):
            for side in range(2):
                if k <= limits[side]:
                    hop(side, 0, p, k).start()
    if shared:
        share(0, z, c).start()
    if meanwhile is not None:
        meanwhile()

    def step(k, carry):
        for p in range(parts):
            for side in range(2):

                @pl.when(k <= limits[side])
                def _():
                    came(side, k, p).wait_recv()

                    @pl.when(k + stride <= limits[side])
                    def _():
                        hop(side, k, p, stride).start()

                    if shared and p == parts - 1:
                        share(index(side, k), far(side, k), c).start()

        @pl.when(k == 1)
        def _():
            if shared:
                share(0, z, 1 - c).wait_recv()
            own()

        def both(j, act):
            def one(side, inner):
                @pl.when((side == 0) | (j <= down))
                def _():
                    zb = lax.rem(z + jnp.where(side == 0, zs - j, j), zs)
                    act(zb, jnp.where(side == 0, j, up + j))

                return inner

            lax.fori_loop(0, 2, one, 0)

        def arrive(zb, i):
            if shared:
                share(i, zb, 1 - c).wait_recv()
            visit(zb)

        @pl.when((k > lag) & (k <= up + lag))
        def _():
            both(k - lag, arrive)

        if after is not None:

            @pl.when(k == delay + lag)
            def _():
                after(z)

            @pl.when(k > delay + lag)
            def _():
                both(k - lag - delay, lambda zb, i: after(zb))

        return carry

    lax.fori_loop(1, up + 1 + lag + delay, step, 0)

    def settle():
        def drain(k, carry):
            for side in range(2):

                @pl.when(k <= limits[side])
                def _():
                    for p in range(parts):
                        came(side, k, p).wait_send()
                    if shared:
                        share(index(side, k), far(side, k), c).wait_send()

            return carry

        lax.fori_loop(1, up + 1, drain, 0)
        if shared:
            share(0, z, c).wait_send()

    return settle


def attend(zs, peers, side, r, meanwhile, later):
    q_ref, buf, cbuf = r.q, r.keys, r.prefix
    best, total, acc = r.best, r.total, r.acc
    tok, width = buf.shape[1:]
    slots = cbuf.shape[2]
    rows = q_ref.shape[0]
    heads = rows // tok
    hand, use = 2, 3
    stride = 2
    up, down = zs // 2, zs // 2 - 1
    limits = (up, down)
    z, c, _, _, twin = place(zs)
    s = 2 * z + c
    e = lax.axis_index("exp")
    ey, ex = e // side, lax.rem(e, side)
    q = jnp.where(c == 0, ex, ey)
    size = tok // side

    def line(j):
        p = lax.rem(q + j, side)
        return jnp.where(c == 0, ey * side + p, p * side + ex)

    def lanes(x, fold):
        parts = [x[:, i * 128 : (i + 1) * 128] for i in range(x.shape[1] // 128)]
        return functools.reduce(fold, parts)

    def wide(x, like):
        return jnp.concatenate([x] * (like // 128), axis=1)

    def absorb(blocks, first=False):
        band = min(rows, 256)
        spans = [slice(at, at + band) for at in range(0, rows, band)]
        scores = []
        for span in spans:
            scores.append([])
            for keys, visible in blocks:
                raw = rdot_t(q_ref[span, :], keys)
                scores[-1].append(
                    raw if visible is None else jnp.where(visible[span], raw, FLOOR)
                )
        for span, held in zip(spans, scores):
            top = functools.reduce(jnp.maximum, [lanes(x, jnp.maximum) for x in held])
            top = jnp.max(top, axis=1, keepdims=True) * SCALE2
            newest = jnp.broadcast_to(top, (band, best.shape[1]))
            if not first:
                before = best[span, :]
                newest = jnp.maximum(before, newest)
                fade = jnp.exp2(before - newest)
            best[span, :] = newest
            weights = [jnp.exp2(x * SCALE2 - wide(newest, x.shape[1])) for x in held]
            added = functools.reduce(jnp.add, [lanes(x, jnp.add) for x in weights])
            total[span, :] = added if first else total[span, :] * fade + added
            summed = functools.reduce(
                jnp.add,
                [
                    rdot(x.astype(jnp.bfloat16), keys[:, :LAT])
                    for x, (keys, _) in zip(weights, blocks)
                ],
            )
            acc[span, :] = summed if first else acc[span, :] * wide(fade, LAT) + summed

    def pair(zb):
        return buf[pl.ds(2 * zb, 2)].reshape(2 * tok, width)

    def far(way, k):
        return lax.rem(z + (zs - k if way == 0 else k), zs)

    def index(way, k):
        return k if way == 0 else up + k

    def piece(zb, p):
        return buf.at[2 * zb + c, pl.ds(pl.multiple_of(p * size, size), size)]

    def hop(way, k, step):
        i = index(way, k + step)
        to = lax.rem(z + (step if way == 0 else zs - step), zs) * 2 + c
        slot = piece(far(way, k), q)
        return remote(slot, slot, r.rs.at[i], r.rr.at[i], to, e)

    def cache_hop(way, k, step):
        i = index(way, k + step)
        to = lax.rem(z + (step if way == 0 else zs - step), zs) * 2 + c
        slot = cbuf.at[c, far(way, k)]
        return remote(slot, slot, r.cs.at[i], r.cr.at[i], to, e)

    def came(way, k):
        i = index(way, k)
        slot = piece(far(way, k), q)
        return remote(slot, slot, r.rs.at[i], r.rr.at[i], twin, e)

    def cache_came(way, k):
        i = index(way, k)
        slot = cbuf.at[c, far(way, k)]
        return remote(slot, slot, r.cs.at[i], r.cr.at[i], twin, e)

    def spread(i, zb, j):
        slot = piece(zb, q)
        return remote(slot, slot, r.ls.at[i, j], r.lr.at[i, j], s, line(j))

    def spread_in(i, zb, j):
        slot = piece(zb, lax.rem(q + side - j, side))
        return remote(slot, slot, r.ls.at[i, j], r.lr.at[i, j], s, line(j))

    def cache_spread(i, zb, j):
        slot = cbuf.at[c, zb]
        return remote(slot, slot, r.ms.at[i, j], r.mr.at[i], s, line(j))

    def share(i, zb, core):
        slot = buf.at[2 * zb + core]
        return remote(slot, slot, r.ts.at[i], r.tr.at[i], twin, e)

    def cache_share(core):
        slot = cbuf.at[core]
        return remote(slot, slot, r.ns.at[0], r.nr.at[0], twin, e)

    def carries(zb):
        return lax.rem(zb, side) == q

    for k in range(1, stride + 1):
        for way in range(2):
            if k <= limits[way]:
                hop(way, 0, k).start()

                @pl.when(carries(z))
                def _():
                    cache_hop(way, 0, k).start()

    share(0, z, c).start()
    meanwhile()

    def step(k, carry):
        for way in range(2):

            @pl.when(k <= limits[way])
            def _():
                came(way, k).wait_recv()

                @pl.when(k + stride <= limits[way])
                def _():
                    hop(way, k, stride).start()

        for way in range(2):
            zb, i = far(way, k), index(way, k)

            @pl.when(k <= limits[way])
            def _():
                @pl.when(zb < z)
                def _():
                    for j in range(1, side):
                        spread(i, zb, j).start()

                @pl.when(carries(zb))
                def _():
                    cache_came(way, k).wait_recv()

                    @pl.when(k + stride <= limits[way])
                    def _():
                        cache_hop(way, k, stride).start()

                    for j in range(1, side):
                        cache_spread(i, zb, j).start()

        for way in range(2):
            zl, il = far(way, k - hand), index(way, k - hand)

            @pl.when((k > hand) & (k - hand <= limits[way]))
            def _():
                @pl.when(zl < z)
                def _():
                    for j in range(1, side):
                        spread_in(il, zl, j).wait_recv()
                    share(il, zl, c).start()

                @pl.when(jnp.logical_not(carries(zl)))
                def _():
                    cache_spread(il, zl, 1).wait_recv()

        @pl.when(k == up + hand)
        def _():
            cache_share(c).start()

        @pl.when(k == 2)
        def _():
            share(0, z, 1 - c).wait_recv()
            row = lax.broadcasted_iota(jnp.int32, (rows, 2 * tok), 0)
            key = lax.broadcasted_iota(jnp.int32, (rows, 2 * tok), 1)
            absorb([(pair(z), key <= lax.rem(row, tok) + c * tok)], True)
            later()

        j = k - use
        lower, upper = far(0, j), far(1, j)
        has_lower = (j >= 1) & (lower < z)
        has_upper = (j >= 1) & (j <= down) & (upper < z)

        @pl.when(has_lower)
        def _():
            share(j, lower, 1 - c).wait_recv()

        @pl.when(has_upper)
        def _():
            share(up + j, upper, 1 - c).wait_recv()

        @pl.when(has_lower & has_upper)
        def _():
            absorb([(pair(lower), None), (pair(upper), None)])

        @pl.when(has_lower != has_upper)
        def _():
            absorb([(pair(jnp.where(has_lower, lower, upper)), None)])

        return carry

    lax.fori_loop(1, up + use + 1, step, 0)

    cache_share(1 - c).wait_recv()
    live = r.live[0]
    prefix = []
    cores = 1 if zs * slots % 128 == 0 else 2
    for core in range(0, 2, cores):
        count = cores * zs * slots
        at = lax.broadcasted_iota(jnp.int32, (rows, count), 1)
        own_core, rest = core + at // (zs * slots), lax.rem(at, zs * slots)
        at = (rest // slots * 2 + own_core) * slots + lax.rem(rest, slots)
        prefix.append((cbuf[core : core + cores].reshape(count, width), at < live))
    absorb(prefix)

    r.vup_copy().wait()
    for h in range(heads):
        part = pl.ds(h * tok, tok)
        weight = jnp.sum(total[part, :], axis=1, keepdims=True)
        context = (acc[part, :] / weight).astype(jnp.bfloat16)
        vh = r.vup.shape[2]
        r.heads[s, :, h * vh : (h + 1) * vh] = rdot(context, r.vup[h]).astype(jnp.bfloat16)

    def settle():
        def drain(k, carry):
            for way in range(2):
                zb, i = far(way, k), index(way, k)

                @pl.when(k <= limits[way])
                def _():
                    came(way, k).wait_send()

                    @pl.when(zb < z)
                    def _():
                        for j in range(1, side):
                            spread(i, zb, j).wait_send()
                        share(i, zb, c).wait_send()

                    origin = jnp.maximum(k - stride, 0)
                    source = lax.rem(z + (zs - origin if way == 0 else origin), zs)

                    @pl.when(carries(source))
                    def _():
                        cache_came(way, k).wait_send()

                    @pl.when(carries(zb))
                    def _():
                        for j in range(1, side):
                            cache_spread(i, zb, j).wait_send()

            return carry

        lax.fori_loop(1, up + 1, drain, 0)
        share(0, z, c).wait_send()
        cache_share(c).wait_send()

    return settle


def project(zs, peers, side, r):
    buf, terms = r.heads, r.terms
    _, tok, inner = buf.shape
    width = r.proj.shape[1]
    z, c, _, _, twin = place(zs)
    s = 2 * z + c
    e = lax.axis_index("exp")
    ey, ex = e // side, lax.rem(e, side)
    one, two = jnp.where(c == 0, ex, ey), jnp.where(c == 0, ey, ex)
    cross = (ey, ex)

    def split(zb):
        to_y, to_x = zb // side, lax.rem(zb, side)
        return jnp.where(c == 0, to_x, to_y), jnp.where(c == 0, to_y, to_x)

    def column(to_one, to_two):
        return jnp.where(c == 0, to_two * side + to_one, to_one * side + to_two)

    def along_one(zb):
        to_one, to_two = split(zb)
        return remote(
            terms.at[zb],
            r.row_in.at[to_two, one],
            r.x_send.at[zb],
            r.x_recv.at[to_two, one],
            s,
            column(to_one, two),
        )

    def along_two(to_two, core):
        return remote(
            r.sums.at[to_two, core],
            r.col_in.at[c, two],
            r.y_send.at[to_two, core],
            r.y_recv.at[c, two],
            2 * z + core,
            column(one, to_two),
        )

    def visit(zb):
        rows = buf[2 * zb + c]
        for core in range(2):
            terms[zb, core] = rdot_t(rows, r.proj[core]).astype(jnp.bfloat16)

        @pl.when(split(zb)[0] != one)
        def _():
            along_one(zb).start()

    def after(zb):
        to_one, to_two = split(zb)

        @pl.when(to_one == one)
        def _():
            for j in range(1, side):
                g = lax.rem(one + j, side)
                slot = r.row_in.at[to_two, g]
                remote(
                    slot, slot, r.x_send.at[zb], r.x_recv.at[to_two, g], s, column(g, two)
                ).wait_recv()
            for core in range(2):
                part = terms[zb, core].astype(jnp.float32)
                for j in range(1, side):
                    part = part + r.row_in[to_two, lax.rem(one + j, side), core].astype(
                        jnp.float32
                    )

                @pl.when((to_two == two) & (core == c))
                def _():
                    span = pl.ds(pl.multiple_of(c * tok, tok), tok)
                    r.hid[span, 0:width] += part

                @pl.when((to_two != two) | (core != c))
                def _():
                    r.sums[to_two, core] = part.astype(jnp.bfloat16)
                    along_two(to_two, core).start()

    def first():
        r.proj_swap(1 - c).wait_recv()

    sems = (r.hs, r.hr, r.hts, r.htr)
    settle_ring = ring_gather(
        zs,
        buf,
        sems,
        lambda: visit(z),
        visit,
        parts=4,
        after=after,
        delay=2,
        meanwhile=first,
        shared=False,
    )

    for core in range(2):
        for j in range(side):
            g = lax.rem(cross[core] + j, side)

            def collect():
                slot = r.col_in.at[core, g]
                remote(
                    slot, slot, r.y_send.at[0, 0], r.y_recv.at[core, g], 2 * z + core, e
                ).wait_recv()
                r.hid[core * tok : (core + 1) * tok, 0:width] += r.col_in[core, g].astype(
                    jnp.float32
                )

            if j == 0:
                pl.when(core != c)(collect)
            else:
                collect()

    def settle():
        settle_ring()
        r.proj_swap(c).wait_send()

        def drain(zb, carry):
            @pl.when(split(zb)[0] != one)
            def _():
                along_one(zb).wait_send()

            return carry

        lax.fori_loop(0, zs, drain, 0)
        for j in range(side):
            for core in range(2):
                to_two = lax.rem(two + j, side)

                @pl.when((to_two != two) | (core != c))
                def _():
                    along_two(to_two, core).wait_send()

    return settle


def swap_exp(peers, send, recv, s_sem, r_sem, meanwhile):
    s = lax.axis_index("seq")
    e = lax.axis_index("exp")

    def copy(j, to, slot):
        return remote(send.at[to], recv.at[slot], s_sem.at[j], r_sem.at[j], s, to)

    def start(j, carry):
        copy(j, lax.rem(e + j, peers), e).start()
        return carry

    lax.fori_loop(1, peers, start, 0)
    recv[e] = send[e]
    meanwhile()

    def finish(j, carry):
        copy(j, lax.rem(e + j, peers), lax.rem(e + peers - j, peers)).wait_recv()
        return carry

    lax.fori_loop(1, peers, finish, 0)

    def settle():
        def drain(j, carry):
            copy(j, lax.rem(e + j, peers), e).wait_send()
            return carry

        lax.fori_loop(1, peers, drain, 0)

    return settle


def tables(peers, r):
    e = lax.axis_index("exp")
    block = r.pick.shape[1]
    cap = r.pack.shape[0]
    span = pl.ds(pl.multiple_of(e * block, block), block)
    named, weights = r.routes[:, span], r.weights[:, span].astype(jnp.float32)
    hits, scaled = [], []
    for x in range(peers):
        hit = named == x
        hits.append(jnp.max(jnp.where(hit, 1.0, 0.0), axis=0, keepdims=True))
        scaled.append(jnp.sum(jnp.where(hit, weights, 0.0), axis=0, keepdims=True))
    chosen = jnp.concatenate(hits, axis=0)
    before = lax.broadcasted_iota(jnp.int32, (block, block), 0)
    order = lax.broadcasted_iota(jnp.int32, (block, block), 1)
    earlier = jnp.where(before < order, 1.0, 0.0).astype(jnp.bfloat16)
    rank = rdot(chosen.astype(jnp.bfloat16), earlier)
    slot = lax.broadcasted_iota(jnp.int32, (SRC_CAP, block), 0).astype(jnp.float32)
    for x in range(peers):
        part = pl.ds(x * SRC_CAP, SRC_CAP)
        here = jnp.where((rank[x : x + 1] == slot) & (hits[x] > 0.0), 1.0, 0.0)
        r.pick[part, :] = here.astype(jnp.bfloat16)
        r.mix[part, :] = (here * scaled[x]).astype(jnp.bfloat16)
    mine = jnp.sum(jnp.where(r.routes[...] == e, 1.0, 0.0), axis=0, keepdims=True)
    mine = [mine[:, x * block : (x + 1) * block] for x in range(peers)]
    count = jnp.sum(jnp.concatenate(mine, axis=0), axis=1, keepdims=True)
    spots = peers * SRC_CAP
    lane = lax.broadcasted_iota(jnp.int32, (peers, spots), 1) // SRC_CAP
    source = lax.broadcasted_iota(jnp.int32, (peers, spots), 0)
    own = jnp.sum(jnp.where(lane == source, count, 0.0), axis=0, keepdims=True)
    start = jnp.sum(jnp.where(lane > source, count, 0.0), axis=0, keepdims=True)
    turn = lax.rem(lax.broadcasted_iota(jnp.int32, (1, spots), 1), SRC_CAP).astype(jnp.float32)
    at = jnp.where(turn < own, start + turn, -1.0)
    row = lax.broadcasted_iota(jnp.int32, (cap, spots), 0).astype(jnp.float32)
    r.pack[...] = jnp.where(row == at, 1.0, 0.0).astype(jnp.bfloat16)


def split_rows(v):
    row = lax.broadcasted_iota(jnp.int32, v.shape, 0)
    high = v.astype(jnp.bfloat16).astype(jnp.float32)
    rest = v - high
    mid = rest.astype(jnp.bfloat16).astype(jnp.float32)
    low = rest - mid
    parts = jnp.where(row == 0, high, jnp.where(row == 1, mid, jnp.where(row == 2, low, 0.0)))
    return parts.astype(jnp.bfloat16)


def join_rows(block):
    return jnp.sum(block.astype(jnp.float32), axis=0, keepdims=True)


def route(zs, peers, features, r, meanwhile):
    width, tokens = r.residual.shape
    wide = r.hid.shape[1]
    cap = r.pack.shape[0]
    half = cap // 2
    cols = r.ibuf.shape[2]
    up, down = zs // 2, zs // 2 - 1
    z, c, _, _, twin = place(zs)
    e = lax.axis_index("exp")

    gain = jnp.concatenate([r.gain[...], jnp.zeros((1, wide - width), jnp.float32)], axis=1)
    hidden = r.hid[...]
    squares = jnp.sum(hidden * hidden, axis=1, keepdims=True)
    high = squares.astype(jnp.bfloat16).astype(jnp.float32)
    rest = squares - high
    mid = rest.astype(jnp.bfloat16).astype(jnp.float32)
    low = rest - mid
    lane = lax.broadcasted_iota(jnp.int32, (tokens, wide), 1)
    ext = jnp.where(
        lane < width,
        hidden * gain,
        jnp.where(
            lane == width,
            high,
            jnp.where(lane == width + 1, mid, jnp.where(lane == width + 2, low, 0.0)),
        ),
    ).astype(jnp.bfloat16)
    r.d_send[...] = rdot(r.pick[...], ext).astype(jnp.bfloat16).reshape(r.d_send.shape)
    settle_rows = swap_exp(peers, r.d_send, r.d_recv, r.ds_sem, r.dr_sem, meanwhile)

    arrived = r.d_recv[...].reshape(peers * SRC_CAP, wide)
    packed = rdot(r.pack[...], arrived).astype(jnp.bfloat16)
    r.xs[...] = packed
    mark = lax.broadcasted_iota(jnp.int32, (16, wide), 1)
    ones = jnp.where((mark >= width) & (mark < width + 3), 1.0, 0.0).astype(jnp.bfloat16)
    r.sqv[...] = jnp.zeros_like(r.sqv)
    for h in range(2):
        span = pl.ds(pl.multiple_of((c if h == 0 else 1 - c) * half, 16), half)
        r.xo[h * half : (h + 1) * half, :] = r.xs[span, 0:width]
        r.sqv[h, :, 0:half] = rdot_t(ones, r.xs[span, :])
    own_sq = r.sqv[0]
    tail = split_rows(r.sqv[1])

    def to_twin(d):
        return pltpu.make_async_remote_copy(
            src_ref=r.other.at[d],
            dst_ref=r.theirs.at[d],
            send_sem=r.ps_sem.at[d],
            recv_sem=r.pr_sem.at[d],
            device_id={"seq": twin, "exp": e},
            device_id_type=MESH,
        )

    def partial(d):
        r.load(d, 0).wait()
        r.load(d, 1).wait()
        both = rdot(r.xo[...], r.wgu[d])
        for p in range(2):
            part = both[:, p * cols : (p + 1) * cols]
            r.other[d, p, 0:half, :] = part[half:].astype(jnp.bfloat16)
            r.other[d, p, half : half + 16, :] = tail
            r.mine[d, p] = part[:half]
        to_twin(d).start()

    def sent_rows(p):
        return pl.ds(0, half + 16 if p == 0 else half)

    def chunk_copy(way, d, p):
        out, into, ssem, rsem = chains[way]
        ahead = jnp.minimum(d, 2)
        to = lax.rem(z + (ahead if way == 0 else zs - ahead), zs) * 2 + c
        return remote(
            out.at[d - 1, p, sent_rows(p)],
            into.at[d - 1, p, sent_rows(p)],
            ssem.at[d - 1, p],
            rsem.at[d - 1, p],
            to,
            e,
        )

    chains = (
        (r.up_out, r.up_in, r.us_sem, r.ur_sem),
        (r.dn_out, r.dn_in, r.ls_sem, r.lr_sem),
    )
    limits = (up, down)

    def end(way, d):
        return lax.rem(z + (d if way == 0 else zs - d), zs)

    def pair_sum(d, p):
        if p == 0:
            to_twin(d).wait_recv()
        body = r.mine[d, p] + r.theirs[d, p, 0:half, :].astype(jnp.float32)
        sq = own_sq + join_rows(r.theirs[d, 0, half : half + 16, :]) if p == 0 else None
        return body, sq

    def relay(way, d, p, first):
        out, into, _, _ = chains[way]
        body, sq = pair_sum(end(way, d), p)
        if not first:
            chunk_copy(way, d + 2, p).wait_recv()
            body = body + into[d + 1, p, 0:half, :].astype(jnp.float32)
            if p == 0:
                sq = sq + join_rows(into[d + 1, p, half : half + 16, :])
        out[d - 1, p, 0:half, :] = body.astype(jnp.bfloat16)
        if p == 0:
            out[d - 1, p, half : half + 16, :] = split_rows(sq)
        chunk_copy(way, d, p).start()

    def order(t):
        return [(way, limits[way] - 2 * t - x) for x in range(2) for way in range(2)]

    for way, d in order(0):
        partial(end(way, d))
    for way, d in order(0):
        if d >= 1:
            for p in range(2):
                relay(way, d, p, True)

    def ring(t, carry):
        for way, d in order(t):
            partial(end(way, d))
        for way, d in order(t):

            @pl.when(d >= 1)
            def _():
                for p in range(2):
                    relay(way, d, p, False)

        return carry

    lax.fori_loop(1, up // 2, ring, 0)

    sums = []
    for p in range(2):
        total, added = pair_sum(z, p)
        for way in range(2):
            for d in range(1, min(2, limits[way]) + 1):
                into = chains[way][1]
                chunk_copy(way, d, p).wait_recv()
                total = total + into[d - 1, p, 0:half, :].astype(jnp.float32)
                if p == 0:
                    added = added + join_rows(into[d - 1, p, half : half + 16, :])
        sums.append(total)
        if p == 0:
            sq = added
    factor = lax.rsqrt(sq[0:1, :] / features + EPS)
    row = lax.broadcasted_iota(jnp.int32, (half, cols), 0)
    lane = lax.broadcasted_iota(jnp.int32, (half, cols), 1)
    factor = jnp.sum(jnp.where(row == lane, factor, 0.0), axis=1, keepdims=True)
    gate = sums[0] * factor
    lift = sums[1] * factor
    r.ibuf[2 * z + c] = (gate / (1.0 + jnp.exp(-gate)) * lift).astype(jnp.bfloat16)

    r.produced[...] = jnp.zeros_like(r.produced)

    def visit(zb):
        block = r.ibuf[pl.ds(2 * zb, 2)].reshape(cap, cols)
        span = pl.ds(pl.multiple_of(zb * cols, cols), cols)
        r.produced[...] += rdot_t(block, r.wd[:, span])

    def settle_sums():
        settle_rows()

        def drain(d, carry):
            to_twin(d).wait_send()
            return carry

        lax.fori_loop(0, zs, drain, 0)

        def drain_ring(t, carry):
            for p in range(2):
                chunk_copy(0, t, p).wait_send()

                @pl.when(t <= down)
                def _():
                    chunk_copy(1, t, p).wait_send()

            return carry

        lax.fori_loop(1, up + 1, drain_ring, 0)
        r.wd_copy().wait()

    sems = (r.is_, r.ir, r.its, r.itr)
    settle_ring = ring_gather(
        zs, r.ibuf, sems, lambda: visit(z), visit, stride=2, meanwhile=settle_sums
    )

    produced = r.produced[...].astype(jnp.bfloat16)
    r.c_send[...] = rdot_tn(r.pack[...], produced).astype(jnp.bfloat16).reshape(r.c_send.shape)
    settle_back = swap_exp(peers, r.c_send, r.c_recv, r.cs_sem, r.cr_sem, settle_ring)
    back = r.c_recv[...].reshape(peers * SRC_CAP, width)
    r.out[...] = (r.hid[:, 0:width] + rdot_tn(r.mix[...], back)).T.astype(jnp.bfloat16)
    settle_back()


def layer_kernel(zs, peers, side, features, names, *refs):
    r = types.SimpleNamespace(**dict(zip(names, refs)))
    z, c, _, _, _ = place(zs)
    s = 2 * z + c
    cols = r.ibuf.shape[2]
    up, down = zs // 2, zs // 2 - 1

    def load(d, which):
        span = pl.ds(pl.multiple_of(d * cols, cols), cols)
        return pltpu.make_async_copy(
            (r.wg_hbm, r.wu_hbm)[which].at[:, span],
            r.wgu.at[d, :, pl.ds(which * cols, cols)],
            r.w_sem.at[d, which],
        )

    def load_all(d, carry):
        load(d, 0).start()
        load(d, 1).start()
        return carry

    r.load = load

    def whole(src, dst, i):
        return lambda: pltpu.make_async_copy(src, dst, r.b_sem.at[i])

    latents_copy = whole(r.latents_hbm, r.latents, 0)
    cache_copy = whole(r.cache_hbm, r.prefix.at[c, z], 1)
    queries_copy = whole(r.queries_hbm, r.queries, 2)
    routes_copy = whole(r.routes_hbm, r.routes, 3)
    weights_copy = whole(r.weights_hbm, r.weights, 4)
    r.res_copy = whole(r.residual_hbm, r.residual, 5)
    r.vup_copy = whole(r.vup_hbm, r.vup, 6)
    r.proj_copy = whole(r.proj_hbm, r.proj.at[c], 7)
    r.proj_swap = lambda core: remote(
        r.proj.at[core],
        r.proj.at[core],
        r.o_sem.at[0],
        r.o_sem.at[1],
        2 * z + 1 - c,
        lax.axis_index("exp"),
    )
    r.wd_copy = whole(r.wd_hbm, r.wd, 8)
    latents_copy().start()
    cache_copy().start()
    greeted = greet(zs, 2, peers, side)
    for copy in (queries_copy, routes_copy, weights_copy, r.res_copy, r.vup_copy):
        copy().start()
    r.proj_copy().start()
    r.wd_copy().start()
    lax.fori_loop(0, zs, load_all, 0)
    latents_copy().wait()
    r.keys[s] = turn(r.latents[...])
    cache_copy().wait()
    greeted()

    def prepare():
        tok = r.keys.shape[1]
        queries_copy().wait()
        for h in range(r.queries.shape[0]):
            r.q[h * tok : (h + 1) * tok, :] = turn(r.queries[h])
        r.proj_copy().wait()
        r.proj_swap(c).start()
        r.res_copy().wait()
        r.hid[...] = jnp.zeros_like(r.hid)
        r.hid[:, 0 : r.residual.shape[0]] = r.residual[...].astype(jnp.float32).T

    def prepare_tables():
        routes_copy().wait()
        weights_copy().wait()
        tables(peers, r)

    settle_keys = attend(zs, peers, side, r, prepare, prepare_tables)
    settle_heads = project(zs, peers, side, r)

    def settle():
        settle_keys()
        settle_heads()

    route(zs, peers, features, r, settle)


def local(
    zs,
    peers,
    queries,
    latents,
    cache,
    prefix_len,
    value_up,
    out_proj,
    residual,
    norm_gain,
    w_gate,
    w_up,
    w_down,
    routes,
    route_weights,
):
    bf16, f32 = jnp.bfloat16, jnp.float32
    dma = pltpu.SemaphoreType.DMA
    tok, heads, qwidth = queries.shape
    slots = cache.shape[0]
    block, width = residual.shape
    inner = out_proj.shape[0]
    cap = SRC_CAP * min(peers, 6)
    half = cap // 2
    wide = -(-(width + 3) // 128) * 128
    cols = w_gate.shape[2] // zs
    up, down = zs // 2, zs // 2 - 1
    features = width * 2 * zs
    rows = tok * heads
    side = math.isqrt(peers)

    operands = dict(
        queries_hbm=(jnp.transpose(queries, (1, 2, 0)), pl.ANY),
        latents_hbm=(latents.T, pl.ANY),
        cache_hbm=(cache, pl.ANY),
        live=(prefix_len, pltpu.SMEM),
        residual_hbm=(residual.T, pl.ANY),
        gain=(norm_gain.reshape(1, width), VMEM),
        routes_hbm=(routes.T, pl.ANY),
        weights_hbm=(route_weights.T, pl.ANY),
        vup_hbm=(value_up, pl.ANY),
        proj_hbm=(out_proj.T, pl.ANY),
        wg_hbm=(w_gate[0], pl.ANY),
        wu_hbm=(w_up[0], pl.ANY),
        wd_hbm=(w_down[0].T, pl.ANY),
    )
    scratch = dict(
        queries=VMEM((heads, qwidth, tok), bf16),
        latents=VMEM((qwidth, tok), bf16),
        residual=VMEM((width, block), bf16),
        routes=VMEM(routes.shape[::-1], jnp.int32),
        weights=VMEM(routes.shape[::-1], bf16),
        q=VMEM((rows, qwidth), bf16),
        keys=VMEM((2 * zs, tok, qwidth), bf16),
        prefix=VMEM((2, zs, slots, qwidth), bf16),
        best=VMEM((rows, 128), f32),
        total=VMEM((rows, 128), f32),
        acc=VMEM((rows, LAT), f32),
        vup=VMEM(value_up.shape, bf16),
        rs=dma((zs,)),
        rr=dma((zs,)),
        cs=dma((zs,)),
        cr=dma((zs,)),
        ls=dma((zs, side)),
        lr=dma((zs, side)),
        ms=dma((zs, side)),
        mr=dma((zs,)),
        ts=dma((zs,)),
        tr=dma((zs,)),
        ns=dma((1,)),
        nr=dma((1,)),
        heads=VMEM((2 * zs, tok, inner), bf16),
        proj=VMEM((2, width, inner), bf16),
        terms=VMEM((peers, 2, tok, width), bf16),
        row_in=VMEM((side, side, 2, tok, width), bf16),
        sums=VMEM((side, 2, tok, width), bf16),
        col_in=VMEM((2, side, tok, width), bf16),
        hid=VMEM((block, wide), f32),
        x_send=dma((peers,)),
        x_recv=dma((side, side)),
        y_send=dma((side, 2)),
        y_recv=dma((2, side)),
        **dict(zip(("hs", "hr", "hts", "htr"), ring_sems(zs, 4))),
        pick=VMEM((peers * SRC_CAP, block), bf16),
        mix=VMEM((peers * SRC_CAP, block), bf16),
        pack=VMEM((cap, peers * SRC_CAP), bf16),
        wgu=VMEM((zs, width, 2 * cols), bf16),
        wd=VMEM((width, w_down.shape[1]), bf16),
        d_send=VMEM((peers, SRC_CAP, wide), bf16),
        d_recv=VMEM((peers, SRC_CAP, wide), bf16),
        xs=VMEM((cap, wide), bf16),
        xo=VMEM((cap, width), bf16),
        sqv=VMEM((2, 16, cols), f32),
        mine=VMEM((zs, 2, half, cols), f32),
        other=VMEM((zs, 2, half + 16, cols), bf16),
        theirs=VMEM((zs, 2, half + 16, cols), bf16),
        up_out=VMEM((up, 2, half + 16, cols), bf16),
        up_in=VMEM((up, 2, half + 16, cols), bf16),
        dn_out=VMEM((down, 2, half + 16, cols), bf16),
        dn_in=VMEM((down, 2, half + 16, cols), bf16),
        ibuf=VMEM((2 * zs, half, cols), bf16),
        produced=VMEM((cap, width), f32),
        c_send=VMEM((peers, SRC_CAP, width), bf16),
        c_recv=VMEM((peers, SRC_CAP, width), bf16),
        w_sem=dma((zs, 2)),
        b_sem=dma((9,)),
        o_sem=dma((2,)),
        ds_sem=dma((peers,)),
        dr_sem=dma((peers,)),
        ps_sem=dma((zs,)),
        pr_sem=dma((zs,)),
        us_sem=dma((up, 2)),
        ur_sem=dma((up, 2)),
        ls_sem=dma((down, 2)),
        lr_sem=dma((down, 2)),
        cs_sem=dma((peers,)),
        cr_sem=dma((peers,)),
        **dict(zip(("is_", "ir", "its", "itr"), ring_sems(zs, 1))),
    )
    names = [*operands, "out", *scratch]
    return pl.pallas_call(
        functools.partial(layer_kernel, zs, peers, side, features, names),
        out_shape=jax.ShapeDtypeStruct((width, block), bf16),
        in_specs=[pl.BlockSpec(memory_space=space) for _, space in operands.values()],
        out_specs=pl.BlockSpec(memory_space=VMEM),
        scratch_shapes=list(scratch.values()),
        compiler_params=pltpu.CompilerParams(
            collective_id=1, has_side_effects=True, vmem_limit_bytes=VMEM_BYTES
        ),
    )(*[value for value, _ in operands.values()]).T


def solution(mesh):
    in_specs = (
        P("seq", "exp", None),
        P("seq", None),
        P("seq", None),
        P(),
        P("exp", None, None),
        P("exp", "seq"),
        P("exp", "seq"),
        P("seq"),
        P("exp", "seq", None),
        P("exp", "seq", None),
        P("exp", None, "seq"),
        P(),
        P(),
    )
    zs, peers = mesh.shape["seq"] // 2, mesh.shape["exp"]
    return jax.shard_map(
        functools.partial(local, zs, peers),
        mesh=mesh,
        in_specs=in_specs,
        out_specs=P("exp", "seq"),
        check_vma=False,
    )
```

```python
import functools
import math
import types

import jax
import jax.numpy as jnp
from jax import lax
from jax.experimental import pallas as pl
from jax.experimental.pallas import tpu as pltpu
from jax.sharding import PartitionSpec as P

LAT = 512
ROPE = 64
QK_NOPE = 128
SRC_CAP = 32

EPS = 1e-06
FLOOR = -1e30
SCALE2 = (QK_NOPE + ROPE) ** (-0.5) * math.log2(math.e)
MESH = pl.DeviceIdType.MESH
VMEM = pltpu.VMEM
VMEM_BYTES = 60 * 1024 * 1024


def rdot(a, b):
    return jnp.dot(a, b, preferred_element_type=jnp.float32)


def rdot_t(a, b):
    return lax.dot_general(
        a, b, (((1,), (1,)), ((), ())), preferred_element_type=jnp.float32
    )


def rdot_tn(a, b):
    return lax.dot_general(
        a, b, (((0,), (0,)), ((), ())), preferred_element_type=jnp.float32
    )


def turn(x):
    return x.astype(jnp.float32).T.astype(jnp.bfloat16)


def place(zs):
    s = lax.axis_index("seq")
    z, c = s // 2, lax.rem(s, 2)
    above = lax.rem(z + 1, zs) * 2 + c
    below = lax.rem(z + zs - 1, zs) * 2 + c
    twin = 2 * z + 1 - c
    return z, c, above, below, twin


def greet(zs, reach, peers, side):
    z, c, _, _, twin = place(zs)
    s = 2 * z + c
    e = lax.axis_index("exp")
    barrier = pltpu.get_barrier_semaphore()

    def hello(seq, exp):
        pl.semaphore_signal(
            barrier, inc=1, device_id={"seq": seq, "exp": exp}, device_id_type=MESH
        )

    def along(j, carry):
        hello(s, lax.rem(e + j, peers))
        return carry

    lax.fori_loop(1, peers, along, 0)
    for k in range(1, reach + 1):
        hello(lax.rem(z + k, zs) * 2 + c, e)
        hello(lax.rem(z + zs - k, zs) * 2 + c, e)
    ey, ex = e // side, lax.rem(e, side)
    for j in range(1, side):
        hello(twin, ey * side + lax.rem(ex + j, side))
        hello(twin, lax.rem(ey + j, side) * side + ex)
    hello(twin, e)
    return lambda: pl.semaphore_wait(barrier, 1 + 2 * reach + peers - 1 + 2 * (side - 1))


def remote(src, dst, ssem, rsem, seq, exp):
    return pltpu.make_async_remote_copy(
        src_ref=src,
        dst_ref=dst,
        send_sem=ssem,
        recv_sem=rsem,
        device_id={"seq": seq, "exp": exp},
        device_id_type=MESH,
    )


def ring_sems(zs, parts):
    dma = pltpu.SemaphoreType.DMA
    return [dma((zs, parts)), dma((zs, parts)), dma((zs,)), dma((zs,))]


def ring_gather(
    zs, buf, sems, own, visit, stride=1, parts=1, after=None, delay=0, meanwhile=None, shared=True
):
    rs, rr, ts, tr = sems
    up, down = zs // 2, zs // 2 - 1
    z, c, _, _, twin = place(zs)
    e = lax.axis_index("exp")
    size = buf.shape[1] // parts
    lag = 1 if shared else 0

    def far(side, k):
        return lax.rem(z + (zs - k if side == 0 else k), zs)

    def index(side, k):
        return k if side == 0 else up + k

    def hop(side, k, p, step):
        slot = buf.at[2 * far(side, k) + c, pl.ds(p * size, size)]
        i = index(side, k + step)
        to = lax.rem(z + (step if side == 0 else zs - step), zs) * 2 + c
        return remote(slot, slot, rs.at[i, p], rr.at[i, p], to, e)

    def came(side, k, p):
        slot = buf.at[2 * far(side, k) + c, pl.ds(p * size, size)]
        i = index(side, k)
        return remote(slot, slot, rs.at[i, p], rr.at[i, p], twin, e)

    def share(i, zb, core):
        slot = buf.at[2 * zb + core]
        return remote(slot, slot, ts.at[i], tr.at[i], twin, e)

    limits = (up, down)
    for p in range(parts):
        for k in range(1, stride + 1):
            for side in range(2):
                if k <= limits[side]:
                    hop(side, 0, p, k).start()
    if shared:
        share(0, z, c).start()
    if meanwhile is not None:
        meanwhile()

    def step(k, carry):
        for p in range(parts):
            for side in range(2):

                @pl.when(k <= limits[side])
                def _():
                    came(side, k, p).wait_recv()

                    @pl.when(k + stride <= limits[side])
                    def _():
                        hop(side, k, p, stride).start()

                    if shared and p == parts - 1:
                        share(index(side, k), far(side, k), c).start()

        @pl.when(k == 1)
        def _():
            if shared:
                share(0, z, 1 - c).wait_recv()
            own()

        def both(j, act):
            def one(side, inner):
                @pl.when((side == 0) | (j <= down))
                def _():
                    zb = lax.rem(z + jnp.where(side == 0, zs - j, j), zs)
                    act(zb, jnp.where(side == 0, j, up + j))

                return inner

            lax.fori_loop(0, 2, one, 0)

        def arrive(zb, i):
            if shared:
                share(i, zb, 1 - c).wait_recv()
            visit(zb)

        @pl.when((k > lag) & (k <= up + lag))
        def _():
            both(k - lag, arrive)

        if after is not None:

            @pl.when(k == delay + lag)
            def _():
                after(z)

            @pl.when(k > delay + lag)
            def _():
                both(k - lag - delay, lambda zb, i: after(zb))

        return carry

    lax.fori_loop(1, up + 1 + lag + delay, step, 0)

    def settle():
        def drain(k, carry):
            for side in range(2):

                @pl.when(k <= limits[side])
                def _():
                    for p in range(parts):
                        came(side, k, p).wait_send()
                    if shared:
                        share(index(side, k), far(side, k), c).wait_send()

            return carry

        lax.fori_loop(1, up + 1, drain, 0)
        if shared:
            share(0, z, c).wait_send()

    return settle


def attend(zs, peers, side, r, meanwhile, later):
    q_ref, buf, cbuf = r.q, r.keys, r.prefix
    best, total, acc = r.best, r.total, r.acc
    tok, width = buf.shape[1:]
    slots = cbuf.shape[2]
    rows = q_ref.shape[0]
    heads = rows // tok
    hand, use = 2, 3
    stride = 2
    up, down = zs // 2, zs // 2 - 1
    limits = (up, down)
    z, c, _, _, twin = place(zs)
    s = 2 * z + c
    e = lax.axis_index("exp")
    ey, ex = e // side, lax.rem(e, side)
    bx, by = lax.rem(ex + c, 2), lax.rem(ey + c, 2)
    mate_x = lax.rem(ex + 1 - 2 * bx + side, side)
    mate_y = lax.rem(ey + 1 - 2 * by + side, side)
    quads = 4
    q = 2 * by + bx
    size = tok // quads

    def member(j):
        p = lax.rem(q + j, quads)
        x = jnp.where(lax.rem(p, 2) == bx, ex, mate_x)
        y = jnp.where(p // 2 == by, ey, mate_y)
        return y * side + x

    def lanes(x, fold):
        parts = [x[:, i * 128 : (i + 1) * 128] for i in range(x.shape[1] // 128)]
        return functools.reduce(fold, parts)

    def wide(x, like):
        return jnp.concatenate([x] * (like // 128), axis=1)

    def absorb(blocks, first=False):
        band = min(rows, 256)
        spans = [slice(at, at + band) for at in range(0, rows, band)]
        scores = []
        for span in spans:
            scores.append([])
            for keys, visible in blocks:
                raw = rdot_t(q_ref[span, :], keys)
                scores[-1].append(
                    raw if visible is None else jnp.where(visible[span], raw, FLOOR)
                )
        for span, held in zip(spans, scores):
            top = functools.reduce(jnp.maximum, [lanes(x, jnp.maximum) for x in held])
            top = jnp.max(top, axis=1, keepdims=True) * SCALE2
            newest = jnp.broadcast_to(top, (band, best.shape[1]))
            if not first:
                before = best[span, :]
                newest = jnp.maximum(before, newest)
                fade = jnp.exp2(before - newest)
            best[span, :] = newest
            weights = [jnp.exp2(x * SCALE2 - wide(newest, x.shape[1])) for x in held]
            added = functools.reduce(jnp.add, [lanes(x, jnp.add) for x in weights])
            total[span, :] = added if first else total[span, :] * fade + added
            summed = functools.reduce(
                jnp.add,
                [
                    rdot(x.astype(jnp.bfloat16), keys[:, :LAT])
                    for x, (keys, _) in zip(weights, blocks)
                ],
            )
            acc[span, :] = summed if first else acc[span, :] * wide(fade, LAT) + summed

    def pair(zb):
        return buf[pl.ds(2 * zb, 2)].reshape(2 * tok, width)

    def far(way, k):
        return lax.rem(z + (zs - k if way == 0 else k), zs)

    def index(way, k):
        return k if way == 0 else up + k

    def piece(zb, p):
        return buf.at[2 * zb + c, pl.ds(pl.multiple_of(p * size, size), size)]

    def hop(way, k, step):
        i = index(way, k + step)
        to = lax.rem(z + (step if way == 0 else zs - step), zs) * 2 + c
        slot = piece(far(way, k), q)
        return remote(slot, slot, r.rs.at[i], r.rr.at[i], to, e)

    def cache_hop(way, k, step):
        i = index(way, k + step)
        to = lax.rem(z + (step if way == 0 else zs - step), zs) * 2 + c
        slot = cbuf.at[c, far(way, k)]
        return remote(slot, slot, r.cs.at[i], r.cr.at[i], to, e)

    def came(way, k):
        i = index(way, k)
        slot = piece(far(way, k), q)
        return remote(slot, slot, r.rs.at[i], r.rr.at[i], twin, e)

    def cache_came(way, k):
        i = index(way, k)
        slot = cbuf.at[c, far(way, k)]
        return remote(slot, slot, r.cs.at[i], r.cr.at[i], twin, e)

    def spread(i, zb, j):
        slot = piece(zb, q)
        return remote(slot, slot, r.ls.at[i, j], r.lr.at[i, j], s, member(j))

    def spread_in(i, zb, j):
        slot = piece(zb, lax.rem(q + quads - j, quads))
        return remote(slot, slot, r.ls.at[i, j], r.lr.at[i, j], s, member(j))

    def cache_spread(i, zb, j):
        slot = cbuf.at[c, zb]
        return remote(slot, slot, r.ms.at[i, j], r.mr.at[i], s, member(j))

    def share(i, zb, core):
        slot = buf.at[2 * zb + core]
        return remote(slot, slot, r.ts.at[i], r.tr.at[i], twin, e)

    def cache_share(core):
        slot = cbuf.at[core]
        return remote(slot, slot, r.ns.at[0], r.nr.at[0], twin, e)

    def carries(zb):
        return lax.rem(zb, quads) == q

    for k in range(1, stride + 1):
        for way in range(2):
            if k <= limits[way]:
                hop(way, 0, k).start()

                @pl.when(carries(z))
                def _():
                    cache_hop(way, 0, k).start()

    share(0, z, c).start()
    meanwhile()

    def step(k, carry):
        for way in range(2):

            @pl.when(k <= limits[way])
            def _():
                came(way, k).wait_recv()

                @pl.when(k + stride <= limits[way])
                def _():
                    hop(way, k, stride).start()

        for way in range(2):
            zb, i = far(way, k), index(way, k)

            @pl.when(k <= limits[way])
            def _():
                @pl.when(zb < z)
                def _():
                    for j in range(1, quads):
                        spread(i, zb, j).start()

                @pl.when(carries(zb))
                def _():
                    cache_came(way, k).wait_recv()

                    @pl.when(k + stride <= limits[way])
                    def _():
                        cache_hop(way, k, stride).start()

                    for j in range(1, quads):
                        cache_spread(i, zb, j).start()

        for way in range(2):
            zl, il = far(way, k - hand), index(way, k - hand)

            @pl.when((k > hand) & (k - hand <= limits[way]))
            def _():
                @pl.when(zl < z)
                def _():
                    for j in range(1, quads):
                        spread_in(il, zl, j).wait_recv()
                    share(il, zl, c).start()

                @pl.when(jnp.logical_not(carries(zl)))
                def _():
                    cache_spread(il, zl, 1).wait_recv()

        @pl.when(k == up + hand)
        def _():
            cache_share(c).start()

        @pl.when(k == 2)
        def _():
            share(0, z, 1 - c).wait_recv()
            row = lax.broadcasted_iota(jnp.int32, (rows, 2 * tok), 0)
            key = lax.broadcasted_iota(jnp.int32, (rows, 2 * tok), 1)
            absorb([(pair(z), key <= lax.rem(row, tok) + c * tok)], True)
            later()

        j = k - use
        lower, upper = far(0, j), far(1, j)
        has_lower = (j >= 1) & (lower < z)
        has_upper = (j >= 1) & (j <= down) & (upper < z)

        @pl.when(has_lower)
        def _():
            share(j, lower, 1 - c).wait_recv()

        @pl.when(has_upper)
        def _():
            share(up + j, upper, 1 - c).wait_recv()

        @pl.when(has_lower & has_upper)
        def _():
            absorb([(pair(lower), None), (pair(upper), None)])

        @pl.when(has_lower != has_upper)
        def _():
            absorb([(pair(jnp.where(has_lower, lower, upper)), None)])

        return carry

    lax.fori_loop(1, up + use + 1, step, 0)

    cache_share(1 - c).wait_recv()
    live = r.live[0]
    prefix = []
    cores = 1 if zs * slots % 128 == 0 else 2
    for core in range(0, 2, cores):
        count = cores * zs * slots
        at = lax.broadcasted_iota(jnp.int32, (rows, count), 1)
        own_core, rest = core + at // (zs * slots), lax.rem(at, zs * slots)
        at = (rest // slots * 2 + own_core) * slots + lax.rem(rest, slots)
        prefix.append((cbuf[core : core + cores].reshape(count, width), at < live))
    absorb(prefix)

    r.vup_copy().wait()
    for h in range(heads):
        part = pl.ds(h * tok, tok)
        weight = jnp.sum(total[part, :], axis=1, keepdims=True)
        context = (acc[part, :] / weight).astype(jnp.bfloat16)
        vh = r.vup.shape[2]
        r.heads[s, :, h * vh : (h + 1) * vh] = rdot(context, r.vup[h]).astype(jnp.bfloat16)

    def settle():
        def drain(k, carry):
            for way in range(2):
                zb, i = far(way, k), index(way, k)

                @pl.when(k <= limits[way])
                def _():
                    came(way, k).wait_send()

                    @pl.when(zb < z)
                    def _():
                        for j in range(1, quads):
                            spread(i, zb, j).wait_send()
                        share(i, zb, c).wait_send()

                    origin = jnp.maximum(k - stride, 0)
                    source = lax.rem(z + (zs - origin if way == 0 else origin), zs)

                    @pl.when(carries(source))
                    def _():
                        cache_came(way, k).wait_send()

                    @pl.when(carries(zb))
                    def _():
                        for j in range(1, quads):
                            cache_spread(i, zb, j).wait_send()

            return carry

        lax.fori_loop(1, up + 1, drain, 0)
        share(0, z, c).wait_send()
        cache_share(c).wait_send()

    return settle


def project(zs, peers, side, r):
    buf, terms = r.heads, r.terms
    _, tok, inner = buf.shape
    width = r.proj.shape[1]
    z, c, _, _, twin = place(zs)
    s = 2 * z + c
    e = lax.axis_index("exp")
    ey, ex = e // side, lax.rem(e, side)
    one, two = jnp.where(c == 0, ex, ey), jnp.where(c == 0, ey, ex)
    cross = (ey, ex)

    def split(zb):
        to_y, to_x = zb // side, lax.rem(zb, side)
        return jnp.where(c == 0, to_x, to_y), jnp.where(c == 0, to_y, to_x)

    def column(to_one, to_two):
        return jnp.where(c == 0, to_two * side + to_one, to_one * side + to_two)

    def along_one(zb):
        to_one, to_two = split(zb)
        return remote(
            terms.at[zb],
            r.row_in.at[to_two, one],
            r.x_send.at[zb],
            r.x_recv.at[to_two, one],
            s,
            column(to_one, two),
        )

    def along_two(to_two, core):
        return remote(
            r.sums.at[to_two, core],
            r.col_in.at[c, two],
            r.y_send.at[to_two, core],
            r.y_recv.at[c, two],
            2 * z + core,
            column(one, to_two),
        )

    def visit(zb):
        rows = buf[2 * zb + c]
        for core in range(2):
            terms[zb, core] = rdot_t(rows, r.proj[core]).astype(jnp.bfloat16)

        @pl.when(split(zb)[0] != one)
        def _():
            along_one(zb).start()

    def after(zb):
        to_one, to_two = split(zb)

        @pl.when(to_one == one)
        def _():
            for j in range(1, side):
                g = lax.rem(one + j, side)
                slot = r.row_in.at[to_two, g]
                remote(
                    slot, slot, r.x_send.at[zb], r.x_recv.at[to_two, g], s, column(g, two)
                ).wait_recv()
            for core in range(2):
                part = terms[zb, core].astype(jnp.float32)
                for j in range(1, side):
                    part = part + r.row_in[to_two, lax.rem(one + j, side), core].astype(
                        jnp.float32
                    )

                @pl.when((to_two == two) & (core == c))
                def _():
                    span = pl.ds(pl.multiple_of(c * tok, tok), tok)
                    r.hid[span, 0:width] += part

                @pl.when((to_two != two) | (core != c))
                def _():
                    r.sums[to_two, core] = part.astype(jnp.bfloat16)
                    along_two(to_two, core).start()

    def first():
        r.proj_swap(1 - c).wait_recv()

    sems = (r.hs, r.hr, r.hts, r.htr)
    settle_ring = ring_gather(
        zs,
        buf,
        sems,
        lambda: visit(z),
        visit,
        parts=4,
        after=after,
        delay=2,
        meanwhile=first,
        shared=False,
    )

    for core in range(2):
        for j in range(side):
            g = lax.rem(cross[core] + j, side)

            def collect():
                slot = r.col_in.at[core, g]
                remote(
                    slot, slot, r.y_send.at[0, 0], r.y_recv.at[core, g], 2 * z + core, e
                ).wait_recv()
                r.hid[core * tok : (core + 1) * tok, 0:width] += r.col_in[core, g].astype(
                    jnp.float32
                )

            if j == 0:
                pl.when(core != c)(collect)
            else:
                collect()

    def settle():
        settle_ring()
        r.proj_swap(c).wait_send()

        def drain(zb, carry):
            @pl.when(split(zb)[0] != one)
            def _():
                along_one(zb).wait_send()

            return carry

        lax.fori_loop(0, zs, drain, 0)
        for j in range(side):
            for core in range(2):
                to_two = lax.rem(two + j, side)

                @pl.when((to_two != two) | (core != c))
                def _():
                    along_two(to_two, core).wait_send()

    return settle


def swap_exp(peers, send, recv, s_sem, r_sem, meanwhile):
    s = lax.axis_index("seq")
    e = lax.axis_index("exp")

    def copy(j, to, slot):
        return remote(send.at[to], recv.at[slot], s_sem.at[j], r_sem.at[j], s, to)

    def start(j, carry):
        copy(j, lax.rem(e + j, peers), e).start()
        return carry

    lax.fori_loop(1, peers, start, 0)
    recv[e] = send[e]
    meanwhile()

    def finish(j, carry):
        copy(j, lax.rem(e + j, peers), lax.rem(e + peers - j, peers)).wait_recv()
        return carry

    lax.fori_loop(1, peers, finish, 0)

    def settle():
        def drain(j, carry):
            copy(j, lax.rem(e + j, peers), e).wait_send()
            return carry

        lax.fori_loop(1, peers, drain, 0)

    return settle


def tables(peers, r):
    e = lax.axis_index("exp")
    block = r.pick.shape[1]
    cap = r.pack.shape[0]
    span = pl.ds(pl.multiple_of(e * block, block), block)
    named, weights = r.routes[:, span], r.weights[:, span].astype(jnp.float32)
    hits, scaled = [], []
    for x in range(peers):
        hit = named == x
        hits.append(jnp.max(jnp.where(hit, 1.0, 0.0), axis=0, keepdims=True))
        scaled.append(jnp.sum(jnp.where(hit, weights, 0.0), axis=0, keepdims=True))
    chosen = jnp.concatenate(hits, axis=0)
    before = lax.broadcasted_iota(jnp.int32, (block, block), 0)
    order = lax.broadcasted_iota(jnp.int32, (block, block), 1)
    earlier = jnp.where(before < order, 1.0, 0.0).astype(jnp.bfloat16)
    rank = rdot(chosen.astype(jnp.bfloat16), earlier)
    slot = lax.broadcasted_iota(jnp.int32, (SRC_CAP, block), 0).astype(jnp.float32)
    for x in range(peers):
        part = pl.ds(x * SRC_CAP, SRC_CAP)
        here = jnp.where((rank[x : x + 1] == slot) & (hits[x] > 0.0), 1.0, 0.0)
        r.pick[part, :] = here.astype(jnp.bfloat16)
        r.mix[part, :] = (here * scaled[x]).astype(jnp.bfloat16)
    mine = jnp.sum(jnp.where(r.routes[...] == e, 1.0, 0.0), axis=0, keepdims=True)
    mine = [mine[:, x * block : (x + 1) * block] for x in range(peers)]
    count = jnp.sum(jnp.concatenate(mine, axis=0), axis=1, keepdims=True)
    spots = peers * SRC_CAP
    lane = lax.broadcasted_iota(jnp.int32, (peers, spots), 1) // SRC_CAP
    source = lax.broadcasted_iota(jnp.int32, (peers, spots), 0)
    own = jnp.sum(jnp.where(lane == source, count, 0.0), axis=0, keepdims=True)
    start = jnp.sum(jnp.where(lane > source, count, 0.0), axis=0, keepdims=True)
    turn = lax.rem(lax.broadcasted_iota(jnp.int32, (1, spots), 1), SRC_CAP).astype(jnp.float32)
    at = jnp.where(turn < own, start + turn, -1.0)
    row = lax.broadcasted_iota(jnp.int32, (cap, spots), 0).astype(jnp.float32)
    r.pack[...] = jnp.where(row == at, 1.0, 0.0).astype(jnp.bfloat16)


def split_rows(v):
    row = lax.broadcasted_iota(jnp.int32, v.shape, 0)
    high = v.astype(jnp.bfloat16).astype(jnp.float32)
    rest = v - high
    mid = rest.astype(jnp.bfloat16).astype(jnp.float32)
    low = rest - mid
    parts = jnp.where(row == 0, high, jnp.where(row == 1, mid, jnp.where(row == 2, low, 0.0)))
    return parts.astype(jnp.bfloat16)


def join_rows(block):
    return jnp.sum(block.astype(jnp.float32), axis=0, keepdims=True)


def route(zs, peers, features, r, meanwhile):
    width, tokens = r.residual.shape
    wide = r.hid.shape[1]
    cap = r.pack.shape[0]
    half = cap // 2
    cols = r.ibuf.shape[2]
    up, down = zs // 2, zs // 2 - 1
    z, c, _, _, twin = place(zs)
    e = lax.axis_index("exp")

    gain = jnp.concatenate([r.gain[...], jnp.zeros((1, wide - width), jnp.float32)], axis=1)
    hidden = r.hid[...]
    squares = jnp.sum(hidden * hidden, axis=1, keepdims=True)
    high = squares.astype(jnp.bfloat16).astype(jnp.float32)
    rest = squares - high
    mid = rest.astype(jnp.bfloat16).astype(jnp.float32)
    low = rest - mid
    lane = lax.broadcasted_iota(jnp.int32, (tokens, wide), 1)
    ext = jnp.where(
        lane < width,
        hidden * gain,
        jnp.where(
            lane == width,
            high,
            jnp.where(lane == width + 1, mid, jnp.where(lane == width + 2, low, 0.0)),
        ),
    ).astype(jnp.bfloat16)
    r.d_send[...] = rdot(r.pick[...], ext).astype(jnp.bfloat16).reshape(r.d_send.shape)
    settle_rows = swap_exp(peers, r.d_send, r.d_recv, r.ds_sem, r.dr_sem, meanwhile)

    arrived = r.d_recv[...].reshape(peers * SRC_CAP, wide)
    packed = rdot(r.pack[...], arrived).astype(jnp.bfloat16)
    r.xs[...] = packed
    mark = lax.broadcasted_iota(jnp.int32, (16, wide), 1)
    ones = jnp.where((mark >= width) & (mark < width + 3), 1.0, 0.0).astype(jnp.bfloat16)
    r.sqv[...] = jnp.zeros_like(r.sqv)
    for h in range(2):
        span = pl.ds(pl.multiple_of((c if h == 0 else 1 - c) * half, 16), half)
        r.xo[h * half : (h + 1) * half, :] = r.xs[span, 0:width]
        r.sqv[h, :, 0:half] = rdot_t(ones, r.xs[span, :])
    own_sq = r.sqv[0]
    tail = split_rows(r.sqv[1])

    def to_twin(d):
        return pltpu.make_async_remote_copy(
            src_ref=r.other.at[d],
            dst_ref=r.theirs.at[d],
            send_sem=r.ps_sem.at[d],
            recv_sem=r.pr_sem.at[d],
            device_id={"seq": twin, "exp": e},
            device_id_type=MESH,
        )

    def partial(d):
        r.load(d, 0).wait()
        r.load(d, 1).wait()
        both = rdot(r.xo[...], r.wgu[d])
        for p in range(2):
            part = both[:, p * cols : (p + 1) * cols]
            r.other[d, p, 0:half, :] = part[half:].astype(jnp.bfloat16)
            r.other[d, p, half : half + 16, :] = tail
            r.mine[d, p] = part[:half]
        to_twin(d).start()

    def sent_rows(p):
        return pl.ds(0, half + 16 if p == 0 else half)

    def chunk_copy(way, d, p):
        out, into, ssem, rsem = chains[way]
        ahead = jnp.minimum(d, 2)
        to = lax.rem(z + (ahead if way == 0 else zs - ahead), zs) * 2 + c
        return remote(
            out.at[d - 1, p, sent_rows(p)],
            into.at[d - 1, p, sent_rows(p)],
            ssem.at[d - 1, p],
            rsem.at[d - 1, p],
            to,
            e,
        )

    chains = (
        (r.up_out, r.up_in, r.us_sem, r.ur_sem),
        (r.dn_out, r.dn_in, r.ls_sem, r.lr_sem),
    )
    limits = (up, down)

    def end(way, d):
        return lax.rem(z + (d if way == 0 else zs - d), zs)

    def pair_sum(d, p):
        if p == 0:
            to_twin(d).wait_recv()
        body = r.mine[d, p] + r.theirs[d, p, 0:half, :].astype(jnp.float32)
        sq = own_sq + join_rows(r.theirs[d, 0, half : half + 16, :]) if p == 0 else None
        return body, sq

    def relay(way, d, p, first):
        out, into, _, _ = chains[way]
        body, sq = pair_sum(end(way, d), p)
        if not first:
            chunk_copy(way, d + 2, p).wait_recv()
            body = body + into[d + 1, p, 0:half, :].astype(jnp.float32)
            if p == 0:
                sq = sq + join_rows(into[d + 1, p, half : half + 16, :])
        out[d - 1, p, 0:half, :] = body.astype(jnp.bfloat16)
        if p == 0:
            out[d - 1, p, half : half + 16, :] = split_rows(sq)
        chunk_copy(way, d, p).start()

    def order(t):
        return [(way, limits[way] - 2 * t - x) for x in range(2) for way in range(2)]

    for way, d in order(0):
        partial(end(way, d))
    for way, d in order(0):
        if d >= 1:
            for p in range(2):
                relay(way, d, p, True)

    def ring(t, carry):
        for way, d in order(t):
            partial(end(way, d))
        for way, d in order(t):

            @pl.when(d >= 1)
            def _():
                for p in range(2):
                    relay(way, d, p, False)

        return carry

    lax.fori_loop(1, up // 2, ring, 0)

    sums = []
    for p in range(2):
        total, added = pair_sum(z, p)
        for way in range(2):
            for d in range(1, min(2, limits[way]) + 1):
                into = chains[way][1]
                chunk_copy(way, d, p).wait_recv()
                total = total + into[d - 1, p, 0:half, :].astype(jnp.float32)
                if p == 0:
                    added = added + join_rows(into[d - 1, p, half : half + 16, :])
        sums.append(total)
        if p == 0:
            sq = added
    factor = lax.rsqrt(sq[0:1, :] / features + EPS)
    row = lax.broadcasted_iota(jnp.int32, (half, cols), 0)
    lane = lax.broadcasted_iota(jnp.int32, (half, cols), 1)
    factor = jnp.sum(jnp.where(row == lane, factor, 0.0), axis=1, keepdims=True)
    gate = sums[0] * factor
    lift = sums[1] * factor
    r.ibuf[2 * z + c] = (gate / (1.0 + jnp.exp(-gate)) * lift).astype(jnp.bfloat16)

    r.produced[...] = jnp.zeros_like(r.produced)

    def visit(zb):
        block = r.ibuf[pl.ds(2 * zb, 2)].reshape(cap, cols)
        span = pl.ds(pl.multiple_of(zb * cols, cols), cols)
        r.produced[...] += rdot_t(block, r.wd[:, span])

    def settle_sums():
        settle_rows()

        def drain(d, carry):
            to_twin(d).wait_send()
            return carry

        lax.fori_loop(0, zs, drain, 0)

        def drain_ring(t, carry):
            for p in range(2):
                chunk_copy(0, t, p).wait_send()

                @pl.when(t <= down)
                def _():
                    chunk_copy(1, t, p).wait_send()

            return carry

        lax.fori_loop(1, up + 1, drain_ring, 0)
        r.wd_copy().wait()

    sems = (r.is_, r.ir, r.its, r.itr)
    settle_ring = ring_gather(
        zs, r.ibuf, sems, lambda: visit(z), visit, stride=2, meanwhile=settle_sums
    )

    produced = r.produced[...].astype(jnp.bfloat16)
    r.c_send[...] = rdot_tn(r.pack[...], produced).astype(jnp.bfloat16).reshape(r.c_send.shape)
    settle_back = swap_exp(peers, r.c_send, r.c_recv, r.cs_sem, r.cr_sem, settle_ring)
    back = r.c_recv[...].reshape(peers * SRC_CAP, width)
    r.out[...] = (r.hid[:, 0:width] + rdot_tn(r.mix[...], back)).T.astype(jnp.bfloat16)
    settle_back()


def layer_kernel(zs, peers, side, features, names, *refs):
    r = types.SimpleNamespace(**dict(zip(names, refs)))
    z, c, _, _, _ = place(zs)
    s = 2 * z + c
    cols = r.ibuf.shape[2]
    up, down = zs // 2, zs // 2 - 1

    def load(d, which):
        span = pl.ds(pl.multiple_of(d * cols, cols), cols)
        return pltpu.make_async_copy(
            (r.wg_hbm, r.wu_hbm)[which].at[:, span],
            r.wgu.at[d, :, pl.ds(which * cols, cols)],
            r.w_sem.at[d, which],
        )

    def load_all(d, carry):
        load(d, 0).start()
        load(d, 1).start()
        return carry

    r.load = load

    def whole(src, dst, i):
        return lambda: pltpu.make_async_copy(src, dst, r.b_sem.at[i])

    latents_copy = whole(r.latents_hbm, r.latents, 0)
    cache_copy = whole(r.cache_hbm, r.prefix.at[c, z], 1)
    queries_copy = whole(r.queries_hbm, r.queries, 2)
    routes_copy = whole(r.routes_hbm, r.routes, 3)
    weights_copy = whole(r.weights_hbm, r.weights, 4)
    r.res_copy = whole(r.residual_hbm, r.residual, 5)
    r.vup_copy = whole(r.vup_hbm, r.vup, 6)
    r.proj_copy = whole(r.proj_hbm, r.proj.at[c], 7)
    r.proj_swap = lambda core: remote(
        r.proj.at[core],
        r.proj.at[core],
        r.o_sem.at[0],
        r.o_sem.at[1],
        2 * z + 1 - c,
        lax.axis_index("exp"),
    )
    r.wd_copy = whole(r.wd_hbm, r.wd, 8)
    latents_copy().start()
    cache_copy().start()
    greeted = greet(zs, 2, peers, side)
    for copy in (queries_copy, routes_copy, weights_copy, r.res_copy, r.vup_copy):
        copy().start()
    r.proj_copy().start()
    r.wd_copy().start()
    lax.fori_loop(0, zs, load_all, 0)
    latents_copy().wait()
    r.keys[s] = turn(r.latents[...])
    cache_copy().wait()
    greeted()

    def prepare():
        tok = r.keys.shape[1]
        queries_copy().wait()
        for h in range(r.queries.shape[0]):
            r.q[h * tok : (h + 1) * tok, :] = turn(r.queries[h])
        r.proj_copy().wait()
        r.proj_swap(c).start()
        r.res_copy().wait()
        r.hid[...] = jnp.zeros_like(r.hid)
        r.hid[:, 0 : r.residual.shape[0]] = r.residual[...].astype(jnp.float32).T

    def prepare_tables():
        routes_copy().wait()
        weights_copy().wait()
        tables(peers, r)

    settle_keys = attend(zs, peers, side, r, prepare, prepare_tables)
    settle_heads = project(zs, peers, side, r)

    def settle():
        settle_keys()
        settle_heads()

    route(zs, peers, features, r, settle)


def local(
    zs,
    peers,
    queries,
    latents,
    cache,
    prefix_len,
    value_up,
    out_proj,
    residual,
    norm_gain,
    w_gate,
    w_up,
    w_down,
    routes,
    route_weights,
):
    bf16, f32 = jnp.bfloat16, jnp.float32
    dma = pltpu.SemaphoreType.DMA
    tok, heads, qwidth = queries.shape
    slots = cache.shape[0]
    block, width = residual.shape
    inner = out_proj.shape[0]
    cap = SRC_CAP * min(peers, 6)
    half = cap // 2
    wide = -(-(width + 3) // 128) * 128
    cols = w_gate.shape[2] // zs
    up, down = zs // 2, zs // 2 - 1
    features = width * 2 * zs
    rows = tok * heads
    side = math.isqrt(peers)

    operands = dict(
        queries_hbm=(jnp.transpose(queries, (1, 2, 0)), pl.ANY),
        latents_hbm=(latents.T, pl.ANY),
        cache_hbm=(cache, pl.ANY),
        live=(prefix_len, pltpu.SMEM),
        residual_hbm=(residual.T, pl.ANY),
        gain=(norm_gain.reshape(1, width), VMEM),
        routes_hbm=(routes.T, pl.ANY),
        weights_hbm=(route_weights.T, pl.ANY),
        vup_hbm=(value_up, pl.ANY),
        proj_hbm=(out_proj.T, pl.ANY),
        wg_hbm=(w_gate[0], pl.ANY),
        wu_hbm=(w_up[0], pl.ANY),
        wd_hbm=(w_down[0].T, pl.ANY),
    )
    scratch = dict(
        queries=VMEM((heads, qwidth, tok), bf16),
        latents=VMEM((qwidth, tok), bf16),
        residual=VMEM((width, block), bf16),
        routes=VMEM(routes.shape[::-1], jnp.int32),
        weights=VMEM(routes.shape[::-1], bf16),
        q=VMEM((rows, qwidth), bf16),
        keys=VMEM((2 * zs, tok, qwidth), bf16),
        prefix=VMEM((2, zs, slots, qwidth), bf16),
        best=VMEM((rows, 128), f32),
        total=VMEM((rows, 128), f32),
        acc=VMEM((rows, LAT), f32),
        vup=VMEM(value_up.shape, bf16),
        rs=dma((zs,)),
        rr=dma((zs,)),
        cs=dma((zs,)),
        cr=dma((zs,)),
        ls=dma((zs, 4)),
        lr=dma((zs, 4)),
        ms=dma((zs, 4)),
        mr=dma((zs,)),
        ts=dma((zs,)),
        tr=dma((zs,)),
        ns=dma((1,)),
        nr=dma((1,)),
        heads=VMEM((2 * zs, tok, inner), bf16),
        proj=VMEM((2, width, inner), bf16),
        terms=VMEM((peers, 2, tok, width), bf16),
        row_in=VMEM((side, side, 2, tok, width), bf16),
        sums=VMEM((side, 2, tok, width), bf16),
        col_in=VMEM((2, side, tok, width), bf16),
        hid=VMEM((block, wide), f32),
        x_send=dma((peers,)),
        x_recv=dma((side, side)),
        y_send=dma((side, 2)),
        y_recv=dma((2, side)),
        **dict(zip(("hs", "hr", "hts", "htr"), ring_sems(zs, 4))),
        pick=VMEM((peers * SRC_CAP, block), bf16),
        mix=VMEM((peers * SRC_CAP, block), bf16),
        pack=VMEM((cap, peers * SRC_CAP), bf16),
        wgu=VMEM((zs, width, 2 * cols), bf16),
        wd=VMEM((width, w_down.shape[1]), bf16),
        d_send=VMEM((peers, SRC_CAP, wide), bf16),
        d_recv=VMEM((peers, SRC_CAP, wide), bf16),
        xs=VMEM((cap, wide), bf16),
        xo=VMEM((cap, width), bf16),
        sqv=VMEM((2, 16, cols), f32),
        mine=VMEM((zs, 2, half, cols), f32),
        other=VMEM((zs, 2, half + 16, cols), bf16),
        theirs=VMEM((zs, 2, half + 16, cols), bf16),
        up_out=VMEM((up, 2, half + 16, cols), bf16),
        up_in=VMEM((up, 2, half + 16, cols), bf16),
        dn_out=VMEM((down, 2, half + 16, cols), bf16),
        dn_in=VMEM((down, 2, half + 16, cols), bf16),
        ibuf=VMEM((2 * zs, half, cols), bf16),
        produced=VMEM((cap, width), f32),
        c_send=VMEM((peers, SRC_CAP, width), bf16),
        c_recv=VMEM((peers, SRC_CAP, width), bf16),
        w_sem=dma((zs, 2)),
        b_sem=dma((9,)),
        o_sem=dma((2,)),
        ds_sem=dma((peers,)),
        dr_sem=dma((peers,)),
        ps_sem=dma((zs,)),
        pr_sem=dma((zs,)),
        us_sem=dma((up, 2)),
        ur_sem=dma((up, 2)),
        ls_sem=dma((down, 2)),
        lr_sem=dma((down, 2)),
        cs_sem=dma((peers,)),
        cr_sem=dma((peers,)),
        **dict(zip(("is_", "ir", "its", "itr"), ring_sems(zs, 1))),
    )
    names = [*operands, "out", *scratch]
    return pl.pallas_call(
        functools.partial(layer_kernel, zs, peers, side, features, names),
        out_shape=jax.ShapeDtypeStruct((width, block), bf16),
        in_specs=[pl.BlockSpec(memory_space=space) for _, space in operands.values()],
        out_specs=pl.BlockSpec(memory_space=VMEM),
        scratch_shapes=list(scratch.values()),
        compiler_params=pltpu.CompilerParams(
            collective_id=1, has_side_effects=True, vmem_limit_bytes=VMEM_BYTES
        ),
    )(*[value for value, _ in operands.values()]).T


def solution(mesh):
    in_specs = (
        P("seq", "exp", None),
        P("seq", None),
        P("seq", None),
        P(),
        P("exp", None, None),
        P("exp", "seq"),
        P("exp", "seq"),
        P("seq"),
        P("exp", "seq", None),
        P("exp", "seq", None),
        P("exp", None, "seq"),
        P(),
        P(),
    )
    zs, peers = mesh.shape["seq"] // 2, mesh.shape["exp"]
    return jax.shard_map(
        functools.partial(local, zs, peers),
        mesh=mesh,
        in_specs=in_specs,
        out_specs=P("exp", "seq"),
        check_vma=False,
    )
```

```python
import functools
import math
import types

import jax
import jax.numpy as jnp
from jax import lax
from jax.experimental import pallas as pl
from jax.experimental.pallas import tpu as pltpu
from jax.sharding import PartitionSpec as P

LAT = 512
ROPE = 64
QK_NOPE = 128
SRC_CAP = 32

EPS = 1e-06
FLOOR = -1e30
SCALE2 = (QK_NOPE + ROPE) ** (-0.5) * math.log2(math.e)
MESH = pl.DeviceIdType.MESH
VMEM = pltpu.VMEM
VMEM_BYTES = 60 * 1024 * 1024


def rdot(a, b):
    return jnp.dot(a, b, preferred_element_type=jnp.float32)


def rdot_t(a, b):
    return lax.dot_general(
        a, b, (((1,), (1,)), ((), ())), preferred_element_type=jnp.float32
    )


def rdot_tn(a, b):
    return lax.dot_general(
        a, b, (((0,), (0,)), ((), ())), preferred_element_type=jnp.float32
    )


def turn(x):
    return x.astype(jnp.float32).T.astype(jnp.bfloat16)


def place(zs):
    s = lax.axis_index("seq")
    z, c = s // 2, lax.rem(s, 2)
    above = lax.rem(z + 1, zs) * 2 + c
    below = lax.rem(z + zs - 1, zs) * 2 + c
    twin = 2 * z + 1 - c
    return z, c, above, below, twin


def greet(zs, reach, peers, side):
    z, c, _, _, twin = place(zs)
    s = 2 * z + c
    e = lax.axis_index("exp")
    barrier = pltpu.get_barrier_semaphore()

    def hello(seq, exp):
        pl.semaphore_signal(
            barrier, inc=1, device_id={"seq": seq, "exp": exp}, device_id_type=MESH
        )

    def along(j, carry):
        hello(s, lax.rem(e + j, peers))
        return carry

    lax.fori_loop(1, peers, along, 0)
    for k in range(1, reach + 1):
        hello(lax.rem(z + k, zs) * 2 + c, e)
        hello(lax.rem(z + zs - k, zs) * 2 + c, e)
    ey, ex = e // side, lax.rem(e, side)
    for j in range(1, side):
        hello(twin, ey * side + lax.rem(ex + j, side))
        hello(twin, lax.rem(ey + j, side) * side + ex)
    hello(twin, e)
    return lambda: pl.semaphore_wait(barrier, 1 + 2 * reach + peers - 1 + 2 * (side - 1))


def remote(src, dst, ssem, rsem, seq, exp):
    return pltpu.make_async_remote_copy(
        src_ref=src,
        dst_ref=dst,
        send_sem=ssem,
        recv_sem=rsem,
        device_id={"seq": seq, "exp": exp},
        device_id_type=MESH,
    )


def ring_sems(zs, parts):
    dma = pltpu.SemaphoreType.DMA
    return [dma((zs, parts)), dma((zs, parts)), dma((zs,)), dma((zs,))]


def ring_gather(
    zs, buf, sems, own, visit, stride=1, parts=1, after=None, delay=0, meanwhile=None, shared=True
):
    rs, rr, ts, tr = sems
    up, down = zs // 2, zs // 2 - 1
    z, c, _, _, twin = place(zs)
    e = lax.axis_index("exp")
    size = buf.shape[1] // parts
    lag = 1 if shared else 0

    def far(side, k):
        return lax.rem(z + (zs - k if side == 0 else k), zs)

    def index(side, k):
        return k if side == 0 else up + k

    def hop(side, k, p, step):
        slot = buf.at[2 * far(side, k) + c, pl.ds(p * size, size)]
        i = index(side, k + step)
        to = lax.rem(z + (step if side == 0 else zs - step), zs) * 2 + c
        return remote(slot, slot, rs.at[i, p], rr.at[i, p], to, e)

    def came(side, k, p):
        slot = buf.at[2 * far(side, k) + c, pl.ds(p * size, size)]
        i = index(side, k)
        return remote(slot, slot, rs.at[i, p], rr.at[i, p], twin, e)

    def share(i, zb, core):
        slot = buf.at[2 * zb + core]
        return remote(slot, slot, ts.at[i], tr.at[i], twin, e)

    limits = (up, down)
    for p in range(parts):
        for k in range(1, stride + 1):
            for side in range(2):
                if k <= limits[side]:
                    hop(side, 0, p, k).start()
    if shared:
        share(0, z, c).start()
    if meanwhile is not None:
        meanwhile()

    def step(k, carry):
        for p in range(parts):
            for side in range(2):

                @pl.when(k <= limits[side])
                def _():
                    came(side, k, p).wait_recv()

                    @pl.when(k + stride <= limits[side])
                    def _():
                        hop(side, k, p, stride).start()

                    if shared and p == parts - 1:
                        share(index(side, k), far(side, k), c).start()

        @pl.when(k == 1)
        def _():
            if shared:
                share(0, z, 1 - c).wait_recv()
            own()

        def both(j, act):
            def one(side, inner):
                @pl.when((side == 0) | (j <= down))
                def _():
                    zb = lax.rem(z + jnp.where(side == 0, zs - j, j), zs)
                    act(zb, jnp.where(side == 0, j, up + j))

                return inner

            lax.fori_loop(0, 2, one, 0)

        def arrive(zb, i):
            if shared:
                share(i, zb, 1 - c).wait_recv()
            visit(zb)

        @pl.when((k > lag) & (k <= up + lag))
        def _():
            both(k - lag, arrive)

        if after is not None:

            @pl.when(k == delay + lag)
            def _():
                after(z)

            @pl.when(k > delay + lag)
            def _():
                both(k - lag - delay, lambda zb, i: after(zb))

        return carry

    lax.fori_loop(1, up + 1 + lag + delay, step, 0)

    def settle():
        def drain(k, carry):
            for side in range(2):

                @pl.when(k <= limits[side])
                def _():
                    for p in range(parts):
                        came(side, k, p).wait_send()
                    if shared:
                        share(index(side, k), far(side, k), c).wait_send()

            return carry

        lax.fori_loop(1, up + 1, drain, 0)
        if shared:
            share(0, z, c).wait_send()

    return settle


def attend(zs, peers, side, r, meanwhile, later):
    q_ref, buf, cbuf = r.q, r.keys, r.prefix
    best, total, acc = r.best, r.total, r.acc
    tok, width = buf.shape[1:]
    slots = cbuf.shape[2]
    rows = q_ref.shape[0]
    heads = rows // tok
    hand, use = 2, 3
    stride = 2
    up, down = zs // 2, zs // 2 - 1
    limits = (up, down)
    z, c, _, _, twin = place(zs)
    s = 2 * z + c
    e = lax.axis_index("exp")
    ey, ex = e // side, lax.rem(e, side)
    q = jnp.where(c == 0, ex, ey)
    size = tok // side

    def line(j):
        p = lax.rem(q + j, side)
        return jnp.where(c == 0, ey * side + p, p * side + ex)

    def lanes(x, fold):
        parts = [x[:, i * 128 : (i + 1) * 128] for i in range(x.shape[1] // 128)]
        return functools.reduce(fold, parts)

    def wide(x, like):
        return jnp.concatenate([x] * (like // 128), axis=1)

    def absorb(blocks, first=False):
        band = min(rows, 256)
        spans = [slice(at, at + band) for at in range(0, rows, band)]
        scores = []
        for span in spans:
            scores.append([])
            for keys, visible in blocks:
                raw = rdot_t(q_ref[span, :], keys)
                scores[-1].append(
                    raw if visible is None else jnp.where(visible[span], raw, FLOOR)
                )
        for span, held in zip(spans, scores):
            top = functools.reduce(jnp.maximum, [lanes(x, jnp.maximum) for x in held])
            top = jnp.max(top, axis=1, keepdims=True) * SCALE2
            newest = jnp.broadcast_to(top, (band, best.shape[1]))
            if not first:
                before = best[span, :]
                newest = jnp.maximum(before, newest)
                fade = jnp.exp2(before - newest)
            best[span, :] = newest
            weights = [jnp.exp2(x * SCALE2 - wide(newest, x.shape[1])) for x in held]
            added = functools.reduce(jnp.add, [lanes(x, jnp.add) for x in weights])
            total[span, :] = added if first else total[span, :] * fade + added
            summed = functools.reduce(
                jnp.add,
                [
                    rdot(x.astype(jnp.bfloat16), keys[:, :LAT])
                    for x, (keys, _) in zip(weights, blocks)
                ],
            )
            acc[span, :] = summed if first else acc[span, :] * wide(fade, LAT) + summed

    def pair(zb):
        return buf[pl.ds(2 * zb, 2)].reshape(2 * tok, width)

    def far(way, k):
        return lax.rem(z + (zs - k if way == 0 else k), zs)

    def index(way, k):
        return k if way == 0 else up + k

    def piece(zb, p):
        return buf.at[2 * zb + c, pl.ds(pl.multiple_of(p * size, size), size)]

    def hop(way, k, step):
        i = index(way, k + step)
        to = lax.rem(z + (step if way == 0 else zs - step), zs) * 2 + c
        slot = piece(far(way, k), q)
        return remote(slot, slot, r.rs.at[i], r.rr.at[i], to, e)

    def cache_hop(way, k, step):
        i = index(way, k + step)
        to = lax.rem(z + (step if way == 0 else zs - step), zs) * 2 + c
        slot = cbuf.at[c, far(way, k)]
        return remote(slot, slot, r.cs.at[i], r.cr.at[i], to, e)

    def came(way, k):
        i = index(way, k)
        slot = piece(far(way, k), q)
        return remote(slot, slot, r.rs.at[i], r.rr.at[i], twin, e)

    def cache_came(way, k):
        i = index(way, k)
        slot = cbuf.at[c, far(way, k)]
        return remote(slot, slot, r.cs.at[i], r.cr.at[i], twin, e)

    def spread(i, zb, j):
        slot = piece(zb, q)
        return remote(slot, slot, r.ls.at[i, j], r.lr.at[i, j], s, line(j))

    def spread_in(i, zb, j):
        slot = piece(zb, lax.rem(q + side - j, side))
        return remote(slot, slot, r.ls.at[i, j], r.lr.at[i, j], s, line(j))

    def cache_spread(i, zb, j):
        slot = cbuf.at[c, zb]
        return remote(slot, slot, r.ms.at[i, j], r.mr.at[i], s, line(j))

    def share(i, zb, core):
        slot = buf.at[2 * zb + core]
        return remote(slot, slot, r.ts.at[i], r.tr.at[i], twin, e)

    def cache_share(core):
        slot = cbuf.at[core]
        return remote(slot, slot, r.ns.at[0], r.nr.at[0], twin, e)

    def carries(zb):
        return lax.rem(zb, side) == q

    for k in range(1, stride + 1):
        for way in range(2):
            if k <= limits[way]:
                hop(way, 0, k).start()

                @pl.when(carries(z))
                def _():
                    cache_hop(way, 0, k).start()

    share(0, z, c).start()
    meanwhile()

    def step(k, carry):
        for way in range(2):

            @pl.when(k <= limits[way])
            def _():
                came(way, k).wait_recv()

                @pl.when(k + stride <= limits[way])
                def _():
                    hop(way, k, stride).start()

        for way in range(2):
            zb, i = far(way, k), index(way, k)

            @pl.when(k <= limits[way])
            def _():
                @pl.when(zb < z)
                def _():
                    for j in range(1, side):
                        spread(i, zb, j).start()

                @pl.when(carries(zb))
                def _():
                    cache_came(way, k).wait_recv()

                    @pl.when(k + stride <= limits[way])
                    def _():
                        cache_hop(way, k, stride).start()

                    for j in range(1, side):
                        cache_spread(i, zb, j).start()

        for way in range(2):
            zl, il = far(way, k - hand), index(way, k - hand)

            @pl.when((k > hand) & (k - hand <= limits[way]))
            def _():
                @pl.when(zl < z)
                def _():
                    for j in range(1, side):
                        spread_in(il, zl, j).wait_recv()
                    share(il, zl, c).start()

                @pl.when(jnp.logical_not(carries(zl)))
                def _():
                    cache_spread(il, zl, 1).wait_recv()

        @pl.when(k == up + hand)
        def _():
            cache_share(c).start()

        @pl.when(k == 2)
        def _():
            share(0, z, 1 - c).wait_recv()
            row = lax.broadcasted_iota(jnp.int32, (rows, 2 * tok), 0)
            key = lax.broadcasted_iota(jnp.int32, (rows, 2 * tok), 1)
            absorb([(pair(z), key <= lax.rem(row, tok) + c * tok)], True)
            later()

        j = k - use
        lower, upper = far(0, j), far(1, j)
        has_lower = (j >= 1) & (lower < z)
        has_upper = (j >= 1) & (j <= down) & (upper < z)

        @pl.when(has_lower)
        def _():
            share(j, lower, 1 - c).wait_recv()

        @pl.when(has_upper)
        def _():
            share(up + j, upper, 1 - c).wait_recv()

        @pl.when(has_lower & has_upper)
        def _():
            absorb([(pair(lower), None), (pair(upper), None)])

        @pl.when(has_lower != has_upper)
        def _():
            absorb([(pair(jnp.where(has_lower, lower, upper)), None)])

        return carry

    lax.fori_loop(1, up + use + 1, step, 0)

    cache_share(1 - c).wait_recv()
    live = r.live[0]
    prefix = []
    cores = 1 if zs * slots % 128 == 0 else 2
    for core in range(0, 2, cores):
        count = cores * zs * slots
        at = lax.broadcasted_iota(jnp.int32, (rows, count), 1)
        own_core, rest = core + at // (zs * slots), lax.rem(at, zs * slots)
        at = (rest // slots * 2 + own_core) * slots + lax.rem(rest, slots)
        prefix.append((cbuf[core : core + cores].reshape(count, width), at < live))
    absorb(prefix)

    r.vup_copy().wait()
    for h in range(heads):
        part = pl.ds(h * tok, tok)
        weight = jnp.sum(total[part, :], axis=1, keepdims=True)
        context = (acc[part, :] / weight).astype(jnp.bfloat16)
        vh = r.vup.shape[2]
        r.heads[s, :, h * vh : (h + 1) * vh] = rdot(context, r.vup[h]).astype(jnp.bfloat16)

    def settle():
        def drain(k, carry):
            for way in range(2):
                zb, i = far(way, k), index(way, k)

                @pl.when(k <= limits[way])
                def _():
                    came(way, k).wait_send()

                    @pl.when(zb < z)
                    def _():
                        for j in range(1, side):
                            spread(i, zb, j).wait_send()
                        share(i, zb, c).wait_send()

                    origin = jnp.maximum(k - stride, 0)
                    source = lax.rem(z + (zs - origin if way == 0 else origin), zs)

                    @pl.when(carries(source))
                    def _():
                        cache_came(way, k).wait_send()

                    @pl.when(carries(zb))
                    def _():
                        for j in range(1, side):
                            cache_spread(i, zb, j).wait_send()

            return carry

        lax.fori_loop(1, up + 1, drain, 0)
        share(0, z, c).wait_send()
        cache_share(c).wait_send()

    return settle


def project(zs, peers, side, r):
    buf, terms = r.heads, r.terms
    _, tok, inner = buf.shape
    width = r.proj.shape[1]
    z, c, _, _, twin = place(zs)
    s = 2 * z + c
    e = lax.axis_index("exp")
    ey, ex = e // side, lax.rem(e, side)
    one, two = jnp.where(c == 0, ex, ey), jnp.where(c == 0, ey, ex)
    cross = (ey, ex)

    def split(zb):
        to_y, to_x = zb // side, lax.rem(zb, side)
        return jnp.where(c == 0, to_x, to_y), jnp.where(c == 0, to_y, to_x)

    def column(to_one, to_two):
        return jnp.where(c == 0, to_two * side + to_one, to_one * side + to_two)

    def along_one(zb):
        to_one, to_two = split(zb)
        return remote(
            terms.at[zb],
            r.row_in.at[to_two, one],
            r.x_send.at[zb],
            r.x_recv.at[to_two, one],
            s,
            column(to_one, two),
        )

    def along_two(to_two, core):
        return remote(
            r.sums.at[to_two, core],
            r.col_in.at[c, two],
            r.y_send.at[to_two, core],
            r.y_recv.at[c, two],
            2 * z + core,
            column(one, to_two),
        )

    def visit(zb):
        rows = buf[2 * zb + c]
        for core in range(2):
            terms[zb, core] = rdot_t(rows, r.proj[core]).astype(jnp.bfloat16)

        @pl.when(split(zb)[0] != one)
        def _():
            along_one(zb).start()

    def after(zb):
        to_one, to_two = split(zb)

        @pl.when(to_one == one)
        def _():
            for j in range(1, side):
                g = lax.rem(one + j, side)
                slot = r.row_in.at[to_two, g]
                remote(
                    slot, slot, r.x_send.at[zb], r.x_recv.at[to_two, g], s, column(g, two)
                ).wait_recv()
            for core in range(2):
                part = terms[zb, core].astype(jnp.float32)
                for j in range(1, side):
                    part = part + r.row_in[to_two, lax.rem(one + j, side), core].astype(
                        jnp.float32
                    )

                @pl.when((to_two == two) & (core == c))
                def _():
                    span = pl.ds(pl.multiple_of(c * tok, tok), tok)
                    r.hid[span, 0:width] += part

                @pl.when((to_two != two) | (core != c))
                def _():
                    r.sums[to_two, core] = part.astype(jnp.bfloat16)
                    along_two(to_two, core).start()

    def first():
        r.proj_swap(1 - c).wait_recv()

    sems = (r.hs, r.hr, r.hts, r.htr)
    settle_ring = ring_gather(
        zs,
        buf,
        sems,
        lambda: visit(z),
        visit,
        parts=2,
        after=after,
        delay=2,
        meanwhile=first,
        shared=False,
    )

    for core in range(2):
        for j in range(side):
            g = lax.rem(cross[core] + j, side)

            def collect():
                slot = r.col_in.at[core, g]
                remote(
                    slot, slot, r.y_send.at[0, 0], r.y_recv.at[core, g], 2 * z + core, e
                ).wait_recv()
                r.hid[core * tok : (core + 1) * tok, 0:width] += r.col_in[core, g].astype(
                    jnp.float32
                )

            if j == 0:
                pl.when(core != c)(collect)
            else:
                collect()

    def settle():
        settle_ring()
        r.proj_swap(c).wait_send()

        def drain(zb, carry):
            @pl.when(split(zb)[0] != one)
            def _():
                along_one(zb).wait_send()

            return carry

        lax.fori_loop(0, zs, drain, 0)
        for j in range(side):
            for core in range(2):
                to_two = lax.rem(two + j, side)

                @pl.when((to_two != two) | (core != c))
                def _():
                    along_two(to_two, core).wait_send()

    return settle


def swap_exp(peers, send, recv, s_sem, r_sem, meanwhile):
    s = lax.axis_index("seq")
    e = lax.axis_index("exp")

    def copy(j, to, slot):
        return remote(send.at[to], recv.at[slot], s_sem.at[j], r_sem.at[j], s, to)

    def start(j, carry):
        copy(j, lax.rem(e + j, peers), e).start()
        return carry

    lax.fori_loop(1, peers, start, 0)
    recv[e] = send[e]
    meanwhile()

    def finish(j, carry):
        copy(j, lax.rem(e + j, peers), lax.rem(e + peers - j, peers)).wait_recv()
        return carry

    lax.fori_loop(1, peers, finish, 0)

    def settle():
        def drain(j, carry):
            copy(j, lax.rem(e + j, peers), e).wait_send()
            return carry

        lax.fori_loop(1, peers, drain, 0)

    return settle


def tables(peers, r):
    e = lax.axis_index("exp")
    block = r.pick.shape[1]
    cap = r.pack.shape[0]
    span = pl.ds(pl.multiple_of(e * block, block), block)
    named, weights = r.routes[:, span], r.weights[:, span].astype(jnp.float32)
    hits, scaled = [], []
    for x in range(peers):
        hit = named == x
        hits.append(jnp.max(jnp.where(hit, 1.0, 0.0), axis=0, keepdims=True))
        scaled.append(jnp.sum(jnp.where(hit, weights, 0.0), axis=0, keepdims=True))
    chosen = jnp.concatenate(hits, axis=0)
    before = lax.broadcasted_iota(jnp.int32, (block, block), 0)
    order = lax.broadcasted_iota(jnp.int32, (block, block), 1)
    earlier = jnp.where(before < order, 1.0, 0.0).astype(jnp.bfloat16)
    rank = rdot(chosen.astype(jnp.bfloat16), earlier)
    slot = lax.broadcasted_iota(jnp.int32, (SRC_CAP, block), 0).astype(jnp.float32)
    for x in range(peers):
        part = pl.ds(x * SRC_CAP, SRC_CAP)
        here = jnp.where((rank[x : x + 1] == slot) & (hits[x] > 0.0), 1.0, 0.0)
        r.pick[part, :] = here.astype(jnp.bfloat16)
        r.mix[part, :] = (here * scaled[x]).astype(jnp.bfloat16)
    mine = jnp.sum(jnp.where(r.routes[...] == e, 1.0, 0.0), axis=0, keepdims=True)
    mine = [mine[:, x * block : (x + 1) * block] for x in range(peers)]
    count = jnp.sum(jnp.concatenate(mine, axis=0), axis=1, keepdims=True)
    spots = peers * SRC_CAP
    lane = lax.broadcasted_iota(jnp.int32, (peers, spots), 1) // SRC_CAP
    source = lax.broadcasted_iota(jnp.int32, (peers, spots), 0)
    own = jnp.sum(jnp.where(lane == source, count, 0.0), axis=0, keepdims=True)
    start = jnp.sum(jnp.where(lane > source, count, 0.0), axis=0, keepdims=True)
    turn = lax.rem(lax.broadcasted_iota(jnp.int32, (1, spots), 1), SRC_CAP).astype(jnp.float32)
    at = jnp.where(turn < own, start + turn, -1.0)
    row = lax.broadcasted_iota(jnp.int32, (cap, spots), 0).astype(jnp.float32)
    r.pack[...] = jnp.where(row == at, 1.0, 0.0).astype(jnp.bfloat16)


def split_rows(v):
    row = lax.broadcasted_iota(jnp.int32, v.shape, 0)
    high = v.astype(jnp.bfloat16).astype(jnp.float32)
    rest = v - high
    mid = rest.astype(jnp.bfloat16).astype(jnp.float32)
    low = rest - mid
    parts = jnp.where(row == 0, high, jnp.where(row == 1, mid, jnp.where(row == 2, low, 0.0)))
    return parts.astype(jnp.bfloat16)


def join_rows(block):
    return jnp.sum(block.astype(jnp.float32), axis=0, keepdims=True)


def route(zs, peers, features, r, meanwhile):
    width, tokens = r.residual.shape
    wide = r.hid.shape[1]
    cap = r.pack.shape[0]
    half = cap // 2
    cols = r.ibuf.shape[2]
    up, down = zs // 2, zs // 2 - 1
    z, c, _, _, twin = place(zs)
    e = lax.axis_index("exp")

    gain = jnp.concatenate([r.gain[...], jnp.zeros((1, wide - width), jnp.float32)], axis=1)
    hidden = r.hid[...]
    squares = jnp.sum(hidden * hidden, axis=1, keepdims=True)
    high = squares.astype(jnp.bfloat16).astype(jnp.float32)
    rest = squares - high
    mid = rest.astype(jnp.bfloat16).astype(jnp.float32)
    low = rest - mid
    lane = lax.broadcasted_iota(jnp.int32, (tokens, wide), 1)
    ext = jnp.where(
        lane < width,
        hidden * gain,
        jnp.where(
            lane == width,
            high,
            jnp.where(lane == width + 1, mid, jnp.where(lane == width + 2, low, 0.0)),
        ),
    ).astype(jnp.bfloat16)
    r.d_send[...] = rdot(r.pick[...], ext).astype(jnp.bfloat16).reshape(r.d_send.shape)
    settle_rows = swap_exp(peers, r.d_send, r.d_recv, r.ds_sem, r.dr_sem, meanwhile)

    arrived = r.d_recv[...].reshape(peers * SRC_CAP, wide)
    packed = rdot(r.pack[...], arrived).astype(jnp.bfloat16)
    r.xs[...] = packed
    mark = lax.broadcasted_iota(jnp.int32, (16, wide), 1)
    ones = jnp.where((mark >= width) & (mark < width + 3), 1.0, 0.0).astype(jnp.bfloat16)
    r.sqv[...] = jnp.zeros_like(r.sqv)
    for h in range(2):
        span = pl.ds(pl.multiple_of((c if h == 0 else 1 - c) * half, 16), half)
        r.xo[h * half : (h + 1) * half, :] = r.xs[span, 0:width]
        r.sqv[h, :, 0:half] = rdot_t(ones, r.xs[span, :])
    own_sq = r.sqv[0]
    tail = split_rows(r.sqv[1])

    def to_twin(d):
        return pltpu.make_async_remote_copy(
            src_ref=r.other.at[d],
            dst_ref=r.theirs.at[d],
            send_sem=r.ps_sem.at[d],
            recv_sem=r.pr_sem.at[d],
            device_id={"seq": twin, "exp": e},
            device_id_type=MESH,
        )

    def partial(d):
        r.load(d, 0).wait()
        r.load(d, 1).wait()
        both = rdot(r.xo[...], r.wgu[d])
        for p in range(2):
            part = both[:, p * cols : (p + 1) * cols]
            r.other[d, p, 0:half, :] = part[half:].astype(jnp.bfloat16)
            r.other[d, p, half : half + 16, :] = tail
            r.mine[d, p] = part[:half]
        to_twin(d).start()

    def sent_rows(p):
        return pl.ds(0, half + 16 if p == 0 else half)

    def chunk_copy(way, d, p):
        out, into, ssem, rsem = chains[way]
        ahead = jnp.minimum(d, 2)
        to = lax.rem(z + (ahead if way == 0 else zs - ahead), zs) * 2 + c
        return remote(
            out.at[d - 1, p, sent_rows(p)],
            into.at[d - 1, p, sent_rows(p)],
            ssem.at[d - 1, p],
            rsem.at[d - 1, p],
            to,
            e,
        )

    chains = (
        (r.up_out, r.up_in, r.us_sem, r.ur_sem),
        (r.dn_out, r.dn_in, r.ls_sem, r.lr_sem),
    )
    limits = (up, down)

    def end(way, d):
        return lax.rem(z + (d if way == 0 else zs - d), zs)

    def pair_sum(d, p):
        if p == 0:
            to_twin(d).wait_recv()
        body = r.mine[d, p] + r.theirs[d, p, 0:half, :].astype(jnp.float32)
        sq = own_sq + join_rows(r.theirs[d, 0, half : half + 16, :]) if p == 0 else None
        return body, sq

    def relay(way, d, p, first):
        out, into, _, _ = chains[way]
        body, sq = pair_sum(end(way, d), p)
        if not first:
            chunk_copy(way, d + 2, p).wait_recv()
            body = body + into[d + 1, p, 0:half, :].astype(jnp.float32)
            if p == 0:
                sq = sq + join_rows(into[d + 1, p, half : half + 16, :])
        out[d - 1, p, 0:half, :] = body.astype(jnp.bfloat16)
        if p == 0:
            out[d - 1, p, half : half + 16, :] = split_rows(sq)
        chunk_copy(way, d, p).start()

    def order(t):
        return [(way, limits[way] - 2 * t - x) for x in range(2) for way in range(2)]

    for way, d in order(0):
        partial(end(way, d))
    for way, d in order(0):
        if d >= 1:
            for p in range(2):
                relay(way, d, p, True)

    def ring(t, carry):
        for way, d in order(t):
            partial(end(way, d))
        for way, d in order(t):

            @pl.when(d >= 1)
            def _():
                for p in range(2):
                    relay(way, d, p, False)

        return carry

    lax.fori_loop(1, up // 2, ring, 0)

    sums = []
    for p in range(2):
        total, added = pair_sum(z, p)
        for way in range(2):
            for d in range(1, min(2, limits[way]) + 1):
                into = chains[way][1]
                chunk_copy(way, d, p).wait_recv()
                total = total + into[d - 1, p, 0:half, :].astype(jnp.float32)
                if p == 0:
                    added = added + join_rows(into[d - 1, p, half : half + 16, :])
        sums.append(total)
        if p == 0:
            sq = added
    factor = lax.rsqrt(sq[0:1, :] / features + EPS)
    row = lax.broadcasted_iota(jnp.int32, (half, cols), 0)
    lane = lax.broadcasted_iota(jnp.int32, (half, cols), 1)
    factor = jnp.sum(jnp.where(row == lane, factor, 0.0), axis=1, keepdims=True)
    gate = sums[0] * factor
    lift = sums[1] * factor
    r.ibuf[2 * z + c] = (gate / (1.0 + jnp.exp(-gate)) * lift).astype(jnp.bfloat16)

    r.produced[...] = jnp.zeros_like(r.produced)

    def visit(zb):
        block = r.ibuf[pl.ds(2 * zb, 2)].reshape(cap, cols)
        span = pl.ds(pl.multiple_of(zb * cols, cols), cols)
        r.produced[...] += rdot_t(block, r.wd[:, span])

    def settle_sums():
        settle_rows()

        def drain(d, carry):
            to_twin(d).wait_send()
            return carry

        lax.fori_loop(0, zs, drain, 0)

        def drain_ring(t, carry):
            for p in range(2):
                chunk_copy(0, t, p).wait_send()

                @pl.when(t <= down)
                def _():
                    chunk_copy(1, t, p).wait_send()

            return carry

        lax.fori_loop(1, up + 1, drain_ring, 0)
        r.wd_copy().wait()

    sems = (r.is_, r.ir, r.its, r.itr)
    settle_ring = ring_gather(
        zs, r.ibuf, sems, lambda: visit(z), visit, stride=2, meanwhile=settle_sums
    )

    produced = r.produced[...].astype(jnp.bfloat16)
    r.c_send[...] = rdot_tn(r.pack[...], produced).astype(jnp.bfloat16).reshape(r.c_send.shape)
    settle_back = swap_exp(peers, r.c_send, r.c_recv, r.cs_sem, r.cr_sem, settle_ring)
    back = r.c_recv[...].reshape(peers * SRC_CAP, width)
    r.out[...] = (r.hid[:, 0:width] + rdot_tn(r.mix[...], back)).T.astype(jnp.bfloat16)
    settle_back()


def layer_kernel(zs, peers, side, features, names, *refs):
    r = types.SimpleNamespace(**dict(zip(names, refs)))
    z, c, _, _, _ = place(zs)
    s = 2 * z + c
    cols = r.ibuf.shape[2]
    up, down = zs // 2, zs // 2 - 1

    def load(d, which):
        span = pl.ds(pl.multiple_of(d * cols, cols), cols)
        return pltpu.make_async_copy(
            (r.wg_hbm, r.wu_hbm)[which].at[:, span],
            r.wgu.at[d, :, pl.ds(which * cols, cols)],
            r.w_sem.at[d, which],
        )

    def load_all(d, carry):
        load(d, 0).start()
        load(d, 1).start()
        return carry

    r.load = load

    def whole(src, dst, i):
        return lambda: pltpu.make_async_copy(src, dst, r.b_sem.at[i])

    latents_copy = whole(r.latents_hbm, r.latents, 0)
    cache_copy = whole(r.cache_hbm, r.prefix.at[c, z], 1)
    queries_copy = whole(r.queries_hbm, r.queries, 2)
    routes_copy = whole(r.routes_hbm, r.routes, 3)
    weights_copy = whole(r.weights_hbm, r.weights, 4)
    r.res_copy = whole(r.residual_hbm, r.residual, 5)
    r.vup_copy = whole(r.vup_hbm, r.vup, 6)
    r.proj_copy = whole(r.proj_hbm, r.proj.at[c], 7)
    r.proj_swap = lambda core: remote(
        r.proj.at[core],
        r.proj.at[core],
        r.o_sem.at[0],
        r.o_sem.at[1],
        2 * z + 1 - c,
        lax.axis_index("exp"),
    )
    r.wd_copy = whole(r.wd_hbm, r.wd, 8)
    latents_copy().start()
    cache_copy().start()
    greeted = greet(zs, 2, peers, side)
    for copy in (queries_copy, routes_copy, weights_copy, r.res_copy, r.vup_copy):
        copy().start()
    r.proj_copy().start()
    r.wd_copy().start()
    lax.fori_loop(0, zs, load_all, 0)
    latents_copy().wait()
    r.keys[s] = turn(r.latents[...])
    cache_copy().wait()
    greeted()

    def prepare():
        tok = r.keys.shape[1]
        queries_copy().wait()
        for h in range(r.queries.shape[0]):
            r.q[h * tok : (h + 1) * tok, :] = turn(r.queries[h])
        r.proj_copy().wait()
        r.proj_swap(c).start()
        r.res_copy().wait()
        r.hid[...] = jnp.zeros_like(r.hid)
        r.hid[:, 0 : r.residual.shape[0]] = r.residual[...].astype(jnp.float32).T

    def prepare_tables():
        routes_copy().wait()
        weights_copy().wait()
        tables(peers, r)

    settle_keys = attend(zs, peers, side, r, prepare, prepare_tables)
    settle_heads = project(zs, peers, side, r)

    def settle():
        settle_keys()
        settle_heads()

    route(zs, peers, features, r, settle)


def local(
    zs,
    peers,
    queries,
    latents,
    cache,
    prefix_len,
    value_up,
    out_proj,
    residual,
    norm_gain,
    w_gate,
    w_up,
    w_down,
    routes,
    route_weights,
):
    bf16, f32 = jnp.bfloat16, jnp.float32
    dma = pltpu.SemaphoreType.DMA
    tok, heads, qwidth = queries.shape
    slots = cache.shape[0]
    block, width = residual.shape
    inner = out_proj.shape[0]
    cap = SRC_CAP * min(peers, 6)
    half = cap // 2
    wide = -(-(width + 3) // 128) * 128
    cols = w_gate.shape[2] // zs
    up, down = zs // 2, zs // 2 - 1
    features = width * 2 * zs
    rows = tok * heads
    side = math.isqrt(peers)

    operands = dict(
        queries_hbm=(jnp.transpose(queries, (1, 2, 0)), pl.ANY),
        latents_hbm=(latents.T, pl.ANY),
        cache_hbm=(cache, pl.ANY),
        live=(prefix_len, pltpu.SMEM),
        residual_hbm=(residual.T, pl.ANY),
        gain=(norm_gain.reshape(1, width), VMEM),
        routes_hbm=(routes.T, pl.ANY),
        weights_hbm=(route_weights.T, pl.ANY),
        vup_hbm=(value_up, pl.ANY),
        proj_hbm=(out_proj.T, pl.ANY),
        wg_hbm=(w_gate[0], pl.ANY),
        wu_hbm=(w_up[0], pl.ANY),
        wd_hbm=(w_down[0].T, pl.ANY),
    )
    scratch = dict(
        queries=VMEM((heads, qwidth, tok), bf16),
        latents=VMEM((qwidth, tok), bf16),
        residual=VMEM((width, block), bf16),
        routes=VMEM(routes.shape[::-1], jnp.int32),
        weights=VMEM(routes.shape[::-1], bf16),
        q=VMEM((rows, qwidth), bf16),
        keys=VMEM((2 * zs, tok, qwidth), bf16),
        prefix=VMEM((2, zs, slots, qwidth), bf16),
        best=VMEM((rows, 128), f32),
        total=VMEM((rows, 128), f32),
        acc=VMEM((rows, LAT), f32),
        vup=VMEM(value_up.shape, bf16),
        rs=dma((zs,)),
        rr=dma((zs,)),
        cs=dma((zs,)),
        cr=dma((zs,)),
        ls=dma((zs, side)),
        lr=dma((zs, side)),
        ms=dma((zs, side)),
        mr=dma((zs,)),
        ts=dma((zs,)),
        tr=dma((zs,)),
        ns=dma((1,)),
        nr=dma((1,)),
        heads=VMEM((2 * zs, tok, inner), bf16),
        proj=VMEM((2, width, inner), bf16),
        terms=VMEM((peers, 2, tok, width), bf16),
        row_in=VMEM((side, side, 2, tok, width), bf16),
        sums=VMEM((side, 2, tok, width), bf16),
        col_in=VMEM((2, side, tok, width), bf16),
        hid=VMEM((block, wide), f32),
        x_send=dma((peers,)),
        x_recv=dma((side, side)),
        y_send=dma((side, 2)),
        y_recv=dma((2, side)),
        **dict(zip(("hs", "hr", "hts", "htr"), ring_sems(zs, 2))),
        pick=VMEM((peers * SRC_CAP, block), bf16),
        mix=VMEM((peers * SRC_CAP, block), bf16),
        pack=VMEM((cap, peers * SRC_CAP), bf16),
        wgu=VMEM((zs, width, 2 * cols), bf16),
        wd=VMEM((width, w_down.shape[1]), bf16),
        d_send=VMEM((peers, SRC_CAP, wide), bf16),
        d_recv=VMEM((peers, SRC_CAP, wide), bf16),
        xs=VMEM((cap, wide), bf16),
        xo=VMEM((cap, width), bf16),
        sqv=VMEM((2, 16, cols), f32),
        mine=VMEM((zs, 2, half, cols), f32),
        other=VMEM((zs, 2, half + 16, cols), bf16),
        theirs=VMEM((zs, 2, half + 16, cols), bf16),
        up_out=VMEM((up, 2, half + 16, cols), bf16),
        up_in=VMEM((up, 2, half + 16, cols), bf16),
        dn_out=VMEM((down, 2, half + 16, cols), bf16),
        dn_in=VMEM((down, 2, half + 16, cols), bf16),
        ibuf=VMEM((2 * zs, half, cols), bf16),
        produced=VMEM((cap, width), f32),
        c_send=VMEM((peers, SRC_CAP, width), bf16),
        c_recv=VMEM((peers, SRC_CAP, width), bf16),
        w_sem=dma((zs, 2)),
        b_sem=dma((9,)),
        o_sem=dma((2,)),
        ds_sem=dma((peers,)),
        dr_sem=dma((peers,)),
        ps_sem=dma((zs,)),
        pr_sem=dma((zs,)),
        us_sem=dma((up, 2)),
        ur_sem=dma((up, 2)),
        ls_sem=dma((down, 2)),
        lr_sem=dma((down, 2)),
        cs_sem=dma((peers,)),
        cr_sem=dma((peers,)),
        **dict(zip(("is_", "ir", "its", "itr"), ring_sems(zs, 1))),
    )
    names = [*operands, "out", *scratch]
    return pl.pallas_call(
        functools.partial(layer_kernel, zs, peers, side, features, names),
        out_shape=jax.ShapeDtypeStruct((width, block), bf16),
        in_specs=[pl.BlockSpec(memory_space=space) for _, space in operands.values()],
        out_specs=pl.BlockSpec(memory_space=VMEM),
        scratch_shapes=list(scratch.values()),
        compiler_params=pltpu.CompilerParams(
            collective_id=1, has_side_effects=True, vmem_limit_bytes=VMEM_BYTES
        ),
    )(*[value for value, _ in operands.values()]).T


def solution(mesh):
    in_specs = (
        P("seq", "exp", None),
        P("seq", None),
        P("seq", None),
        P(),
        P("exp", None, None),
        P("exp", "seq"),
        P("exp", "seq"),
        P("seq"),
        P("exp", "seq", None),
        P("exp", "seq", None),
        P("exp", None, "seq"),
        P(),
        P(),
    )
    zs, peers = mesh.shape["seq"] // 2, mesh.shape["exp"]
    return jax.shard_map(
        functools.partial(local, zs, peers),
        mesh=mesh,
        in_specs=in_specs,
        out_specs=P("exp", "seq"),
        check_vma=False,
    )
```
